32 devices in a mesh: wide: 4 (over y, x), narrow: 8 (over z, core).
Axes of the slice: x: 2, y: 2, z: 4, core: 2. Of those that a mesh axis runs over, the one named last changes fastest.
Arguments:
- params: float32 [2260992], P(('wide', 'narrow')), as said below
- first_moment: float32 [2260992], P(('wide', 'narrow')), may hold values from -9.1552734e-05 to 9.1552734e-05
- second_moment: float32 [2260992], P(('wide', 'narrow')), may hold values from 2.8638002e-11 to 1.14817995e-10
- smalls: float32 [8192], P(('wide', 'narrow')), as said below
- small_first: float32 [8192], P(('wide', 'narrow')), may hold values from -0.00030517578 to 0.00030517578
- small_second: float32 [8192], P(('wide', 'narrow')), may hold values from 4.0297128e-12 to 1.6118851e-11
- images: float32 [96, 3072], P(('wide', 'narrow')), may hold values from 0 to 1
- noise: float32 [96, 3072], P(('wide', 'narrow')), may hold values from -6 to 6
- sigma: float32 [96], P(('wide', 'narrow')), may hold values from 0.01 to 50
- freq: float32 [128], replicated, may hold values from -64 to 64
- counts: int32 [32], P(('wide', 'narrow')), may hold values from 1 to 3, as said below
- partner: int32 [32, 3], P(('wide', 'narrow')), may hold values from 0 to 2, as said below
Outputs:
- loss: float32 [], replicated
- grad_norm: float32 [], replicated
- new_params: float32 [2260992], P(('wide', 'narrow'))
- new_first: float32 [2260992], P(('wide', 'narrow'))
- new_second: float32 [2260992], P(('wide', 'narrow'))
- new_smalls: float32 [8192], P(('wide', 'narrow'))
- new_small_first: float32 [8192], P(('wide', 'narrow'))
- new_small_second: float32 [8192], P(('wide', 'narrow'))
- small_grad: float32 [8192], P(('wide', 'narrow'))
The draws below stay inside these ranges and needn't reach their ends.
Inputs may be any that keep to these rules, and one draw needn't show every extreme that they name: The first counts[d] slots of device d are live; device 0 holds 3 and the last device 1. partner[d, s] is a live slot of the device whose wide index differs from d's by 2 at the same narrow index. `params`: matrices in layout order, each of order its fan-in to the power -1/2 (attn_out four times that). `smalls`: gains near one, biases of both signs.
All inputs are finite; a program needn't handle non-finite values.
Results may differ from the reference program's by a relative error of at most 0.01.
The reference program's roundings to bfloat16 on the way count: a program that leaves them out, or rounds other values in their place, can miss the bound.
Values may be sent and summed in bfloat16 or wider, within the bound.
No kernel may reach another device: no remote copies, remote signals or barrier semaphores. Data moves between devices by JAX's collectives and lax.ppermute only.
A program may use at most 192 MiB of HBM per device.

```python
import math
import jax
import jax.numpy as jnp
from jax import lax

NF = 128
MID_CHANNELS = 256
TEMB = 512
NFOUR = 128
IMG = 32
GROUPS = 32
CHAN = 3
SLOTS = 3
STEP = 7
RAWP = 2255744
PARAMS = 2260992
SMALLS = 8192
PIX = 3072
IMAGES = 96
N_WIDE = 4
N_NARROW = 8


def mat_shapes():
    return [('temb_one', (2 * NFOUR, TEMB)), ('temb_two', (TEMB, TEMB)), ('conv_in', (3, 3, CHAN, NF)), ('pyramid', (CHAN, MID_CHANNELS)), ('down_one', (3, 3, NF, MID_CHANNELS)), ('down_time', (TEMB, MID_CHANNELS)), ('down_two', (3, 3, MID_CHANNELS, MID_CHANNELS)), ('down_skip', (NF, MID_CHANNELS)), ('attn_qkv', (MID_CHANNELS, 3 * MID_CHANNELS)), ('attn_out', (MID_CHANNELS, MID_CHANNELS)), ('up_one', (3, 3, MID_CHANNELS, NF)), ('up_time', (TEMB, NF)), ('up_two', (3, 3, NF, NF)), ('up_skip', (MID_CHANNELS, NF)), ('conv_out', (3, 3, 2 * NF, CHAN))]


def small_kinds():
    return [(TEMB, 0), (TEMB, 0), (NF, 0), (MID_CHANNELS, 0), (NF, 1), (NF, 0), (MID_CHANNELS, 0), (MID_CHANNELS, 0), (MID_CHANNELS, 1), (MID_CHANNELS, 0), (MID_CHANNELS, 0), (MID_CHANNELS, 0), (MID_CHANNELS, 1), (MID_CHANNELS, 0), (MID_CHANNELS, 0), (MID_CHANNELS, 0), (MID_CHANNELS, 0), (MID_CHANNELS, 1), (MID_CHANNELS, 0), (NF, 0), (NF, 0), (NF, 1), (NF, 0), (NF, 0), (NF, 0), (2 * NF, 1), (2 * NF, 0), (CHAN, 0)]


def draw_params(key, part):
    key = jax.random.fold_in(key, 3)
    pieces = []
    used = 0
    for label, shape in mat_shapes():
        length = math.prod(shape)
        boost = 4.0 if label == 'attn_out' else 1.0
        pieces.append(jnp.full((length,), boost * float(length // shape[-1]) ** (-0.5), jnp.float32))
        used += length
    pieces.append(jnp.full((PARAMS - used,), 0.02, jnp.float32))
    scales = jnp.concatenate(pieces)
    base = jax.random.normal(key, (PARAMS,), jnp.float32)
    return scales * base


def draw_smalls(key, part):
    key = jax.random.fold_in(key, 5)
    pieces = []
    used = 0
    for length, is_gain in small_kinds():
        pieces.append(jnp.full((length,), float(is_gain), jnp.float32))
        used += length
    pieces.append(jnp.zeros((SMALLS - used,), jnp.float32))
    gains = jnp.concatenate(pieces)
    base = jax.random.normal(key, (SMALLS,), jnp.float32)
    return gains * (1.0 + 0.15 * base) + (1.0 - gains) * 0.3 * base


def count_draw(key):
    inner = jax.random.fold_in(key, 11)
    value_rows = jax.random.randint(inner, (N_WIDE * N_NARROW,), 1, SLOTS + 1)
    value_rows = value_rows.at[0].set(SLOTS)
    return value_rows.at[N_WIDE * N_NARROW - 1].set(1).astype(jnp.int32)


def draw_counts(key, part):
    return count_draw(key)


def draw_partner(key, part):
    counts = count_draw(key)
    index = jnp.arange(N_WIDE * N_NARROW, dtype=jnp.int32)
    other = jnp.bitwise_xor(index // N_NARROW, N_WIDE // 2) * N_NARROW + index % N_NARROW
    limit = counts[other]
    offset = jax.random.randint(jax.random.fold_in(key, 23), (N_WIDE * N_NARROW,), 0, SLOTS)
    slots = jnp.arange(SLOTS, dtype=jnp.int32)
    return ((slots[None, :] + offset[:, None]) % limit[:, None]).astype(jnp.int32)


def block_scale(own_key, shape, cuts, least, largest):
    factor_of, own = 1.0, jax.random.fold_in(own_key, 6)
    for axis_at, blocks in cuts:
        draws = jnp.exp(jax.random.uniform(jax.random.fold_in(own, axis_at), (blocks,), jnp.float32, least / len(cuts), largest / len(cuts)))
        factor_of = factor_of * jnp.repeat(draws, shape[axis_at] // blocks).reshape([-1 if axis == axis_at else 1 for axis in range(len(shape))])
    return factor_of


def bell_draw(key, extent, scale, most, cuts=(), held_as=jnp.bfloat16):
    loudness = block_scale(key, extent, cuts, -0.22, 0.18) if cuts else 1.0
    array = jax.random.normal(key, extent, jnp.float32) * scale * loudness
    return jnp.minimum(jnp.maximum(array, -most), most).astype(held_as)


def setup_inputs(seed: int = 0) -> dict:
    splits = jax.random.split(jax.random.key(seed), 13)
    return {
        "params": draw_params(jax.random.fold_in(splits[12], 71), 0),
        "first_moment": bell_draw(splits[1], (PARAMS,), (0.01 * RAWP ** -0.5), 9.1552734375e-05, ((0, 32),), jnp.float32),
        "second_moment": jnp.clip(jnp.exp(math.log(1.1481799538914927e-10) - 1.3886137 * jax.random.uniform(splits[2], (PARAMS,), jnp.float32) ** block_scale(splits[2], (PARAMS,), ((0, 32),), -0.2, 0.2)), 2.86380016922827e-11, 1.1481799538914927e-10),
        "smalls": draw_smalls(jax.random.fold_in(splits[12], 71), 0),
        "small_first": bell_draw(splits[4], (SMALLS,), (0.03 * RAWP ** -0.5), 0.00030517578, ((0, 32),), jnp.float32),
        "small_second": jnp.clip(jnp.exp(math.log(1.6118851045576754e-11) - 1.3862944 * jax.random.uniform(splits[5], (SMALLS,), jnp.float32) ** block_scale(splits[5], (SMALLS,), ((0, 32),), -0.2, 0.2)), 4.0297127613941885e-12, 1.6118851045576754e-11),
        "images": jnp.clip(1.0 * jax.random.uniform(splits[6], (IMAGES, PIX), jnp.float32) ** block_scale(splits[6], (IMAGES, PIX), ((0, 32),), -0.2, 0.2), 0.0, 1.0),
        "noise": bell_draw(splits[7], (IMAGES, PIX), 1.0, 6.0, ((0, 32),), jnp.float32),
        "sigma": jnp.clip(jnp.exp(math.log(50.0) - 8.517193 * jax.random.uniform(splits[8], (IMAGES,), jnp.float32) ** block_scale(splits[8], (IMAGES,), ((0, 32),), -0.2, 0.2)), 0.01, 50.0),
        "freq": bell_draw(splits[9], (NFOUR,), 16.0, 64.0, (), jnp.float32),
        "counts": draw_counts(jax.random.fold_in(splits[12], 71), 0),
        "partner": draw_partner(jax.random.fold_in(splits[12], 71), 0),
    }


@jax.custom_vjp
def low(v):
    return lax.optimization_barrier(v.astype(jnp.bfloat16)).astype(jnp.float32)

@jax.custom_vjp
def low_back(v):
    return v

def low_keep(v):
    return (low(v), None)

def low_pass(kept, grad):
    return (grad,)

def back_keep(v):
    return (v, None)

def back_low(kept, grad):
    return (low(grad),)
low.defvjp(low_keep, low_pass)
low_back.defvjp(back_keep, back_low)
HIGH_PRECISION = lax.Precision.HIGHEST
INV_ROOT = 0.7071067811865476

def mat_layout():
    return [('temb_one', (2 * NFOUR, TEMB)), ('temb_two', (TEMB, TEMB)), ('conv_in', (3, 3, CHAN, NF)), ('pyramid', (CHAN, MID_CHANNELS)), ('down_one', (3, 3, NF, MID_CHANNELS)), ('down_time', (TEMB, MID_CHANNELS)), ('down_two', (3, 3, MID_CHANNELS, MID_CHANNELS)), ('down_skip', (NF, MID_CHANNELS)), ('attn_qkv', (MID_CHANNELS, 3 * MID_CHANNELS)), ('attn_out', (MID_CHANNELS, MID_CHANNELS)), ('up_one', (3, 3, MID_CHANNELS, NF)), ('up_time', (TEMB, NF)), ('up_two', (3, 3, NF, NF)), ('up_skip', (MID_CHANNELS, NF)), ('conv_out', (3, 3, 2 * NF, CHAN))]

def small_layout():
    return [('temb_one_b', TEMB), ('temb_two_b', TEMB), ('conv_in_b', NF), ('pyramid_b', MID_CHANNELS), ('down_gain_a', NF), ('down_bias_a', NF), ('down_one_b', MID_CHANNELS), ('down_time_b', MID_CHANNELS), ('down_gain_b', MID_CHANNELS), ('down_bias_b', MID_CHANNELS), ('down_two_b', MID_CHANNELS), ('down_skip_b', MID_CHANNELS), ('attn_gain', MID_CHANNELS), ('attn_bias', MID_CHANNELS), ('query_b', MID_CHANNELS), ('value_b', MID_CHANNELS), ('attn_out_b', MID_CHANNELS), ('up_gain_a', MID_CHANNELS), ('up_bias_a', MID_CHANNELS), ('up_one_b', NF), ('up_time_b', NF), ('up_gain_b', NF), ('up_bias_b', NF), ('up_two_b', NF), ('up_skip_b', NF), ('final_gain', 2 * NF), ('final_bias', 2 * NF), ('conv_out_b', CHAN)]

def unpack(flat, layout):
    result = {}
    offset = 0
    for label, shape in layout:
        dims = shape if isinstance(shape, tuple) else (shape,)
        length = math.prod(dims)
        result[label] = flat[offset:offset + length].reshape(dims)
        offset += length
    return result

def fir_down(side):
    rows = jnp.arange(side // 2)[:, None]
    cols = jnp.arange(side)[None, :]
    offset = cols - 2 * rows + 1
    taps = jnp.where((offset == 0) | (offset == 3), 1.0, 0.0) + jnp.where((offset == 1) | (offset == 2), 3.0, 0.0)
    return (taps / 8.0).astype(jnp.float32)

def resample(value, matrix):
    value = jnp.einsum('ih,bhwc->biwc', matrix, value, precision=HIGH_PRECISION)
    return jnp.einsum('jw,biwc->bijc', matrix, value, precision=HIGH_PRECISION)

def conv_three(value, kernel):
    return lax.conv_general_dilated(value, kernel, (1, 1), 'SAME', dimension_numbers=('NHWC', 'HWIO', 'NHWC'), precision=HIGH_PRECISION)

def dense(value, matrix):
    return jnp.einsum('...c,cd->...d', value, matrix, precision=HIGH_PRECISION)

def swish(value):
    return value * jax.nn.sigmoid(value)

def group_norm(value, gain, bias):
    batch, height, width, chans = value.shape
    grouped = value.reshape(batch, height, width, GROUPS, chans // GROUPS)
    center = lax.optimization_barrier(jnp.mean(grouped, axis=(1, 2, 4), keepdims=True))
    spread = lax.optimization_barrier(jnp.mean((grouped - center) ** 2, axis=(1, 2, 4), keepdims=True))
    normed = ((grouped - center) * lax.rsqrt(spread + 1e-06)).reshape(value.shape)
    return normed * gain + bias

def network(mats, smalls, noisy, sigma, freq, rounding_helper):
    phase = jnp.log(sigma)[:, None] * freq[None, :] * (2.0 * math.pi)
    features = jnp.concatenate([jnp.sin(phase), jnp.cos(phase)], axis=-1)
    time_embed = dense(rounding_helper(features), mats['temb_one']) + smalls['temb_one_b']
    time_embed = dense(rounding_helper(swish(time_embed)), mats['temb_two']) + smalls['temb_two_b']
    time_act = rounding_helper(swish(time_embed))
    first = conv_three(rounding_helper(noisy), mats['conv_in']) + smalls['conv_in_b']
    shrink = fir_down(IMG)
    branch = resample(swish(group_norm(first, smalls['down_gain_a'], smalls['down_bias_a'])), shrink)
    branch = conv_three(rounding_helper(branch), mats['down_one']) + smalls['down_one_b'] + (dense(time_act, mats['down_time']) + smalls['down_time_b'])[:, None, None, :]
    branch = swish(group_norm(branch, smalls['down_gain_b'], smalls['down_bias_b']))
    branch = conv_three(rounding_helper(branch), mats['down_two']) + smalls['down_two_b']
    skipped = dense(rounding_helper(resample(first, shrink)), mats['down_skip']) + smalls['down_skip_b']
    lower = (branch + skipped) * INV_ROOT
    lower = (lower + dense(rounding_helper(resample(noisy, shrink)), mats['pyramid']) + smalls['pyramid_b']) * INV_ROOT
    batch = lower.shape[0]
    normed = rounding_helper(group_norm(lower, smalls['attn_gain'], smalls['attn_bias'])).reshape(batch, -1, MID_CHANNELS)
    projected = dense(normed, mats['attn_qkv'])
    query_rows = rounding_helper(projected[..., :MID_CHANNELS] + smalls['query_b'])
    key_rows = rounding_helper(projected[..., MID_CHANNELS:2 * MID_CHANNELS])
    value_rows = rounding_helper(projected[..., 2 * MID_CHANNELS:] + smalls['value_b'])
    attention_scores = jnp.einsum('zan,zin->zai', query_rows, key_rows, precision=HIGH_PRECISION) * MID_CHANNELS ** (-0.5)
    attention_probabilities = rounding_helper(jax.nn.softmax(attention_scores, axis=-1))
    attended_values = rounding_helper(jnp.einsum('tdg,tgj->tdj', attention_probabilities, value_rows, precision=HIGH_PRECISION))
    attended = dense(attended_values, mats['attn_out']) + smalls['attn_out_b']
    middle = (lower + attended.reshape(lower.shape)) * INV_ROOT
    grow = 2.0 * fir_down(IMG).T
    branch = resample(swish(group_norm(middle, smalls['up_gain_a'], smalls['up_bias_a'])), grow)
    branch = conv_three(rounding_helper(branch), mats['up_one']) + smalls['up_one_b'] + (dense(time_act, mats['up_time']) + smalls['up_time_b'])[:, None, None, :]
    branch = swish(group_norm(branch, smalls['up_gain_b'], smalls['up_bias_b']))
    branch = conv_three(rounding_helper(branch), mats['up_two']) + smalls['up_two_b']
    skipped = dense(rounding_helper(resample(middle, grow)), mats['up_skip']) + smalls['up_skip_b']
    upper = (branch + skipped) * INV_ROOT
    final = swish(group_norm(jnp.concatenate([upper, first], axis=-1), smalls['final_gain'], smalls['final_bias']))
    return conv_three(rounding_helper(final), mats['conv_out']) + smalls['conv_out_b']

def device_errors(mats, smalls, images, noise, sigma, freq, rounding_helper):
    noisy = (images + sigma[:, None] * noise).reshape(-1, IMG, IMG, CHAN)
    output = network(mats, smalls, noisy, sigma, freq, rounding_helper).reshape(images.shape)
    score = output / sigma[:, None]
    return score * sigma[:, None] + noise

def adamw(weight, moment, second, grad, rate):
    moment_new = 0.5 * moment + 0.5 * grad
    second_new = 0.99 * second + 0.01 * grad * grad
    direction = moment_new / (1.0 - 0.5 ** STEP) / (jnp.sqrt(second_new / (1.0 - 0.99 ** STEP)) + 1e-08)
    return (weight - rate * (direction + 0.01 * weight), moment_new, second_new)

def reference(params, first_moment, second_moment, smalls, small_first, small_second, images, noise, sigma, freq, counts, partner):
    devices = counts.shape[0]

    def loss_of(weights, gains):
        mats = unpack(low(weights), mat_layout())
        vectors = unpack(low(gains), small_layout())

        def one_device(group):
            return device_errors(mats, vectors, group[0], group[1], group[2], freq, low)
        errors = lax.map(jax.checkpoint(one_device), (images.reshape(devices, SLOTS, PIX), noise.reshape(devices, SLOTS, PIX), sigma.reshape(devices, SLOTS)))
        index = jnp.arange(devices, dtype=jnp.int32)
        other = (jnp.bitwise_xor(index // N_NARROW, N_WIDE // 2) * N_NARROW + index % N_NARROW).astype(jnp.int32)
        paired = errors[other[:, None], partner]
        live = (jnp.arange(SLOTS, dtype=jnp.int32)[None, :] < counts[:, None]).astype(jnp.float32)
        own_term = 0.5 * lax.optimization_barrier(jnp.mean(errors * errors, axis=-1))
        pair_term = 0.25 * lax.optimization_barrier(jnp.mean((errors - paired) ** 2, axis=-1))
        return jnp.sum(live * (own_term + pair_term)) / jnp.sum(counts).astype(jnp.float32)
    loss, pullback = jax.vjp(loss_of, params, smalls)
    grad_params, grad_smalls = pullback(jnp.ones((), jnp.float32))
    grad_norm = jnp.sqrt(jnp.sum(grad_params * grad_params) + jnp.sum(grad_smalls * grad_smalls))
    factor = jnp.minimum(1.0, 0.01 / (grad_norm + 1e-06))
    clipped = factor * grad_params
    small_grad = factor * grad_smalls
    new_params, new_first, new_second = adamw(params, first_moment, second_moment, clipped, 0.15)
    new_smalls, new_small_first, new_small_second = adamw(smalls, small_first, small_second, small_grad, 0.2)
    return (loss, grad_norm, new_params, new_first, new_second, new_smalls, new_small_first, new_small_second, small_grad)
```

```python
import functools
import math
from types import SimpleNamespace

import jax
import jax.numpy as jnp
import numpy as np
from jax import lax
from jax.experimental import pallas as pl
from jax.experimental.pallas import tpu as pltpu
from jax.sharding import PartitionSpec as P

NF = 128
MID = 256
TEMB = 512
NFOUR = 128
IMG = 32
GROUPS = 32
CHAN = 3
STEP = 7
PIX = IMG * IMG
HALF = PIX // 4
INV_ROOT = 0.7071067811865476
WIDE, NARROW = AXES = ("wide", "narrow")
F32 = jnp.float32
BF16 = jnp.bfloat16

LANES = 128
BLOCKS = 32
ROWS = 552
SMALL_ROWS = 2
BLOCK = 560


def mat_layout():
    return dict(
        temb_one=(2 * NFOUR, TEMB),
        temb_two=(TEMB, TEMB),
        conv_in=(9 * CHAN, NF),
        pyramid=(CHAN, MID),
        down_one=(9 * NF, MID),
        down_time=(TEMB, MID),
        down_two=(9 * MID, MID),
        down_skip=(NF, MID),
        attn_qkv=(MID, 3 * MID),
        attn_out=(MID, MID),
        up_one=(9 * MID, NF),
        up_time=(TEMB, NF),
        up_two=(9 * NF, NF),
        up_skip=(MID, NF),
        conv_out=(9 * 2 * NF, CHAN),
    )


def small_layout():
    return dict(
        temb_one_b=TEMB,
        temb_two_b=TEMB,
        conv_in_b=NF,
        pyramid_b=MID,
        down_gain_a=NF,
        down_bias_a=NF,
        down_one_b=MID,
        down_time_b=MID,
        down_gain_b=MID,
        down_bias_b=MID,
        down_two_b=MID,
        down_skip_b=MID,
        attn_gain=MID,
        attn_bias=MID,
        query_b=MID,
        value_b=MID,
        attn_out_b=MID,
        up_gain_a=MID,
        up_bias_a=MID,
        up_one_b=NF,
        up_time_b=NF,
        up_gain_b=NF,
        up_bias_b=NF,
        up_two_b=NF,
        up_skip_b=NF,
        final_gain=2 * NF,
        final_bias=2 * NF,
        conv_out_b=CHAN,
    )


def offsets():
    mats, smalls, used = {}, {}, 0
    for label, shape in mat_layout().items():
        mats[label] = (used // LANES,) + shape
        used += math.prod(shape)
    used = 0
    for label, length in small_layout().items():
        smalls[label] = (used // LANES, length)
        used += length
    return SimpleNamespace(**mats), SimpleNamespace(**smalls)


MATS, SMALLS = offsets()
WEIGHTS = list(mat_layout())
WEIGHT_SHAPES = mat_layout() | dict(conv_in=(32, NF), pyramid=(16, MID), conv_out=(LANES, 2 * NF))
TAPS = [(dy, dx) for dy in range(3) for dx in range(3)]


def pixel_order(side):
    across, down = side // 8, side // 2
    order = np.empty((across, down, 2, 8), np.int32)
    for xl in range(across):
        for yl in range(down):
            for yh in range(2):
                for xh in range(8):
                    order[xl, yl, yh, xh] = (yh * down + yl) * side + xh * across + xl
    return order.reshape(-1)


def fir_matrix():
    rows = np.arange(IMG // 2)[:, None]
    cols = np.arange(IMG)[None, :]
    offset = cols - 2 * rows + 1
    taps = np.where((offset == 0) | (offset == 3), 1.0, 0.0) + np.where(
        (offset == 1) | (offset == 2), 3.0, 0.0
    )
    both = np.kron(taps / 8.0, taps / 8.0)
    return both[pixel_order(IMG // 2)][:, pixel_order(IMG)].astype(np.float32)


def to_order(value):
    shape = value.shape
    value = value.reshape(shape[0], 2, 16, 8, 4, shape[2])
    return value.transpose(0, 4, 2, 1, 3, 5).reshape(shape)


def dot(a, b):
    return lax.dot_general(a, b, (((1,), (0,)), ((), ())), preferred_element_type=F32)


def dot_nt(a, b):
    return lax.dot_general(a, b, (((1,), (1,)), ((), ())), preferred_element_type=F32)


def dot_tn(a, b):
    return lax.dot_general(a, b, (((0,), (0,)), ((), ())), preferred_element_type=F32)


def two(value):
    high = value.astype(BF16)
    return high, (value - high.astype(F32)).astype(BF16)


def sigmoid(value):
    return 1.0 / (1.0 + jnp.exp(-value))


def rowsum(value):
    return jnp.sum(value, axis=0, keepdims=True)


def group_sums(rows, width):
    chans = rows[0].shape[1]
    at = lax.broadcasted_iota(jnp.int32, (16, chans), 0)
    stack = jnp.zeros((16, chans), F32)
    for n, row in enumerate(rows):
        rest = row
        for part in range(3):
            piece = rest.astype(BF16).astype(F32)
            stack = jnp.where(at == 3 * n + part, piece, stack)
            rest = rest - piece
    one = lax.broadcasted_iota(jnp.int32, (chans, chans), 0) // width
    other = lax.broadcasted_iota(jnp.int32, (chans, chans), 1) // width
    same = jnp.where(one == other, 1.0, 0.0).astype(BF16)
    sums = dot(stack.astype(BF16), same)
    return [sums[3 * n : 3 * n + 1] + sums[3 * n + 1 : 3 * n + 2] + sums[3 * n + 2 : 3 * n + 3] for n in range(len(rows))]


def norm_stats(value, width):
    count = float(value.shape[0] * width)
    center = group_sums([rowsum(value)], width)[0] / count
    shifted = value - center
    spread = group_sums([rowsum(shifted * shifted)], width)[0] / count
    return center, lax.rsqrt(spread + 1e-06)


def norm_back(grad, normed, gain, scale, width):
    count = float(grad.shape[0] * width)
    dbias = rowsum(grad)
    dgain = rowsum(grad * normed)
    first, second = group_sums([dbias * gain, dgain * gain], width)
    back = scale * (grad * gain - first / count - normed * (second / count))
    return back, dgain, dbias


def swish_back(pre):
    gate = sigmoid(pre)
    return gate * (1.0 + pre * (1.0 - gate))


def small(ref, label):
    at, length = label
    rows = max(1, length // LANES)
    return jnp.concatenate(
        [ref[(at + i) // 2, (at + i) % 2 : (at + i) % 2 + 1, :] for i in range(rows)], axis=1
    ) if rows > 1 else ref[at // 2, at % 2 : at % 2 + 1, :]


def add_small(ref, label, value):
    at, _ = label
    for i in range(value.shape[1] // LANES):
        j = at + i
        ref[j // 2, j % 2 : j % 2 + 1, :] += value[:, i * LANES : (i + 1) * LANES]


def fill_halo(ref, b, across, down):
    chans = ref.shape[-1]
    zero = jnp.zeros((across, 8, chans), F32)
    last = ref[b, 1 : across + 1, down].astype(F32)
    ref[b, 1 : across + 1, 0] = jnp.concatenate([zero, last[:, 0:8]], axis=1).astype(BF16)
    first = ref[b, 1 : across + 1, 1].astype(F32)
    ref[b, 1 : across + 1, down + 1] = jnp.concatenate([first[:, 8:16], zero], axis=1).astype(BF16)
    tiles = (down + 2) * 2
    at = lax.broadcasted_iota(jnp.int32, (tiles, 8, chans), 1)
    side = ref[b, across].astype(F32).reshape(tiles, 8, chans)
    side = jnp.where(at == 0, 0.0, pltpu.roll(side, 1, axis=1))
    ref[b, 0] = side.reshape(down + 2, 16, chans).astype(BF16)
    side = ref[b, 1].astype(F32).reshape(tiles, 8, chans)
    side = jnp.where(at == 7, 0.0, pltpu.roll(side, 7, axis=1))
    ref[b, across + 1] = side.reshape(down + 2, 16, chans).astype(BF16)


def set_inner(ref, b, across, down, value):
    chans = value.shape[1]
    ref[b, 1 : across + 1, 1 : down + 1] = value.astype(BF16).reshape(across, down, 16, chans)
    fill_halo(ref, b, across, down)


def taps_of(ref, b, xl, count, down, flip):
    chans = ref.shape[-1]
    parts = []
    for dy, dx in TAPS:
        y, x = (2 - dy, 2 - dx) if flip else (dy, dx)
        parts.append(ref[b, xl + x : xl + x + count, y : y + down].reshape(count * down * 16, chans))
    return jnp.concatenate(parts, axis=1)


def tap_columns(ref, chans):
    return jnp.concatenate([ref[t * chans : (t + 1) * chans, :] for t in range(9)], axis=1)


def picks(o):
    row = lax.broadcasted_iota(jnp.int32, (6 * LANES, 2 * NF), 0)
    col = lax.broadcasted_iota(jnp.int32, (6 * LANES, 2 * NF), 1)
    return jnp.where(row == CHAN * col + o, 1.0, 0.0).astype(BF16)


SAVED = dict(
    h0=((PIX, NF), F32),
    ed1=((4, 10, 16, NF), BF16),
    sk0=((HALF, NF), BF16),
    a1=((HALF, MID), F32),
    ed2=((4, 10, 16, MID), BF16),
    h1=((HALF, MID), F32),
    g=((HALF, MID), BF16),
    qkv=((HALF, 3 * MID), BF16),
    prob=((HALF, HALF), BF16),
    mixed=((HALF, MID), BF16),
    h2=((HALF, MID), F32),
    eu1=((6, 18, 16, MID), BF16),
    sku=((PIX, MID), BF16),
    b1=((PIX, NF), F32),
    eu2=((6, 18, 16, NF), BF16),
    h3=((PIX, NF), F32),
    final=((PIX, 2 * NF), BF16),
    stats=((16, MID), F32),
)
TIME_SAVED = dict(
    t1=((8, TEMB), F32),
    s1=((8, TEMB), BF16),
    t2=((8, TEMB), F32),
    tact=((8, TEMB), BF16),
)


def forward_kernel(piece_marks, slots, names, *refs):
    r_pieces, refs = refs[: len(piece_marks)], refs[len(piece_marks) :]
    r = SimpleNamespace(**dict(zip(names, refs)))
    me = r.me[0]
    stage, sm = r.stage, r.sm
    for n, marks in enumerate(piece_marks):
        for i, mark in enumerate(marks):
            home = jnp.bitwise_xor(me, mark)
            block = r_pieces[n][i].astype(F32)
            stage[pl.ds(pl.multiple_of(home * ROWS, 8), ROWS), :] = block[:ROWS]
            sm[home] = block[ROWS:]
    for label in WEIGHTS:
        at, depth, width = getattr(MATS, label)
        out = getattr(r, "w_" + label)
        if width == CHAN:
            flat = jnp.concatenate([stage[pl.ds(at + i, 9, stride=6), :] for i in range(6)], axis=1).astype(BF16)
            out[...] = jnp.zeros(out.shape, BF16)
            pad = jnp.zeros((7, 2 * NF), F32)
            for o in range(CHAN):
                out[16 * o : 16 * o + 16, :] = jnp.concatenate([dot(flat, picks(o)), pad], axis=0).astype(BF16)
            continue
        pad = out.shape[0] - depth
        for j in range(width // LANES):
            part = stage[pl.ds(at + j, depth, stride=width // LANES), :] if width > LANES else stage[pl.ds(at, depth), :]
            if pad:
                part = jnp.concatenate([part, jnp.zeros((pad, LANES), F32)], axis=0)
            out[:, j * LANES : (j + 1) * LANES] = part.astype(BF16)

    t1 = dot(r.feats[...], r.w_temb_one[...]) + small(sm, SMALLS.temb_one_b)
    r.t1[...] = t1
    s1 = (t1 * sigmoid(t1)).astype(BF16)
    r.s1[...] = s1
    t2 = dot(s1, r.w_temb_two[...]) + small(sm, SMALLS.temb_two_b)
    r.t2[...] = t2
    tact = (t2 * sigmoid(t2)).astype(BF16)
    r.tact[...] = tact
    r.pd[...] = dot(tact, r.w_down_time[...]) + (small(sm, SMALLS.down_time_b) + small(sm, SMALLS.down_one_b))
    r.pu[...] = dot(tact, r.w_up_time[...]) + (small(sm, SMALLS.up_time_b) + small(sm, SMALLS.up_one_b))

    def image(b, carry):
        stats = r.stats

        def normed(value, width, gain, bias, at):
            center, scale = norm_stats(value, width)
            chans = value.shape[1]
            stats[b, 2 * at : 2 * at + 1, :chans] = center
            stats[b, 2 * at + 1 : 2 * at + 2, :chans] = scale
            return (value - center) * (scale * gain) + bias

        h0 = dot(r.xcol[b], r.w_conv_in[...]) + small(sm, SMALLS.conv_in_b)
        r.h0[b] = h0
        y = normed(h0, 4, small(sm, SMALLS.down_gain_a), small(sm, SMALLS.down_bias_a), 0)
        y = y * sigmoid(y)
        down = dot(r.shrink[...], jnp.concatenate([*two(y), *two(h0)], axis=1))
        set_inner(r.ed1, b, 2, 8, down[:, :NF] + down[:, NF : 2 * NF])
        sk0 = (down[:, 2 * NF : 3 * NF] + down[:, 3 * NF :]).astype(BF16)
        r.sk0[b] = sk0
        a1 = dot(taps_of(r.ed1, b, 0, 2, 8, False), r.w_down_one[...]) + r.pd[pl.ds(b, 1), :]
        r.a1[b] = a1
        y = normed(a1, 8, small(sm, SMALLS.down_gain_b), small(sm, SMALLS.down_bias_b), 1)
        set_inner(r.ed2, b, 2, 8, y * sigmoid(y))
        a2 = dot(taps_of(r.ed2, b, 0, 2, 8, False), r.w_down_two[...]) + dot(sk0, r.w_down_skip[...])
        a2 = (a2 + (small(sm, SMALLS.down_two_b) + small(sm, SMALLS.down_skip_b))) * INV_ROOT
        h1 = (a2 + dot(r.tiny[b], r.w_pyramid[...]) + small(sm, SMALLS.pyramid_b)) * INV_ROOT
        r.h1[b] = h1
        g = normed(h1, 8, small(sm, SMALLS.attn_gain), small(sm, SMALLS.attn_bias), 2).astype(BF16)
        r.g[b] = g
        proj = dot(g, r.w_attn_qkv[...])
        q = (proj[:, :MID] + small(sm, SMALLS.query_b)).astype(BF16)
        k = proj[:, MID : 2 * MID].astype(BF16)
        v = (proj[:, 2 * MID :] + small(sm, SMALLS.value_b)).astype(BF16)
        r.qkv[b] = jnp.concatenate([q, k, v], axis=1)
        scores = dot_nt(q, k) * (MID**-0.5)
        weight = jnp.exp(scores - jnp.max(scores, axis=1, keepdims=True))
        prob = (weight / jnp.sum(weight, axis=1, keepdims=True)).astype(BF16)
        r.prob[b] = prob
        mixed = dot(prob, v).astype(BF16)
        r.mixed[b] = mixed
        h2 = (h1 + dot(mixed, r.w_attn_out[...]) + small(sm, SMALLS.attn_out_b)) * INV_ROOT
        r.h2[b] = h2
        y = normed(h2, 8, small(sm, SMALLS.up_gain_a), small(sm, SMALLS.up_bias_a), 3)
        y = y * sigmoid(y)
        coarse = jnp.concatenate([*two(y), *two(h2)], axis=1)
        for xl in range(4):
            fine = dot(r.grow[xl * 256 : (xl + 1) * 256, :], coarse)
            part = (fine[:, :MID] + fine[:, MID : 2 * MID]).astype(BF16)
            r.eu1[b, xl + 1, 1:17] = part.reshape(16, 16, MID)
            r.sku[b, xl * 256 : (xl + 1) * 256, :] = (fine[:, 2 * MID : 3 * MID] + fine[:, 3 * MID :]).astype(BF16)
        fill_halo(r.eu1, b, 4, 16)
        for xl in range(4):
            r.b1[b, xl * 256 : (xl + 1) * 256, :] = (
                dot(taps_of(r.eu1, b, xl, 1, 16, False), r.w_up_one[...]) + r.pu[pl.ds(b, 1), :]
            )
        y = normed(r.b1[b], 4, small(sm, SMALLS.up_gain_b), small(sm, SMALLS.up_bias_b), 4)
        set_inner(r.eu2, b, 4, 16, y * sigmoid(y))
        bias = small(sm, SMALLS.up_two_b) + small(sm, SMALLS.up_skip_b)
        for xl in range(4):
            part = slice(xl * 256, (xl + 1) * 256)
            up = dot(taps_of(r.eu2, b, xl, 1, 16, False), r.w_up_two[...])
            r.h3[b, part, :] = (up + dot(r.sku[b, part, :], r.w_up_skip[...]) + bias) * INV_ROOT
        gain, bias = small(sm, SMALLS.final_gain), small(sm, SMALLS.final_bias)
        y = normed(r.h3[b], 8, gain[:, :NF], bias[:, :NF], 5)
        r.final[b, :, :NF] = (y * sigmoid(y)).astype(BF16)
        y = normed(r.h0[b], 8, gain[:, NF:], bias[:, NF:], 6)
        r.final[b, :, NF:] = (y * sigmoid(y)).astype(BF16)
        wide = dot_nt(r.final[b], r.w_conv_out[...])
        field = r.field
        set_field(field, wide)
        lane = lax.broadcasted_iota(jnp.int32, (PIX, LANES), 1) % 16
        total = jnp.zeros((PIX, LANES), F32)
        for t, (dy, dx) in enumerate(TAPS):
            total = jnp.where(lane == t, field[dx : dx + 4, dy : dy + 16].reshape(PIX, LANES), total)
        high, rest = two(total)
        fold = colour_fold()
        out = dot_nt(fold, high) + dot_nt(fold, rest)
        bias = r.out_bias[...]
        r.err[b] = out + bias + r.noise[b]
        return carry

    prepare_out_bias(r, sm)
    lax.fori_loop(0, slots, image, 0)


def prepare_out_bias(r, sm):
    bias = small(sm, SMALLS.conv_out_b)
    row = lax.broadcasted_iota(jnp.int32, (8, LANES), 0)
    lane = lax.broadcasted_iota(jnp.int32, (8, LANES), 1)
    own = jnp.sum(jnp.where((lane == row) & (row < CHAN), bias, 0.0), axis=1, keepdims=True)
    r.out_bias[...] = jnp.broadcast_to(own, (8, PIX))


def colour_fold():
    row = lax.broadcasted_iota(jnp.int32, (16, LANES), 0)
    lane = lax.broadcasted_iota(jnp.int32, (16, LANES), 1)
    return jnp.where((lane // 16 == row) & (lane % 16 < 9) & (row < CHAN), 1.0, 0.0).astype(BF16)[:8]


def set_field(field, value):
    field[1:5, 1:17] = value.reshape(4, 16, 16, LANES)
    zero = jnp.zeros((4, 8, LANES), F32)
    field[1:5, 0] = jnp.concatenate([zero, field[1:5, 16, 0:8]], axis=1)
    field[1:5, 17] = jnp.concatenate([field[1:5, 1, 8:16], zero], axis=1)
    at = lax.broadcasted_iota(jnp.int32, (36, 8, LANES), 1)
    side = pltpu.roll(field[4].reshape(36, 8, LANES), 1, axis=1)
    field[0] = jnp.where(at == 0, 0.0, side).reshape(18, 16, LANES)
    side = pltpu.roll(field[1].reshape(36, 8, LANES), 7, axis=1)
    field[5] = jnp.where(at == 7, 0.0, side).reshape(18, 16, LANES)


def backward_kernel(slots, names, *refs):
    r = SimpleNamespace(**dict(zip(names, refs)))
    me = r.me[0]
    sm, stage, gsm = r.sm, r.stage, r.gsm
    stats = r.stats
    total = r.total[0]
    gsm[...] = jnp.zeros(gsm.shape, F32)
    r.dpd[...] = jnp.zeros(r.dpd.shape, F32)
    r.dpu[...] = jnp.zeros(r.dpu.shape, F32)
    r.dout_sum[...] = jnp.zeros(r.dout_sum.shape, F32)
    r.loss[...] = jnp.zeros(r.loss.shape, F32)
    counts, pairs = r.ints[0], r.ints
    other_counts = r.other_ints[0]

    def put(label, value, first=0):
        at, _, width = label
        step = width // LANES
        for j in range(step):
            part = value[:, j * LANES : (j + 1) * LANES]
            if step == 1:
                stage[pl.ds(at + first, value.shape[0]), :] = part
            else:
                stage[pl.ds(at + first * step + j, value.shape[0], stride=step), :] = part

    def image(b, carry):
        def stat(at, chans):
            return stats[b, 2 * at : 2 * at + 1, :chans], stats[b, 2 * at + 1 : 2 * at + 2, :chans]

        def renorm(value, at, gain, bias):
            center, scale = stat(at, value.shape[1])
            normed = (value - center) * scale
            return normed, normed * gain + bias, scale

        err = r.err[b]
        mine = r.other[pairs[1 + b]].astype(F32)
        gap = err - mine
        live = jnp.where(b < counts, 1.0, 0.0)
        scale = 1.0 / (total * (CHAN * PIX))
        r.loss[...] += (live * scale) * (0.5 * err * err + 0.25 * gap * gap)
        grad = (live * scale) * (err + 0.5 * gap)
        for s in range(slots):
            theirs = r.other[s].astype(F32)
            on = jnp.where((r.other_ints[1 + s] == b) & (s < other_counts), 0.5 * scale, 0.0)
            grad += on * (err - theirs)
        r.dout_sum[...] += grad
        spread = dot_tn_field(grad)
        field = r.field
        set_field(field, spread)
        lane = lax.broadcasted_iota(jnp.int32, (PIX, LANES), 1) % 16
        cols = jnp.zeros((PIX, LANES), F32)
        for t, (dy, dx) in enumerate(TAPS):
            cols = jnp.where(lane == t, field[2 - dx : 6 - dx, 2 - dy : 18 - dy].reshape(PIX, LANES), cols)
        cols = cols.astype(BF16)
        r.cols[b] = cols
        gain, bias = small(sm, SMALLS.final_gain), small(sm, SMALLS.final_bias)
        back = dot(cols, r.w_conv_out[...])
        n3, y3, scale3 = renorm(r.h3[b], 5, gain[:, :NF], bias[:, :NF])
        dh3, dgain, dbias = norm_back(back[:, :NF] * swish_back(y3), n3, gain[:, :NF], scale3, 8)
        n0, y0, scale0 = renorm(r.h0[b], 6, gain[:, NF:], bias[:, NF:])
        dh0, dgain0, dbias0 = norm_back(back[:, NF:] * swish_back(y0), n0, gain[:, NF:], scale0, 8)
        add_small(gsm, SMALLS.final_gain, jnp.concatenate([dgain, dgain0], axis=1))
        add_small(gsm, SMALLS.final_bias, jnp.concatenate([dbias, dbias0], axis=1))
        r.dh0[b] = dh0
        dh3 = dh3 * INV_ROOT
        add_small(gsm, SMALLS.up_two_b, rowsum(dh3))
        set_inner(r.gu2, b, 4, 16, dh3)
        turned = tap_columns(r.w_up_two, NF)
        for xl in range(4):
            r.wide[xl * 256 : (xl + 1) * 256, :NF] = dot_nt(taps_of(r.gu2, b, xl, 1, 16, True), turned)
        gain, bias = small(sm, SMALLS.up_gain_b), small(sm, SMALLS.up_bias_b)
        n, y, scale1 = renorm(r.b1[b], 4, gain, bias)
        db1, dgain, dbias = norm_back(r.wide[:, :NF] * swish_back(y), n, gain, scale1, 4)
        add_small(gsm, SMALLS.up_gain_b, dgain)
        add_small(gsm, SMALLS.up_bias_b, dbias)
        r.dpu[pl.ds(b, 1), :] = rowsum(db1)
        set_inner(r.gu1, b, 4, 16, db1)
        turned = tap_columns(r.w_up_one, MID)
        half = jnp.zeros((HALF, 2 * MID), F32)
        for xl in range(4):
            branch = dot_nt(taps_of(r.gu1, b, xl, 1, 16, True), turned)
            skip = dot_nt(r.gu2[b, xl + 1, 1:17].reshape(256, NF), r.w_up_skip[...])
            both = jnp.concatenate([branch.astype(BF16), skip.astype(BF16)], axis=1)
            half += dot(r.shrink[:, xl * 256 : (xl + 1) * 256], both)
        half = half * 4.0
        gain, bias = small(sm, SMALLS.up_gain_a), small(sm, SMALLS.up_bias_a)
        n, y, scale2 = renorm(r.h2[b], 3, gain, bias)
        dh2, dgain, dbias = norm_back(half[:, :MID] * swish_back(y), n, gain, scale2, 8)
        add_small(gsm, SMALLS.up_gain_a, dgain)
        add_small(gsm, SMALLS.up_bias_a, dbias)
        dh2 = (dh2 + half[:, MID:]) * INV_ROOT
        add_small(gsm, SMALLS.attn_out_b, rowsum(dh2))
        datt = dh2.astype(BF16)
        r.datt[b] = datt
        dmixed = dot_nt(datt, r.w_attn_out[...]).astype(BF16)
        q, k, v = r.qkv[b, :, :MID], r.qkv[b, :, MID : 2 * MID], r.qkv[b, :, 2 * MID :]
        prob = r.prob[b]
        dprob = dot_nt(dmixed, v)
        dv = dot_tn(prob, dmixed)
        wide = prob.astype(F32)
        dscore = wide * (dprob - jnp.sum(wide * dprob, axis=1, keepdims=True))
        dscore = (dscore * (MID**-0.5)).astype(BF16)
        dq = dot(dscore, k)
        dk = dot_tn(dscore, q)
        add_small(gsm, SMALLS.query_b, rowsum(dq))
        add_small(gsm, SMALLS.value_b, rowsum(dv))
        dqkv = jnp.concatenate([dq, dk, dv], axis=1).astype(BF16)
        r.dqkv[b] = dqkv
        dg = dot_nt(dqkv, r.w_attn_qkv[...])
        gain, bias = small(sm, SMALLS.attn_gain), small(sm, SMALLS.attn_bias)
        n, _, scale2 = renorm(r.h1[b], 2, gain, bias)
        dh1, dgain, dbias = norm_back(dg, n, gain, scale2, 8)
        add_small(gsm, SMALLS.attn_gain, dgain)
        add_small(gsm, SMALLS.attn_bias, dbias)
        dh1 = (dh1 + dh2) * INV_ROOT
        r.dpyr[b] = dh1.astype(BF16)
        add_small(gsm, SMALLS.pyramid_b, rowsum(dh1))
        da2 = dh1 * INV_ROOT
        add_small(gsm, SMALLS.down_two_b, rowsum(da2))
        set_inner(r.gd2, b, 2, 8, da2)
        dsk0 = dot_nt(r.gd2[b, 1:3, 1:9].reshape(HALF, MID), r.w_down_skip[...])
        turned = tap_columns(r.w_down_two, MID)
        du = dot_nt(taps_of(r.gd2, b, 0, 2, 8, True), turned)
        gain, bias = small(sm, SMALLS.down_gain_b), small(sm, SMALLS.down_bias_b)
        n, y, scale2 = renorm(r.a1[b], 1, gain, bias)
        da1, dgain, dbias = norm_back(du * swish_back(y), n, gain, scale2, 8)
        add_small(gsm, SMALLS.down_gain_b, dgain)
        add_small(gsm, SMALLS.down_bias_b, dbias)
        r.dpd[pl.ds(b, 1), :] = rowsum(da1)
        set_inner(r.gd1, b, 2, 8, da1)
        turned = tap_columns(r.w_down_one, NF)
        dd0 = dot_nt(taps_of(r.gd1, b, 0, 2, 8, True), turned)
        both = jnp.concatenate([dd0, dsk0], axis=1).astype(BF16)
        fine = dot(r.grow[...], both) * 0.25
        gain, bias = small(sm, SMALLS.down_gain_a), small(sm, SMALLS.down_bias_a)
        n, y, scale1 = renorm(r.h0[b], 0, gain, bias)
        back0, dgain, dbias = norm_back(fine[:, :NF] * swish_back(y), n, gain, scale1, 4)
        add_small(gsm, SMALLS.down_gain_a, dgain)
        add_small(gsm, SMALLS.down_bias_a, dbias)
        dh0 = r.dh0[b] + back0 + fine[:, NF:]
        add_small(gsm, SMALLS.conv_in_b, rowsum(dh0))
        r.din[b] = dh0.astype(BF16)
        return carry

    lax.fori_loop(0, slots, image, 0)

    whole = slots * PIX
    fewer = slots * HALF
    dout = dot_tn(r.cols[...].reshape(whole, LANES), r.final[...].reshape(whole, 2 * NF))
    flat = jnp.zeros((16, 6 * LANES), F32)
    for o in range(CHAN):
        flat += dot_nt(dout[16 * o : 16 * o + 16].astype(BF16), picks(o))
    at = MATS.conv_out[0]
    for i in range(6):
        for t in range(9):
            stage[at + 6 * t + i : at + 6 * t + i + 1, :] = flat[t : t + 1, i * LANES : (i + 1) * LANES]

    def conv_grad(label, acts, grads, across, down):
        chans, rows = acts.shape[-1], slots * across * down * 16
        left = acts[:, 1 : across + 1, 1 : down + 1].reshape(rows, chans)
        for dy in range(3):
            right = jnp.concatenate(
                [
                    grads[:, 2 - dx : 2 - dx + across, 2 - dy : 2 - dy + down].reshape(rows, grads.shape[-1])
                    for dx in range(3)
                ],
                axis=1,
            )
            back = dot_tn(left, right)
            for dx in range(3):
                put(label, back[:, dx * grads.shape[-1] : (dx + 1) * grads.shape[-1]], (3 * dy + dx) * chans)

    conv_grad(MATS.up_two, r.eu2, r.gu2, 4, 16)
    conv_grad(MATS.up_one, r.eu1, r.gu1, 4, 16)
    conv_grad(MATS.down_two, r.ed2, r.gd2, 2, 8)
    conv_grad(MATS.down_one, r.ed1, r.gd1, 2, 8)
    put(MATS.up_skip, dot_tn(r.sku[...].reshape(whole, MID), r.gu2[:, 1:5, 1:17].reshape(whole, NF)))
    put(MATS.down_skip, dot_tn(r.sk0[...].reshape(fewer, NF), r.gd2[:, 1:3, 1:9].reshape(fewer, MID)))
    put(MATS.attn_out, dot_tn(r.mixed[...].reshape(fewer, MID), r.datt[...].reshape(fewer, MID)))
    put(MATS.attn_qkv, dot_tn(r.g[...].reshape(fewer, MID), r.dqkv[...].reshape(fewer, 3 * MID)))
    put(MATS.pyramid, dot_tn(r.tiny[...].reshape(fewer, 16), r.dpyr[...].reshape(fewer, MID))[:CHAN])
    put(MATS.conv_in, dot_tn(r.xcol[...].reshape(whole, 32), r.din[...].reshape(whole, NF))[: 9 * CHAN])
    dpd, dpu = r.dpd[...], r.dpu[...]
    for label in (SMALLS.down_time_b, SMALLS.down_one_b):
        add_small(gsm, label, rowsum(dpd))
    for label in (SMALLS.up_time_b, SMALLS.up_one_b):
        add_small(gsm, label, rowsum(dpu))
    dpd16, dpu16 = dpd.astype(BF16), dpu.astype(BF16)
    put(MATS.down_time, dot_tn(r.tact[...], dpd16))
    put(MATS.up_time, dot_tn(r.tact[...], dpu16))
    dtact = dot_nt(dpd16, r.w_down_time[...]) + dot_nt(dpu16, r.w_up_time[...])
    dt2 = dtact * swish_back(r.t2[...])
    add_small(gsm, SMALLS.temb_two_b, rowsum(dt2))
    put(MATS.temb_two, dot_tn(r.s1[...], dt2.astype(BF16)))
    dt1 = dot_nt(dt2.astype(BF16), r.w_temb_two[...]) * swish_back(r.t1[...])
    add_small(gsm, SMALLS.temb_one_b, rowsum(dt1))
    put(MATS.temb_one, dot_tn(r.feats[...], dt1.astype(BF16)))
    for label, twin in ((SMALLS.up_skip_b, SMALLS.up_two_b), (SMALLS.down_skip_b, SMALLS.down_two_b)):
        value = small(gsm, twin)
        add_small(gsm, label, value)
    sums = jnp.sum(r.dout_sum[...], axis=1, keepdims=True)
    row = lax.broadcasted_iota(jnp.int32, (8, LANES), 0)
    lane = lax.broadcasted_iota(jnp.int32, (8, LANES), 1)
    add_small(gsm, SMALLS.conv_out_b, rowsum(jnp.where((row == lane) & (row < CHAN), sums, 0.0)))
    last = MATS.conv_out[0] + 54
    stage[last : BLOCKS * ROWS, :] = jnp.zeros((BLOCKS * ROWS - last, LANES), F32)

    def give(d, carry):
        block = jnp.concatenate([stage[pl.ds(pl.multiple_of(d * ROWS, 8), ROWS), :], gsm[d]], axis=0)
        r.grads[jnp.bitwise_xor(d, me)] = block.astype(BF16)
        return carry

    lax.fori_loop(0, BLOCKS, give, 0)


def dot_tn_field(grad):
    row = lax.broadcasted_iota(jnp.int32, (8, LANES), 0)
    lane = lax.broadcasted_iota(jnp.int32, (8, LANES), 1)
    fan = jnp.where(lane // 16 == row, 1.0, 0.0).astype(BF16)
    return dot_tn(grad.astype(BF16), fan)


def vmem():
    return pl.BlockSpec(memory_space=pltpu.VMEM)


def smem():
    return pl.BlockSpec(memory_space=pltpu.SMEM)


LIMIT = 60 * 1024 * 1024


def run_forward(me, pieces, marks, data):
    slots = data.xcol.shape[0]
    ins = dict(me=me) | vars(data)
    outs = {"w_" + label: (WEIGHT_SHAPES[label], BF16) for label in WEIGHTS}
    outs |= dict(sm=((BLOCKS, 8, LANES), F32)) | TIME_SAVED
    outs |= {label: ((slots,) + shape, dtype) for label, (shape, dtype) in SAVED.items()}
    outs |= dict(err=((slots, 8, PIX), F32))
    scratch = dict(
        stage=((BLOCKS * ROWS, LANES), F32),
        pd=((8, MID), F32),
        pu=((8, NF), F32),
        field=((6, 18, 16, LANES), F32),
        out_bias=((8, PIX), F32),
    )
    names = list(ins) + list(outs) + list(scratch)
    results = pl.pallas_call(
        functools.partial(forward_kernel, marks, slots, names),
        out_shape=[jax.ShapeDtypeStruct(*v) for v in outs.values()],
        in_specs=[vmem()] * len(pieces) + [smem()] + [vmem()] * (len(ins) - 1),
        out_specs=[vmem()] * len(outs),
        scratch_shapes=[pltpu.VMEM(*v) for v in scratch.values()],
        compiler_params=pltpu.CompilerParams(vmem_limit_bytes=LIMIT),
        name="forward",
    )(*pieces, *ins.values())
    return SimpleNamespace(**dict(zip(outs, results)))


def run_backward(me, total, ints, other_ints, other, kept, data):
    slots = other.shape[0]
    ins = dict(me=me, total=total, ints=ints, other_ints=other_ints)
    scalars = len(ins)
    ins |= dict(other=other) | vars(kept)
    ins |= dict(xcol=data.xcol, tiny=data.tiny, feats=data.feats, shrink=data.shrink, grow=data.grow)
    outs = dict(grads=((BLOCKS, BLOCK, LANES), BF16), loss=((8, PIX), F32))
    scratch = dict(
        stage=((BLOCKS * ROWS, LANES), F32),
        gsm=((BLOCKS, 8, LANES), F32),
        dpd=((8, MID), F32),
        dpu=((8, NF), F32),
        dout_sum=((8, PIX), F32),
        field=((6, 18, 16, LANES), F32),
        cols=((slots, PIX, LANES), BF16),
        gu2=((slots, 6, 18, 16, NF), BF16),
        gu1=((slots, 6, 18, 16, NF), BF16),
        gd2=((slots, 4, 10, 16, MID), BF16),
        gd1=((slots, 4, 10, 16, MID), BF16),
        wide=((PIX, NF), F32),
        dh0=((slots, PIX, NF), F32),
        din=((slots, PIX, NF), BF16),
        datt=((slots, HALF, MID), BF16),
        dqkv=((slots, HALF, 3 * MID), BF16),
        dpyr=((slots, HALF, MID), BF16),
    )
    names = list(ins) + list(outs) + list(scratch)
    results = pl.pallas_call(
        functools.partial(backward_kernel, slots, names),
        out_shape=[jax.ShapeDtypeStruct(*v) for v in outs.values()],
        in_specs=[smem()] * scalars + [vmem()] * (len(ins) - scalars),
        out_specs=[vmem()] * len(outs),
        scratch_shapes=[pltpu.VMEM(*v) for v in scratch.values()],
        compiler_params=pltpu.CompilerParams(vmem_limit_bytes=LIMIT),
        name="backward",
    )(*ins.values())
    return SimpleNamespace(**dict(zip(outs, results)))


def swap(value, axis, mask):
    size = lax.axis_size(axis)
    return lax.ppermute(value, axis, [(i, i ^ mask) for i in range(size)])


def sum_everywhere(value):
    for axis in (NARROW, WIDE):
        bit = 1
        while bit < lax.axis_size(axis):
            value = value + swap(value, axis, bit)
            bit *= 2
    return value


def gather_all(params, smalls):
    if lax.axis_size(WIDE) == 4 and lax.axis_size(NARROW) == 8:
        own = jnp.concatenate(
            [params.reshape(ROWS, LANES), smalls.reshape(SMALL_ROWS, LANES), jnp.zeros((BLOCK - ROWS - SMALL_ROWS, LANES), F32)]
        ).astype(BF16)[None]
        z1, z2, z3 = (swap(own, NARROW, m) for m in (2, 4, 6))
        a, b = jnp.concatenate([own, z1]), jnp.concatenate([z2, z3])
        near = jnp.concatenate([a, b])
        near_core = swap(near, NARROW, 1)
        ax, by = swap(a, WIDE, 1), swap(b, WIDE, 2)
        side = jnp.concatenate([ax, by])
        side_core = swap(side, NARROW, 1)
        far_a = swap(jnp.concatenate([a, ax]), WIDE, 2)
        far_b = swap(jnp.concatenate([b, by]), WIDE, 1)
        far_a_core, far_b_core = swap(far_a, NARROW, 1), swap(far_b, NARROW, 1)
        near_marks = [0, 2, 4, 6]
        side_marks = [8, 10, 20, 22]
        a_marks = [16, 18, 24, 26]
        b_marks = [12, 14, 28, 30]
        plain = [(near, near_marks), (side, side_marks), (far_a, a_marks), (far_b, b_marks)]
        core = [(near_core, near_marks), (side_core, side_marks), (far_a_core, a_marks), (far_b_core, b_marks)]
        core = [(array, [m + 1 for m in marks]) for array, marks in core]
        both = plain + core
        return [array for array, _ in both], [marks for _, marks in both], True
    whole = lax.all_gather(params.astype(BF16), AXES, axis=0, tiled=True).reshape(BLOCKS, ROWS, LANES)
    little = lax.all_gather(smalls.astype(BF16), AXES, axis=0, tiled=True).reshape(BLOCKS, SMALL_ROWS, LANES)
    pad = jnp.zeros((BLOCKS, BLOCK - ROWS - SMALL_ROWS, LANES), BF16)
    return [jnp.concatenate([whole, little, pad], axis=1)], [list(range(BLOCKS))], False


def scatter_sums(grads, relative):
    if relative:

        def join(kept, received):
            return (kept.astype(F32) + received.astype(F32)).astype(BF16)

        pairs = grads.reshape(BLOCKS // 2, 2, BLOCK, LANES)
        part = join(pairs[:, 0], swap(pairs[:, 1], NARROW, 1)).reshape(2, 2, 4, BLOCK, LANES)
        a, b = part[:, :, :2], part[:, :, 2:]
        a1, b1 = join(a[0], swap(a[1], WIDE, 2)), join(b[:, 0], swap(b[:, 1], WIDE, 1))
        a2, b2 = join(a1[0], swap(a1[1], WIDE, 1)), join(b1[0], swap(b1[1], WIDE, 2))
        own = a2[0].astype(F32)
        for value, mask in ((a2[1], 2), (b2[0], 4), (b2[1], 6)):
            own = own + swap(value, NARROW, mask).astype(F32)
        return own[:ROWS].reshape(-1), own[ROWS : ROWS + SMALL_ROWS].reshape(-1)
    large = grads[:, :ROWS].reshape(-1).astype(F32)
    little = grads[:, ROWS : ROWS + SMALL_ROWS].reshape(-1).astype(F32)
    return (
        lax.psum_scatter(large, AXES, scatter_dimension=0, tiled=True),
        lax.psum_scatter(little, AXES, scatter_dimension=0, tiled=True),
    )


def adamw(weight, moment, second, grad, rate):
    moment_new = 0.5 * moment + 0.5 * grad
    second_new = 0.99 * second + 0.01 * grad * grad
    direction = moment_new / (1.0 - 0.5**STEP) / (jnp.sqrt(second_new / (1.0 - 0.99**STEP)) + 1e-08)
    return (weight - rate * (direction + 0.01 * weight), moment_new, second_new)


def body(
    params,
    first_moment,
    second_moment,
    smalls,
    small_first,
    small_second,
    images,
    noise,
    sigma,
    freq,
    counts,
    partner,
):
    slots = images.shape[0]
    pieces, marks, relative = gather_all(params, smalls)
    index = lax.axis_index(WIDE) * lax.axis_size(NARROW) + lax.axis_index(NARROW)
    me = (index if relative else jnp.zeros_like(index)).astype(jnp.int32)[None]

    ints = jnp.concatenate([counts, partner[0]]).astype(jnp.int32)
    across = lax.axis_size(WIDE) // 2
    other_ints = swap(ints, WIDE, across)
    total = sum_everywhere(counts.astype(F32))

    noisy = (images + sigma[:, None] * noise).reshape(slots, IMG, IMG, CHAN)
    edged = jnp.pad(noisy.astype(BF16), ((0, 0), (1, 1), (1, 1), (0, 0)))
    xcol = jnp.concatenate([edged[:, dy : dy + IMG, dx : dx + IMG] for dy, dx in TAPS], axis=-1)
    xcol = to_order(jnp.pad(xcol.reshape(slots, PIX, 9 * CHAN), ((0, 0), (0, 0), (0, 32 - 9 * CHAN))))
    shrink = fir_matrix()
    in_order = to_order(noisy.reshape(slots, PIX, CHAN))
    tiny = jnp.einsum("hp,bpc->bhc", jnp.asarray(shrink), in_order, precision=lax.Precision.HIGHEST)
    tiny = jnp.pad(tiny.astype(BF16), ((0, 0), (0, 0), (0, 16 - CHAN)))
    phase = jnp.log(sigma)[:, None] * freq[None, :] * (2.0 * math.pi)
    feats = jnp.concatenate([jnp.sin(phase), jnp.cos(phase)], axis=-1)
    feats = jnp.pad(feats.astype(BF16), ((0, 8 - slots), (0, 0)))
    noise_rows = to_order(noise.reshape(slots, PIX, CHAN)).transpose(0, 2, 1)
    noise_rows = jnp.pad(noise_rows, ((0, 0), (0, 8 - CHAN), (0, 0)))
    data = SimpleNamespace(
        xcol=xcol,
        tiny=tiny,
        feats=feats,
        noise=noise_rows,
        shrink=jnp.asarray(shrink, BF16),
        grow=jnp.asarray(4.0 * shrink.T, BF16),
    )
    kept = run_forward(me, pieces, marks, data)
    other = swap(kept.err.astype(BF16), WIDE, across)
    done = run_backward(me, total, ints, other_ints, other, kept, data)
    grad_params, grad_smalls = scatter_sums(done.grads, relative)
    squares = jnp.sum(grad_params * grad_params) + jnp.sum(grad_smalls * grad_smalls)
    both = sum_everywhere(jnp.stack([squares, jnp.sum(done.loss)]))
    loss, grad_norm = both[1], jnp.sqrt(both[0])
    factor = jnp.minimum(1.0, 0.01 / (grad_norm + 1e-06))
    small_grad = factor * grad_smalls
    new_params, new_first, new_second = adamw(
        params, first_moment, second_moment, factor * grad_params, 0.15
    )
    new_smalls, new_small_first, new_small_second = adamw(
        smalls, small_first, small_second, small_grad, 0.2
    )
    return (
        loss,
        grad_norm,
        new_params,
        new_first,
        new_second,
        new_smalls,
        new_small_first,
        new_small_second,
        small_grad,
    )


def solution(mesh):
    flat, rows = P(AXES), P(AXES, None)
    return jax.shard_map(
        body,
        mesh=mesh,
        in_specs=(flat, flat, flat, flat, flat, flat, rows, rows, flat, P(), flat, rows),
        out_specs=(P(), P(), flat, flat, flat, flat, flat, flat, flat),
        check_vma=False,
    )
```

```python
import functools
import math
from types import SimpleNamespace

import jax
import jax.numpy as jnp
import numpy as np
from jax import lax
from jax.experimental import pallas as pl
from jax.experimental.pallas import tpu as pltpu
from jax.sharding import PartitionSpec as P

NF = 128
MID = 256
TEMB = 512
NFOUR = 128
IMG = 32
GROUPS = 32
CHAN = 3
STEP = 7
PIX = IMG * IMG
HALF = PIX // 4
INV_ROOT = 0.7071067811865476
WIDE, NARROW = AXES = ("wide", "narrow")
F32 = jnp.float32
BF16 = jnp.bfloat16

LANES = 128
BLOCKS = 32
ROWS = 552
SMALL_ROWS = 2
BLOCK = 560


def mat_layout():
    return dict(
        temb_one=(2 * NFOUR, TEMB),
        temb_two=(TEMB, TEMB),
        conv_in=(9 * CHAN, NF),
        pyramid=(CHAN, MID),
        down_one=(9 * NF, MID),
        down_time=(TEMB, MID),
        down_two=(9 * MID, MID),
        down_skip=(NF, MID),
        attn_qkv=(MID, 3 * MID),
        attn_out=(MID, MID),
        up_one=(9 * MID, NF),
        up_time=(TEMB, NF),
        up_two=(9 * NF, NF),
        up_skip=(MID, NF),
        conv_out=(9 * 2 * NF, CHAN),
    )


def small_layout():
    return dict(
        temb_one_b=TEMB,
        temb_two_b=TEMB,
        conv_in_b=NF,
        pyramid_b=MID,
        down_gain_a=NF,
        down_bias_a=NF,
        down_one_b=MID,
        down_time_b=MID,
        down_gain_b=MID,
        down_bias_b=MID,
        down_two_b=MID,
        down_skip_b=MID,
        attn_gain=MID,
        attn_bias=MID,
        query_b=MID,
        value_b=MID,
        attn_out_b=MID,
        up_gain_a=MID,
        up_bias_a=MID,
        up_one_b=NF,
        up_time_b=NF,
        up_gain_b=NF,
        up_bias_b=NF,
        up_two_b=NF,
        up_skip_b=NF,
        final_gain=2 * NF,
        final_bias=2 * NF,
        conv_out_b=CHAN,
    )


def offsets():
    mats, smalls, used = {}, {}, 0
    for label, shape in mat_layout().items():
        mats[label] = (used // LANES,) + shape
        used += math.prod(shape)
    used = 0
    for label, length in small_layout().items():
        smalls[label] = (used // LANES, length)
        used += length
    return SimpleNamespace(**mats), SimpleNamespace(**smalls)


MATS, SMALLS = offsets()
WEIGHTS = list(mat_layout())
WEIGHT_SHAPES = mat_layout() | dict(conv_in=(LANES, NF), pyramid=(8, MID), conv_out=(LANES, 2 * NF))
RING = 8
TAPS = [(dy, dx) for dy in range(3) for dx in range(3)]


def pixel_order(side):
    across, down = side // 8, side // 2
    order = np.empty((across, down, 2, 8), np.int32)
    for xl in range(across):
        for yl in range(down):
            for yh in range(2):
                for xh in range(8):
                    order[xl, yl, yh, xh] = (yh * down + yl) * side + xh * across + xl
    return order.reshape(-1)


def fir_matrix():
    rows = np.arange(IMG // 2)[:, None]
    cols = np.arange(IMG)[None, :]
    offset = cols - 2 * rows + 1
    taps = np.where((offset == 0) | (offset == 3), 1.0, 0.0) + np.where(
        (offset == 1) | (offset == 2), 3.0, 0.0
    )
    both = np.kron(taps / 8.0, taps / 8.0)
    return both[pixel_order(IMG // 2)][:, pixel_order(IMG)].astype(np.float32)


def dot(a, b):
    return lax.dot_general(a, b, (((1,), (0,)), ((), ())), preferred_element_type=F32)


def dot_nt(a, b):
    return lax.dot_general(a, b, (((1,), (1,)), ((), ())), preferred_element_type=F32)


def dot_tn(a, b):
    return lax.dot_general(a, b, (((0,), (0,)), ((), ())), preferred_element_type=F32)


def two(value):
    high = value.astype(BF16)
    return high, (value - high.astype(F32)).astype(BF16)


def sigmoid(value):
    return 1.0 / (1.0 + jnp.exp(-value))


def rowsum(value):
    return jnp.sum(value, axis=0, keepdims=True)


def group_sums(rows, width):
    chans = rows[0].shape[1]
    at = lax.broadcasted_iota(jnp.int32, (16, chans), 0)
    stack = jnp.zeros((16, chans), F32)
    for n, row in enumerate(rows):
        rest = row
        for part in range(3):
            piece = rest.astype(BF16).astype(F32)
            stack = jnp.where(at == 3 * n + part, piece, stack)
            rest = rest - piece
    one = lax.broadcasted_iota(jnp.int32, (chans, chans), 0) // width
    other = lax.broadcasted_iota(jnp.int32, (chans, chans), 1) // width
    same = jnp.where(one == other, 1.0, 0.0).astype(BF16)
    sums = dot(stack.astype(BF16), same)
    return [sums[3 * n : 3 * n + 1] + sums[3 * n + 1 : 3 * n + 2] + sums[3 * n + 2 : 3 * n + 3] for n in range(len(rows))]


def norm_stats(value, width):
    count = float(value.shape[0] * width)
    center = group_sums([rowsum(value)], width)[0] / count
    shifted = value - center
    spread = group_sums([rowsum(shifted * shifted)], width)[0] / count
    return center, lax.rsqrt(spread + 1e-06)


def norm_back(grad, normed, gain, scale, width):
    count = float(grad.shape[0] * width)
    dbias = rowsum(grad)
    dgain = rowsum(grad * normed)
    first, second = group_sums([dbias * gain, dgain * gain], width)
    back = scale * (grad * gain - first / count - normed * (second / count))
    return back, dgain, dbias


def swish_back(pre):
    gate = sigmoid(pre)
    return gate * (1.0 + pre * (1.0 - gate))


def small(ref, label):
    at, length = label
    rows = max(1, length // LANES)
    return jnp.concatenate(
        [ref[(at + i) // 2, (at + i) % 2 : (at + i) % 2 + 1, :] for i in range(rows)], axis=1
    ) if rows > 1 else ref[at // 2, at % 2 : at % 2 + 1, :]


def add_small(ref, label, value):
    at, _ = label
    for i in range(value.shape[1] // LANES):
        j = at + i
        ref[j // 2, j % 2 : j % 2 + 1, :] += value[:, i * LANES : (i + 1) * LANES]


def fill_halo(ref, b, across, down):
    chans = ref.shape[-1]
    zero = jnp.zeros((across, 8, chans), F32)
    last = ref[b, 1 : across + 1, down].astype(F32)
    ref[b, 1 : across + 1, 0] = jnp.concatenate([zero, last[:, 0:8]], axis=1).astype(BF16)
    first = ref[b, 1 : across + 1, 1].astype(F32)
    ref[b, 1 : across + 1, down + 1] = jnp.concatenate([first[:, 8:16], zero], axis=1).astype(BF16)
    tiles = (down + 2) * 2
    at = lax.broadcasted_iota(jnp.int32, (tiles, 8, chans), 1)
    side = ref[b, across].astype(F32).reshape(tiles, 8, chans)
    side = jnp.where(at == 0, 0.0, pltpu.roll(side, 1, axis=1))
    ref[b, 0] = side.reshape(down + 2, 16, chans).astype(BF16)
    side = ref[b, 1].astype(F32).reshape(tiles, 8, chans)
    side = jnp.where(at == 7, 0.0, pltpu.roll(side, 7, axis=1))
    ref[b, across + 1] = side.reshape(down + 2, 16, chans).astype(BF16)


def set_inner(ref, b, across, down, value):
    chans = value.shape[1]
    ref[b, 1 : across + 1, 1 : down + 1] = value.astype(BF16).reshape(across, down, 16, chans)
    fill_halo(ref, b, across, down)


def taps_of(ref, b, xl, count, down, flip):
    chans = ref.shape[-1]
    parts = []
    for dy, dx in TAPS:
        y, x = (2 - dy, 2 - dx) if flip else (dy, dx)
        parts.append(ref[b, xl + x : xl + x + count, y : y + down].reshape(count * down * 16, chans))
    return jnp.concatenate(parts, axis=1)


def tap_columns(ref, chans):
    return jnp.concatenate([ref[t * chans : (t + 1) * chans, :] for t in range(9)], axis=1)


def picks(o):
    row = lax.broadcasted_iota(jnp.int32, (6 * LANES, 2 * NF), 0)
    col = lax.broadcasted_iota(jnp.int32, (6 * LANES, 2 * NF), 1)
    return jnp.where(row == CHAN * col + o, 1.0, 0.0).astype(BF16)


SAVED = dict(
    xin=((PIX, LANES), BF16),
    tiny=((HALF, 8), BF16),
    h0=((PIX, NF), F32),
    ed1=((4, 10, 16, NF), BF16),
    sk0=((HALF, NF), BF16),
    a1=((HALF, MID), F32),
    ed2=((4, 10, 16, MID), BF16),
    h1=((HALF, MID), F32),
    g=((HALF, MID), BF16),
    qkv=((HALF, 3 * MID), BF16),
    prob=((HALF, HALF), BF16),
    mixed=((HALF, MID), BF16),
    h2=((HALF, MID), F32),
    eu1=((6, 18, 16, MID), BF16),
    sku=((PIX, MID), BF16),
    b1=((PIX, NF), F32),
    eu2=((6, 18, 16, NF), BF16),
    h3=((PIX, NF), F32),
    final=((PIX, 2 * NF), BF16),
    stats=((16, MID), F32),
)
EARLY = list(dict(sm=0, xin=0, tiny=0, h0=0, ed1=0, sk0=0, a1=0, ed2=0, h1=0, g=0, qkv=0, prob=0, mixed=0, h2=0))
TIME_SAVED = dict(
    t1=((8, TEMB), F32),
    s1=((8, TEMB), BF16),
    t2=((8, TEMB), F32),
    tact=((8, TEMB), BF16),
)


def in_step(parts):
    for _ in zip(*parts, strict=True):
        pass


def forward_kernel(piece_marks, slots, names, sent, *refs):
    r_pieces, refs = refs[: len(piece_marks)], refs[len(piece_marks) :]
    r = SimpleNamespace(**dict(zip(names, refs)))
    me = r.me[0]
    copies = []
    early = [name for name in sent if name[:2] == "w_" or name in TIME_SAVED or name in EARLY]

    def send(names):
        for name in names:
            source, target = getattr(r, name), getattr(r, "out_" + name)
            copies.append(pltpu.make_async_copy(source, target, r.sems.at[len(copies)]))
            copies[-1].start()

    stage, sm = r.stage, r.sm
    for n, marks in enumerate(piece_marks):
        for i, mark in enumerate(marks):
            home = jnp.bitwise_xor(me, mark)
            block = r_pieces[n][i].astype(F32)
            stage[pl.ds(pl.multiple_of(home * ROWS, 8), ROWS), :] = block[:ROWS]
            sm[home] = block[ROWS:]
    for label in WEIGHTS:
        at, depth, width = getattr(MATS, label)
        out = getattr(r, "w_" + label)
        if width == CHAN:
            flat = jnp.concatenate([stage[pl.ds(at + i, 9, stride=6), :] for i in range(6)], axis=1).astype(BF16)
            out[...] = jnp.zeros(out.shape, BF16)
            pad = jnp.zeros((7, 2 * NF), F32)
            for o in range(CHAN):
                out[16 * o : 16 * o + 16, :] = jnp.concatenate([dot(flat, picks(o)), pad], axis=0).astype(BF16)
            continue
        if depth == 9 * CHAN:
            out[...] = jnp.zeros(out.shape, BF16)
            pad = jnp.zeros((7, NF), F32)
            for c in range(CHAN):
                part = stage[pl.ds(at + c, 9, stride=CHAN), :]
                out[16 * c : 16 * c + 16, :] = jnp.concatenate([part, pad], axis=0).astype(BF16)
            continue
        pad = out.shape[0] - depth
        for j in range(width // LANES):
            part = stage[pl.ds(at + j, depth, stride=width // LANES), :] if width > LANES else stage[pl.ds(at, depth), :]
            if pad:
                part = jnp.concatenate([part, jnp.zeros((pad, LANES), F32)], axis=0)
            out[:, j * LANES : (j + 1) * LANES] = part.astype(BF16)

    t1 = dot(r.feats[...], r.w_temb_one[...]) + small(sm, SMALLS.temb_one_b)
    r.t1[...] = t1
    s1 = (t1 * sigmoid(t1)).astype(BF16)
    r.s1[...] = s1
    t2 = dot(s1, r.w_temb_two[...]) + small(sm, SMALLS.temb_two_b)
    r.t2[...] = t2
    tact = (t2 * sigmoid(t2)).astype(BF16)
    r.tact[...] = tact
    r.pd[...] = dot(tact, r.w_down_time[...]) + (small(sm, SMALLS.down_time_b) + small(sm, SMALLS.down_one_b))
    r.pu[...] = dot(tact, r.w_up_time[...]) + (small(sm, SMALLS.up_time_b) + small(sm, SMALLS.up_one_b))

    def image(b):
        stats = r.stats

        def normed(value, width, gain, bias, at):
            center, scale = norm_stats(value, width)
            chans = value.shape[1]
            stats[b, 2 * at : 2 * at + 1, :chans] = center
            stats[b, 2 * at + 1 : 2 * at + 2, :chans] = scale
            return (value - center) * (scale * gain) + bias

        noisy = r.images[b] + r.sigma[b] * r.noise[b]
        high, rest = two(noisy)
        r.tiny[b] = (dot_nt(r.shrink[...], high) + dot_nt(r.shrink[...], rest)).astype(BF16)
        field = r.field.at[b]
        set_field(field, dot_tn(high, colour_fan()))
        r.xin[b] = tap_lanes(field, False).astype(BF16)
        yield
        h0 = dot(r.xin[b], r.w_conv_in[...]) + small(sm, SMALLS.conv_in_b)
        r.h0[b] = h0
        yield
        y = normed(h0, 4, small(sm, SMALLS.down_gain_a), small(sm, SMALLS.down_bias_a), 0)
        y = y * sigmoid(y)
        yield
        down = dot(r.shrink[...], jnp.concatenate([*two(y), *two(h0)], axis=1))
        set_inner(r.ed1, b, 2, 8, down[:, :NF] + down[:, NF : 2 * NF])
        sk0 = (down[:, 2 * NF : 3 * NF] + down[:, 3 * NF :]).astype(BF16)
        r.sk0[b] = sk0
        yield
        a1 = dot(taps_of(r.ed1, b, 0, 2, 8, False), r.w_down_one[...]) + r.pd[pl.ds(b, 1), :]
        r.a1[b] = a1
        yield
        y = normed(a1, 8, small(sm, SMALLS.down_gain_b), small(sm, SMALLS.down_bias_b), 1)
        set_inner(r.ed2, b, 2, 8, y * sigmoid(y))
        yield
        a2 = dot(taps_of(r.ed2, b, 0, 2, 8, False), r.w_down_two[...]) + dot(sk0, r.w_down_skip[...])
        a2 = (a2 + (small(sm, SMALLS.down_two_b) + small(sm, SMALLS.down_skip_b))) * INV_ROOT
        h1 = (a2 + dot(r.tiny[b], r.w_pyramid[...]) + small(sm, SMALLS.pyramid_b)) * INV_ROOT
        r.h1[b] = h1
        yield
        g = normed(h1, 8, small(sm, SMALLS.attn_gain), small(sm, SMALLS.attn_bias), 2).astype(BF16)
        r.g[b] = g
        yield
        proj = dot(g, r.w_attn_qkv[...])
        q = (proj[:, :MID] + small(sm, SMALLS.query_b)).astype(BF16)
        k = proj[:, MID : 2 * MID].astype(BF16)
        v = (proj[:, 2 * MID :] + small(sm, SMALLS.value_b)).astype(BF16)
        r.qkv[b] = jnp.concatenate([q, k, v], axis=1)
        yield
        scores = dot_nt(q, k) * (MID**-0.5)
        yield
        weight = jnp.exp(scores - jnp.max(scores, axis=1, keepdims=True))
        prob = (weight / jnp.sum(weight, axis=1, keepdims=True)).astype(BF16)
        r.prob[b] = prob
        yield
        mixed = dot(prob, v).astype(BF16)
        r.mixed[b] = mixed
        yield
        h2 = (h1 + dot(mixed, r.w_attn_out[...]) + small(sm, SMALLS.attn_out_b)) * INV_ROOT
        r.h2[b] = h2
        yield
        if b == 0:
            send(early)
        y = normed(h2, 8, small(sm, SMALLS.up_gain_a), small(sm, SMALLS.up_bias_a), 3)
        y = y * sigmoid(y)
        coarse = jnp.concatenate([*two(y), *two(h2)], axis=1)
        yield
        for xl in range(4):
            fine = dot(r.grow[xl * 256 : (xl + 1) * 256, :], coarse)
            part = (fine[:, :MID] + fine[:, MID : 2 * MID]).astype(BF16)
            r.eu1[b, xl + 1, 1:17] = part.reshape(16, 16, MID)
            r.sku[b, xl * 256 : (xl + 1) * 256, :] = (fine[:, 2 * MID : 3 * MID] + fine[:, 3 * MID :]).astype(BF16)
        fill_halo(r.eu1, b, 4, 16)
        yield
        for xl in range(4):
            r.b1[b, xl * 256 : (xl + 1) * 256, :] = (
                dot(taps_of(r.eu1, b, xl, 1, 16, False), r.w_up_one[...]) + r.pu[pl.ds(b, 1), :]
            )
        yield
        y = normed(r.b1[b], 4, small(sm, SMALLS.up_gain_b), small(sm, SMALLS.up_bias_b), 4)
        set_inner(r.eu2, b, 4, 16, y * sigmoid(y))
        yield
        bias = small(sm, SMALLS.up_two_b) + small(sm, SMALLS.up_skip_b)
        for xl in range(4):
            part = slice(xl * 256, (xl + 1) * 256)
            up = dot(taps_of(r.eu2, b, xl, 1, 16, False), r.w_up_two[...])
            r.h3[b, part, :] = (up + dot(r.sku[b, part, :], r.w_up_skip[...]) + bias) * INV_ROOT
        yield
        gain, bias = small(sm, SMALLS.final_gain), small(sm, SMALLS.final_bias)
        y = normed(r.h3[b], 8, gain[:, :NF], bias[:, :NF], 5)
        r.final[b, :, :NF] = (y * sigmoid(y)).astype(BF16)
        yield
        y = normed(r.h0[b], 8, gain[:, NF:], bias[:, NF:], 6)
        r.final[b, :, NF:] = (y * sigmoid(y)).astype(BF16)
        yield
        wide = dot_nt(r.final[b], r.w_conv_out[...])
        field = r.field.at[b]
        set_field(field, wide)
        total = tap_lanes(field, False)
        high, rest = two(total)
        fold = colour_fold()
        out = dot_nt(fold, high) + dot_nt(fold, rest)
        bias = r.out_bias[...]
        err = out + bias + r.noise[b]
        r.err[b] = err
        r.err16[b] = err.astype(BF16)

    prepare_out_bias(r, sm)
    notes = r.sm[jnp.bitwise_xor(me, BLOCKS // 2)]
    row = lax.broadcasted_iota(jnp.int32, (8, LANES), 0)
    lane = lax.broadcasted_iota(jnp.int32, (8, LANES), 1)

    def number(value, at):
        return jnp.sum(jnp.where((row == SMALL_ROWS) & (lane == at), value, 0.0))

    r.total[0] = number(jnp.sum(sm[...], axis=0), 0)
    for n in range(slots + 1):
        r.other_ints[n] = number(notes, n + 1).astype(jnp.int32)
    in_step([image(b) for b in range(slots)])
    send(name for name in sent if name not in early)
    for copy in copies:
        copy.wait()


def prepare_out_bias(r, sm):
    bias = small(sm, SMALLS.conv_out_b)
    row = lax.broadcasted_iota(jnp.int32, (8, LANES), 0)
    lane = lax.broadcasted_iota(jnp.int32, (8, LANES), 1)
    own = jnp.sum(jnp.where((lane == row) & (row < CHAN), bias, 0.0), axis=1, keepdims=True)
    r.out_bias[...] = jnp.broadcast_to(own, (8, PIX))


def colour_fold():
    row = lax.broadcasted_iota(jnp.int32, (16, LANES), 0)
    lane = lax.broadcasted_iota(jnp.int32, (16, LANES), 1)
    return jnp.where((lane // 16 == row) & (lane % 16 < 9) & (row < CHAN), 1.0, 0.0).astype(BF16)[:8]


def set_field(field, value):
    field[1:5, 1:17] = value.reshape(4, 16, 16, LANES)
    zero = jnp.zeros((4, 8, LANES), F32)
    field[1:5, 0] = jnp.concatenate([zero, field[1:5, 16, 0:8]], axis=1)
    field[1:5, 17] = jnp.concatenate([field[1:5, 1, 8:16], zero], axis=1)
    at = lax.broadcasted_iota(jnp.int32, (36, 8, LANES), 1)
    side = pltpu.roll(field[4].reshape(36, 8, LANES), 1, axis=1)
    field[0] = jnp.where(at == 0, 0.0, side).reshape(18, 16, LANES)
    side = pltpu.roll(field[1].reshape(36, 8, LANES), 7, axis=1)
    field[5] = jnp.where(at == 7, 0.0, side).reshape(18, 16, LANES)


def backward_kernel(slots, names, fetched, *refs):
    r = SimpleNamespace(**dict(zip(names, refs)))
    copies = []
    for n, name in enumerate(fetched):
        copies.append(pltpu.make_async_copy(getattr(r, "in_" + name), getattr(r, name), r.sems.at[n]))
        copies[-1].start()

    def arrive(name):
        while len(copies) > len(fetched) - 1 - fetched.index(name):
            copies.pop(0).wait()

    me = r.me[0]
    sm, stage, gsm = r.sm, r.stage, r.gsm
    stats = r.stats
    total = r.total[0]
    gsm[...] = jnp.zeros(gsm.shape, F32)
    r.dpd[...] = jnp.zeros(r.dpd.shape, F32)
    r.dpu[...] = jnp.zeros(r.dpu.shape, F32)
    r.dout_sum[...] = jnp.zeros(r.dout_sum.shape, F32)
    r.loss[...] = jnp.zeros(r.loss.shape, F32)
    counts, pairs = r.ints[0], r.ints
    other_counts = r.other_ints[0]

    def put(label, value, first=0):
        at, _, width = label
        step = width // LANES
        for j in range(step):
            part = value[:, j * LANES : (j + 1) * LANES]
            if step == 1:
                stage[pl.ds(at + first, value.shape[0]), :] = part
            else:
                stage[pl.ds(at + first * step + j, value.shape[0], stride=step), :] = part

    def image(b):
        def stat(at, chans):
            return stats[b, 2 * at : 2 * at + 1, :chans], stats[b, 2 * at + 1 : 2 * at + 2, :chans]

        def renorm(value, at, gain, bias):
            center, scale = stat(at, value.shape[1])
            normed = (value - center) * scale
            return normed, normed * gain + bias, scale

        err = r.err[b]
        mine = r.other[pairs[1 + b]].astype(F32)
        gap = err - mine
        live = jnp.where(b < counts, 1.0, 0.0)
        scale = 1.0 / (total * (CHAN * PIX))
        r.loss[...] += (live * scale) * (0.5 * err * err + 0.25 * gap * gap)
        grad = (live * scale) * (err + 0.5 * gap)
        for s in range(slots):
            theirs = r.other[s].astype(F32)
            on = jnp.where((r.other_ints[1 + s] == b) & (s < other_counts), 0.5 * scale, 0.0)
            grad += on * (err - theirs)
        yield
        if b == 0:
            arrive(FETCH_ORDER[6])
        r.dout_sum[...] += grad
        field = r.field.at[b]
        set_field(field, dot_tn(grad.astype(BF16), colour_fan()))
        cols = tap_lanes(field, True).astype(BF16)
        r.cols[b] = cols
        yield
        gain, bias = small(sm, SMALLS.final_gain), small(sm, SMALLS.final_bias)
        back = dot(cols, r.w_conv_out[...])
        yield
        n3, y3, scale3 = renorm(r.h3[b], 5, gain[:, :NF], bias[:, :NF])
        dh3, dgain, dbias = norm_back(back[:, :NF] * swish_back(y3), n3, gain[:, :NF], scale3, 8)
        n0, y0, scale0 = renorm(r.h0[b], 6, gain[:, NF:], bias[:, NF:])
        dh0, dgain0, dbias0 = norm_back(back[:, NF:] * swish_back(y0), n0, gain[:, NF:], scale0, 8)
        add_small(gsm, SMALLS.final_gain, jnp.concatenate([dgain, dgain0], axis=1))
        add_small(gsm, SMALLS.final_bias, jnp.concatenate([dbias, dbias0], axis=1))
        r.dh0[b] = dh0
        yield
        dh3 = dh3 * INV_ROOT
        add_small(gsm, SMALLS.up_two_b, rowsum(dh3))
        set_inner(r.gu2, b, 4, 16, dh3)
        yield
        turned = tap_columns(r.w_up_two, NF)
        for xl in range(4):
            r.wide[b, xl * 256 : (xl + 1) * 256, :] = dot_nt(taps_of(r.gu2, b, xl, 1, 16, True), turned)
        yield
        gain, bias = small(sm, SMALLS.up_gain_b), small(sm, SMALLS.up_bias_b)
        n, y, scale1 = renorm(r.b1[b], 4, gain, bias)
        db1, dgain, dbias = norm_back(r.wide[b] * swish_back(y), n, gain, scale1, 4)
        add_small(gsm, SMALLS.up_gain_b, dgain)
        add_small(gsm, SMALLS.up_bias_b, dbias)
        r.dpu[pl.ds(b, 1), :] = rowsum(db1)
        set_inner(r.gu1, b, 4, 16, db1)
        yield
        turned = tap_columns(r.w_up_one, MID)
        half = jnp.zeros((HALF, 2 * MID), F32)
        for xl in range(4):
            branch = dot_nt(taps_of(r.gu1, b, xl, 1, 16, True), turned)
            skip = dot_nt(r.gu2[b, xl + 1, 1:17].reshape(256, NF), r.w_up_skip[...])
            both = jnp.concatenate([branch.astype(BF16), skip.astype(BF16)], axis=1)
            half += dot(r.shrink[:, xl * 256 : (xl + 1) * 256], both)
        half = half * 4.0
        yield
        if b == 0:
            arrive(FETCH_ORDER[-1])
            arrive(fetched[-1])
        gain, bias = small(sm, SMALLS.up_gain_a), small(sm, SMALLS.up_bias_a)
        n, y, scale2 = renorm(r.h2[b], 3, gain, bias)
        dh2, dgain, dbias = norm_back(half[:, :MID] * swish_back(y), n, gain, scale2, 8)
        add_small(gsm, SMALLS.up_gain_a, dgain)
        add_small(gsm, SMALLS.up_bias_a, dbias)
        dh2 = (dh2 + half[:, MID:]) * INV_ROOT
        add_small(gsm, SMALLS.attn_out_b, rowsum(dh2))
        datt = dh2.astype(BF16)
        r.datt[b] = datt
        yield
        dmixed = dot_nt(datt, r.w_attn_out[...]).astype(BF16)
        q, k, v = r.qkv[b, :, :MID], r.qkv[b, :, MID : 2 * MID], r.qkv[b, :, 2 * MID :]
        prob = r.prob[b]
        dprob = dot_nt(dmixed, v)
        yield
        dv = dot_tn(prob, dmixed)
        yield
        wide = prob.astype(F32)
        dscore = wide * (dprob - jnp.sum(wide * dprob, axis=1, keepdims=True))
        dscore = (dscore * (MID**-0.5)).astype(BF16)
        yield
        dq = dot(dscore, k)
        dk = dot_tn(dscore, q)
        add_small(gsm, SMALLS.query_b, rowsum(dq))
        add_small(gsm, SMALLS.value_b, rowsum(dv))
        dqkv = jnp.concatenate([dq, dk, dv], axis=1).astype(BF16)
        r.dqkv[b] = dqkv
        yield
        dg = dot_nt(dqkv, r.w_attn_qkv[...])
        yield
        gain, bias = small(sm, SMALLS.attn_gain), small(sm, SMALLS.attn_bias)
        n, _, scale2 = renorm(r.h1[b], 2, gain, bias)
        dh1, dgain, dbias = norm_back(dg, n, gain, scale2, 8)
        add_small(gsm, SMALLS.attn_gain, dgain)
        add_small(gsm, SMALLS.attn_bias, dbias)
        dh1 = (dh1 + dh2) * INV_ROOT
        r.dpyr[b] = dh1.astype(BF16)
        add_small(gsm, SMALLS.pyramid_b, rowsum(dh1))
        da2 = dh1 * INV_ROOT
        add_small(gsm, SMALLS.down_two_b, rowsum(da2))
        set_inner(r.gd2, b, 2, 8, da2)
        yield
        dsk0 = dot_nt(r.gd2[b, 1:3, 1:9].reshape(HALF, MID), r.w_down_skip[...])
        turned = tap_columns(r.w_down_two, MID)
        du = dot_nt(taps_of(r.gd2, b, 0, 2, 8, True), turned)
        yield
        gain, bias = small(sm, SMALLS.down_gain_b), small(sm, SMALLS.down_bias_b)
        n, y, scale2 = renorm(r.a1[b], 1, gain, bias)
        da1, dgain, dbias = norm_back(du * swish_back(y), n, gain, scale2, 8)
        add_small(gsm, SMALLS.down_gain_b, dgain)
        add_small(gsm, SMALLS.down_bias_b, dbias)
        r.dpd[pl.ds(b, 1), :] = rowsum(da1)
        set_inner(r.gd1, b, 2, 8, da1)
        yield
        turned = tap_columns(r.w_down_one, NF)
        dd0 = dot_nt(taps_of(r.gd1, b, 0, 2, 8, True), turned)
        both = jnp.concatenate([dd0, dsk0], axis=1).astype(BF16)
        fine = dot(r.grow[...], both) * 0.25
        yield
        gain, bias = small(sm, SMALLS.down_gain_a), small(sm, SMALLS.down_bias_a)
        n, y, scale1 = renorm(r.h0[b], 0, gain, bias)
        back0, dgain, dbias = norm_back(fine[:, :NF] * swish_back(y), n, gain, scale1, 4)
        add_small(gsm, SMALLS.down_gain_a, dgain)
        add_small(gsm, SMALLS.down_bias_a, dbias)
        dh0 = r.dh0[b] + back0 + fine[:, NF:]
        add_small(gsm, SMALLS.conv_in_b, rowsum(dh0))
        r.din[b] = dh0.astype(BF16)

    in_step([image(b) for b in range(slots)])

    whole = slots * PIX
    fewer = slots * HALF
    def conv_grad(label, acts, grads, across, down):
        chans, rows = acts.shape[-1], slots * across * down * 16
        left = acts[:, 1 : across + 1, 1 : down + 1].reshape(rows, chans)
        for dy in range(3):
            right = jnp.concatenate(
                [
                    grads[:, 2 - dx : 2 - dx + across, 2 - dy : 2 - dy + down].reshape(rows, grads.shape[-1])
                    for dx in range(3)
                ],
                axis=1,
            )
            back = dot_tn(left, right)
            for dx in range(3):
                put(label, back[:, dx * grads.shape[-1] : (dx + 1) * grads.shape[-1]], (3 * dy + dx) * chans)

    dpd, dpu = r.dpd[...], r.dpu[...]
    for label in (SMALLS.down_time_b, SMALLS.down_one_b):
        add_small(gsm, label, rowsum(dpd))
    for label in (SMALLS.up_time_b, SMALLS.up_one_b):
        add_small(gsm, label, rowsum(dpu))
    dpd16, dpu16 = dpd.astype(BF16), dpu.astype(BF16)
    put(MATS.down_time, dot_tn(r.tact[...], dpd16))
    put(MATS.up_time, dot_tn(r.tact[...], dpu16))
    dtact = dot_nt(dpd16, r.w_down_time[...]) + dot_nt(dpu16, r.w_up_time[...])
    dt2 = dtact * swish_back(r.t2[...])
    add_small(gsm, SMALLS.temb_two_b, rowsum(dt2))
    put(MATS.temb_two, dot_tn(r.s1[...], dt2.astype(BF16)))
    dt1 = dot_nt(dt2.astype(BF16), r.w_temb_two[...]) * swish_back(r.t1[...])
    add_small(gsm, SMALLS.temb_one_b, rowsum(dt1))
    put(MATS.temb_one, dot_tn(r.feats[...], dt1.astype(BF16)))
    for label, twin in ((SMALLS.up_skip_b, SMALLS.up_two_b), (SMALLS.down_skip_b, SMALLS.down_two_b)):
        value = small(gsm, twin)
        add_small(gsm, label, value)
    sums = jnp.sum(r.dout_sum[...], axis=1, keepdims=True)
    row = lax.broadcasted_iota(jnp.int32, (8, LANES), 0)
    lane = lax.broadcasted_iota(jnp.int32, (8, LANES), 1)
    add_small(gsm, SMALLS.conv_out_b, rowsum(jnp.where((row == lane) & (row < CHAN), sums, 0.0)))
    dout = dot_tn(r.cols[...].reshape(whole, LANES), r.final[...].reshape(whole, 2 * NF))
    flat = jnp.zeros((16, 6 * LANES), F32)
    for o in range(CHAN):
        flat += dot_nt(dout[16 * o : 16 * o + 16].astype(BF16), picks(o))
    at = MATS.conv_out[0]
    for i in range(6):
        for t in range(9):
            stage[at + 6 * t + i : at + 6 * t + i + 1, :] = flat[t : t + 1, i * LANES : (i + 1) * LANES]

    last = MATS.conv_out[0] + 54
    stage[last : BLOCKS * ROWS, :] = jnp.zeros((BLOCKS * ROWS - last, LANES), F32)
    put(MATS.up_skip, dot_tn(r.sku[...].reshape(whole, MID), r.gu2[:, 1:5, 1:17].reshape(whole, NF)))
    conv_grad(MATS.up_two, r.eu2, r.gu2, 4, 16)
    conv_grad(MATS.up_one, r.eu1, r.gu1, 4, 16)
    put(MATS.attn_out, dot_tn(r.mixed[...].reshape(fewer, MID), r.datt[...].reshape(fewer, MID)))
    put(MATS.attn_qkv, dot_tn(r.g[...].reshape(fewer, MID), r.dqkv[...].reshape(fewer, 3 * MID)))
    put(MATS.down_skip, dot_tn(r.sk0[...].reshape(fewer, NF), r.gd2[:, 1:3, 1:9].reshape(fewer, MID)))
    conv_grad(MATS.down_two, r.ed2, r.gd2, 2, 8)
    conv_grad(MATS.down_one, r.ed1, r.gd1, 2, 8)
    put(MATS.pyramid, dot_tn(r.tiny[...].reshape(fewer, 8), r.dpyr[...].reshape(fewer, MID))[:CHAN])
    back = dot_tn(r.xin[...].reshape(whole, LANES), r.din[...].reshape(whole, NF))
    for c in range(CHAN):
        stage[pl.ds(MATS.conv_in[0] + c, 9, stride=CHAN), :] = back[16 * c : 16 * c + 9]
    ring, sems = r.ring, r.ring_sems

    def sending(part, d, slot):
        return pltpu.make_async_copy(ring.at[slot], part.at[block_place(jnp.bitwise_xor(d, me))], sems.at[slot])

    def give(d, carry):
        slot = d % RING

        @pl.when(d >= RING)
        def _():
            sending(r.stay, d, slot).wait()

        block = jnp.concatenate([stage[pl.ds(pl.multiple_of(d * ROWS, 8), ROWS), :], gsm[d]], axis=0)
        ring[slot] = block.astype(BF16)
        goes = jnp.bitwise_xor(d, me) % 2 == 1

        @pl.when(goes)
        def _():
            sending(r.leave, d, slot).start()

        @pl.when(jnp.logical_not(goes))
        def _():
            sending(r.stay, d, slot).start()

        return carry

    lax.fori_loop(0, BLOCKS, give, 0)
    for d in range(BLOCKS - RING, BLOCKS):
        sending(r.stay, d, d % RING).wait()


def colour_fan():
    row = lax.broadcasted_iota(jnp.int32, (8, LANES), 0)
    lane = lax.broadcasted_iota(jnp.int32, (8, LANES), 1)
    return jnp.where(lane // 16 == row, 1.0, 0.0).astype(BF16)


def tap_lanes(field, flip):
    lane = lax.broadcasted_iota(jnp.int32, (PIX, LANES), 1) % 16
    total = jnp.zeros((PIX, LANES), F32)
    for t, (dy, dx) in enumerate(TAPS):
        y, x = (2 - dy, 2 - dx) if flip else (dy, dx)
        total = jnp.where(lane == t, field[x : x + 4, y : y + 16].reshape(PIX, LANES), total)
    return total


def block_place(mark):
    low, high, x, y = (mark // 2) % 2, (mark // 4) % 2, (mark // 8) % 2, mark // 16
    return high * 8 + (4 * y + 2 * x + high * 2 * (x - y)) + low


def vmem():
    return pl.BlockSpec(memory_space=pltpu.VMEM)


def anywhere():
    return pl.BlockSpec(memory_space=pl.ANY)


def smem():
    return pl.BlockSpec(memory_space=pltpu.SMEM)


LIMIT = 60 * 1024 * 1024


def run_forward(me, sigma, pieces, marks, data):
    slots = data.images.shape[0]
    ins = dict(me=me, sigma=sigma) | vars(data)
    outs = {"w_" + label: (WEIGHT_SHAPES[label], BF16) for label in WEIGHTS}
    outs |= dict(sm=((BLOCKS, 8, LANES), F32)) | TIME_SAVED
    outs |= {label: ((slots,) + shape, dtype) for label, (shape, dtype) in SAVED.items()}
    outs |= dict(err=((slots, 8, PIX), F32), err16=((slots, 8, PIX), BF16))
    numbers = dict(total=((1,), F32), other_ints=((slots + 1,), jnp.int32))
    scratch = dict(
        stage=((BLOCKS * ROWS, LANES), F32),
        pd=((8, MID), F32),
        pu=((8, NF), F32),
        out_bias=((8, PIX), F32),
        field=((slots, 6, 18, 16, LANES), F32),
    )
    names = list(ins) + ["out_" + label for label in outs] + list(numbers) + list(outs) + list(scratch) + ["sems"]
    results = pl.pallas_call(
        functools.partial(forward_kernel, marks, slots, names, list(outs)),
        out_shape=[jax.ShapeDtypeStruct(*v) for v in (outs | numbers).values()],
        in_specs=[vmem()] * len(pieces) + [smem()] * 2 + [vmem()] * (len(ins) - 2),
        out_specs=[anywhere()] * len(outs) + [smem()] * len(numbers),
        scratch_shapes=[pltpu.VMEM(*v) for v in (outs | scratch).values()] + [pltpu.SemaphoreType.DMA((len(outs),))],
        compiler_params=pltpu.CompilerParams(vmem_limit_bytes=LIMIT),
        name="forward",
    )(*pieces, *ins.values())
    return SimpleNamespace(**dict(zip(outs | numbers, results)))


FETCH_ORDER = list(
    dict(
        w_conv_out=0,
        h3=0,
        h0=0,
        w_up_two=0,
        b1=0,
        w_up_skip=0,
        w_up_one=0,
        h2=0,
        w_attn_out=0,
        qkv=0,
        prob=0,
        w_attn_qkv=0,
        h1=0,
        w_down_skip=0,
        w_down_two=0,
        a1=0,
        w_down_one=0,
        w_down_time=0,
        w_up_time=0,
        t2=0,
        s1=0,
        w_temb_two=0,
        t1=0,
        tact=0,
        final=0,
        sku=0,
        eu2=0,
        eu1=0,
        mixed=0,
        g=0,
        sk0=0,
        ed2=0,
        ed1=0,
        xin=0,
        tiny=0,
    )
)


def run_backward(me, ints, other, kept, data):
    slots = other.shape[0]
    ins = dict(me=me, total=kept.total, ints=ints, other_ints=kept.other_ints)
    scalars = len(ins)
    ins |= dict(other=other, err=kept.err, sm=kept.sm, stats=kept.stats)
    direct = len(ins)
    fetched = dict(shrink=data.shrink)
    fetched |= {name: getattr(kept, name) for name in FETCH_ORDER}
    fetched |= dict(grow=data.grow, feats=data.feats)
    ins |= {"in_" + name: value for name, value in fetched.items()}
    part = ((BLOCKS // 2, BLOCK, LANES), BF16)
    outs = dict(stay=part, leave=part, loss=((8, PIX), F32))
    scratch = {name: (value.shape, value.dtype) for name, value in fetched.items()}
    scratch |= dict(
        stage=((BLOCKS * ROWS, LANES), F32),
        gsm=((BLOCKS, 8, LANES), F32),
        ring=((RING, BLOCK, LANES), BF16),
        dpd=((8, MID), F32),
        dpu=((8, NF), F32),
        dout_sum=((8, PIX), F32),
        field=((slots, 6, 18, 16, LANES), F32),
        cols=((slots, PIX, LANES), BF16),
        gu2=((slots, 6, 18, 16, NF), BF16),
        gu1=((slots, 6, 18, 16, NF), BF16),
        gd2=((slots, 4, 10, 16, MID), BF16),
        gd1=((slots, 4, 10, 16, MID), BF16),
        wide=((slots, PIX, NF), F32),
        dh0=((slots, PIX, NF), F32),
        din=((slots, PIX, NF), BF16),
        datt=((slots, HALF, MID), BF16),
        dqkv=((slots, HALF, 3 * MID), BF16),
        dpyr=((slots, HALF, MID), BF16),
    )
    names = list(ins) + list(outs) + list(scratch) + ["sems", "ring_sems"]
    results = pl.pallas_call(
        functools.partial(backward_kernel, slots, names, list(fetched)),
        out_shape=[jax.ShapeDtypeStruct(*v) for v in outs.values()],
        in_specs=[smem()] * scalars + [vmem()] * (direct - scalars) + [anywhere()] * (len(ins) - direct),
        out_specs=[anywhere(), anywhere(), vmem()],
        scratch_shapes=[pltpu.VMEM(*v) for v in scratch.values()]
        + [pltpu.SemaphoreType.DMA((len(fetched),)), pltpu.SemaphoreType.DMA((RING,))],
        compiler_params=pltpu.CompilerParams(vmem_limit_bytes=LIMIT),
        name="backward",
    )(*ins.values())
    return SimpleNamespace(**dict(zip(outs, results)))


def swap(value, axis, mask):
    size = lax.axis_size(axis)
    return lax.ppermute(value, axis, [(i, i ^ mask) for i in range(size)])


def sum_everywhere(value):
    for axis in (NARROW, WIDE):
        bit = 1
        while bit < lax.axis_size(axis):
            value = value + swap(value, axis, bit)
            bit *= 2
    return value


def notes(live, ints):
    return jnp.pad(jnp.concatenate([live, ints]).astype(F32), (0, LANES - 1 - ints.shape[0]))[None]


def gather_all(params, smalls, ints, meanwhile):
    if lax.axis_size(WIDE) == 4 and lax.axis_size(NARROW) == 8:
        own = jnp.concatenate(
            [
                params.reshape(ROWS, LANES),
                smalls.reshape(SMALL_ROWS, LANES),
                jnp.pad(notes(ints[:1], ints), ((0, BLOCK - ROWS - SMALL_ROWS - 1), (0, 0))),
            ]
        ).astype(BF16)[None]
        z1, z2, z3 = (swap(own, NARROW, m) for m in (2, 4, 6))
        a, b = jnp.concatenate([own, z1]), jnp.concatenate([z2, z3])
        a, b, first = lax.optimization_barrier((a, b, meanwhile[:2]))
        near = jnp.concatenate([a, b])
        near_core = swap(near, NARROW, 1)
        ax, by = swap(a, WIDE, 1), swap(b, WIDE, 2)
        ax, by, second = lax.optimization_barrier((ax, by, meanwhile[2:]))
        side = jnp.concatenate([ax, by])
        side_core = swap(side, NARROW, 1)
        far_a = swap(jnp.concatenate([a, ax]), WIDE, 2)
        far_b = swap(jnp.concatenate([b, by]), WIDE, 1)
        far_a_core, far_b_core = swap(far_a, NARROW, 1), swap(far_b, NARROW, 1)
        near_marks = [0, 2, 4, 6]
        side_marks = [8, 10, 20, 22]
        a_marks = [16, 18, 24, 26]
        b_marks = [12, 14, 28, 30]
        plain = [(near, near_marks), (side, side_marks), (far_a, a_marks), (far_b, b_marks)]
        core = [(near_core, near_marks), (side_core, side_marks), (far_a_core, a_marks), (far_b_core, b_marks)]
        core = [(array, [m + 1 for m in marks]) for array, marks in core]
        both = plain + core
        return [array for array, _ in both], [marks for _, marks in both], True, first + second
    whole = lax.all_gather(params.astype(BF16), AXES, axis=0, tiled=True).reshape(BLOCKS, ROWS, LANES)
    little = lax.all_gather(smalls.astype(BF16), AXES, axis=0, tiled=True).reshape(BLOCKS, SMALL_ROWS, LANES)
    live = lax.all_gather(ints[:1], AXES, axis=0, tiled=True).reshape(BLOCKS, -1).sum(axis=1)
    others = swap(ints, WIDE, lax.axis_size(WIDE) // 2)
    extra = jnp.stack([notes(live[d : d + 1], others) for d in range(BLOCKS)])
    extra = jnp.pad(extra, ((0, 0), (0, BLOCK - ROWS - SMALL_ROWS - 1), (0, 0))).astype(BF16)
    return [jnp.concatenate([whole, little, extra], axis=1)], [list(range(BLOCKS))], False, meanwhile


def scatter_sums(stay, leave, relative):
    if relative:

        def join(kept, received):
            return (kept.astype(F32) + received.astype(F32)).astype(BF16)

        half = (2, BLOCKS // 8, BLOCK, LANES)
        a, b = join(stay, swap(leave, NARROW, 1)).reshape((2,) + half)
        a1, b1 = join(a[0], swap(a[1], WIDE, 2)), join(b[0], swap(b[1], WIDE, 1))
        a2, b2 = join(a1[:2], swap(a1[2:], WIDE, 1)), join(b1[:2], swap(b1[2:], WIDE, 2))
        own = a2[0].astype(F32)
        for value, mask in ((a2[1], 2), (b2[0], 4), (b2[1], 6)):
            own = own + swap(value, NARROW, mask).astype(F32)
        return own[:ROWS].reshape(-1), own[ROWS : ROWS + SMALL_ROWS].reshape(-1)
    grads = jnp.stack([(leave if d % 2 else stay)[block_place(d)] for d in range(BLOCKS)])
    large = grads[:, :ROWS].reshape(-1).astype(F32)
    little = grads[:, ROWS : ROWS + SMALL_ROWS].reshape(-1).astype(F32)
    return (
        lax.psum_scatter(large, AXES, scatter_dimension=0, tiled=True),
        lax.psum_scatter(little, AXES, scatter_dimension=0, tiled=True),
    )


def adamw(weight, moment, second, grad, rate):
    moment_new = 0.5 * moment + 0.5 * grad
    second_new = 0.99 * second + 0.01 * grad * grad
    direction = moment_new / (1.0 - 0.5**STEP) / (jnp.sqrt(second_new / (1.0 - 0.99**STEP)) + 1e-08)
    return (weight - rate * (direction + 0.01 * weight), moment_new, second_new)


def body(
    params,
    first_moment,
    second_moment,
    smalls,
    small_first,
    small_second,
    images,
    noise,
    sigma,
    freq,
    counts,
    partner,
):
    slots = images.shape[0]
    ints = jnp.concatenate([counts, partner[0]]).astype(jnp.int32)
    shrink = fir_matrix()
    phase = jnp.log(sigma)[:, None] * freq[None, :] * (2.0 * math.pi)
    feats = jnp.concatenate([jnp.sin(phase), jnp.cos(phase)], axis=-1)

    def planes(value):
        value = value.reshape(slots, 2, 16, 8, 4, CHAN).transpose(0, 5, 4, 2, 1, 3)
        return jnp.pad(value.reshape(slots, CHAN, PIX), ((0, 0), (0, 8 - CHAN), (0, 0)))

    feats = jnp.pad(feats.astype(BF16), ((0, 8 - slots), (0, 0)))
    own = (feats, planes(images), planes(noise))
    pieces, marks, relative, own = gather_all(params, smalls, ints, own)
    index = lax.axis_index(WIDE) * lax.axis_size(NARROW) + lax.axis_index(NARROW)
    me = (index if relative else jnp.zeros_like(index)).astype(jnp.int32)[None]
    data = SimpleNamespace(
        feats=own[0],
        images=own[1],
        noise=own[2],
        shrink=jnp.asarray(shrink, BF16),
        grow=jnp.asarray(4.0 * shrink.T, BF16),
    )
    kept = run_forward(me, sigma, pieces, marks, data)
    other = swap(kept.err16, WIDE, lax.axis_size(WIDE) // 2)
    done = run_backward(me, ints, other, kept, data)
    grad_params, grad_smalls = scatter_sums(done.stay, done.leave, relative)
    squares = jnp.sum(grad_params * grad_params) + jnp.sum(grad_smalls * grad_smalls)
    both = sum_everywhere(jnp.stack([squares, jnp.sum(done.loss)]))
    loss, grad_norm = both[1], jnp.sqrt(both[0])
    factor = jnp.minimum(1.0, 0.01 / (grad_norm + 1e-06))
    small_grad = factor * grad_smalls
    new_params, new_first, new_second = adamw(
        params, first_moment, second_moment, factor * grad_params, 0.15
    )
    new_smalls, new_small_first, new_small_second = adamw(
        smalls, small_first, small_second, small_grad, 0.2
    )
    return (
        loss,
        grad_norm,
        new_params,
        new_first,
        new_second,
        new_smalls,
        new_small_first,
        new_small_second,
        small_grad,
    )


def solution(mesh):
    flat, rows = P(AXES), P(AXES, None)
    return jax.shard_map(
        body,
        mesh=mesh,
        in_specs=(flat, flat, flat, flat, flat, flat, rows, rows, flat, P(), flat, rows),
        out_specs=(P(), P(), flat, flat, flat, flat, flat, flat, flat),
        check_vma=False,
    )
```

```python
import functools
import math
from types import SimpleNamespace

import jax
import jax.numpy as jnp
import numpy as np
from jax import lax
from jax.experimental import pallas as pl
from jax.experimental.pallas import tpu as pltpu
from jax.sharding import PartitionSpec as P

NF = 128
MID = 256
TEMB = 512
NFOUR = 128
IMG = 32
GROUPS = 32
CHAN = 3
STEP = 7
PIX = IMG * IMG
HALF = PIX // 4
INV_ROOT = 0.7071067811865476
WIDE, NARROW = AXES = ("wide", "narrow")
F32 = jnp.float32
BF16 = jnp.bfloat16

LANES = 128
BLOCKS = 32
ROWS = 552
SMALL_ROWS = 2
BLOCK = 560
CUT = 288


def mat_layout():
    return dict(
        temb_one=(2 * NFOUR, TEMB),
        temb_two=(TEMB, TEMB),
        conv_in=(9 * CHAN, NF),
        pyramid=(CHAN, MID),
        down_one=(9 * NF, MID),
        down_time=(TEMB, MID),
        down_two=(9 * MID, MID),
        down_skip=(NF, MID),
        attn_qkv=(MID, 3 * MID),
        attn_out=(MID, MID),
        up_one=(9 * MID, NF),
        up_time=(TEMB, NF),
        up_two=(9 * NF, NF),
        up_skip=(MID, NF),
        conv_out=(9 * 2 * NF, CHAN),
    )


def small_layout():
    return dict(
        temb_one_b=TEMB,
        temb_two_b=TEMB,
        conv_in_b=NF,
        pyramid_b=MID,
        down_gain_a=NF,
        down_bias_a=NF,
        down_one_b=MID,
        down_time_b=MID,
        down_gain_b=MID,
        down_bias_b=MID,
        down_two_b=MID,
        down_skip_b=MID,
        attn_gain=MID,
        attn_bias=MID,
        query_b=MID,
        value_b=MID,
        attn_out_b=MID,
        up_gain_a=MID,
        up_bias_a=MID,
        up_one_b=NF,
        up_time_b=NF,
        up_gain_b=NF,
        up_bias_b=NF,
        up_two_b=NF,
        up_skip_b=NF,
        final_gain=2 * NF,
        final_bias=2 * NF,
        conv_out_b=CHAN,
    )


def offsets():
    mats, smalls, used = {}, {}, 0
    for label, shape in mat_layout().items():
        mats[label] = (used // LANES,) + shape
        used += math.prod(shape)
    used = 0
    for label, length in small_layout().items():
        smalls[label] = (used // LANES, length)
        used += length
    return SimpleNamespace(**mats), SimpleNamespace(**smalls)


MATS, SMALLS = offsets()
WEIGHTS = list(mat_layout())
WEIGHT_SHAPES = mat_layout() | dict(conv_in=(LANES, NF), pyramid=(LANES, MID), conv_out=(LANES, 2 * NF))
RING = 8
TAPS = [(dy, dx) for dy in range(3) for dx in range(3)]


def pixel_order(side):
    across, down = side // 8, side // 2
    order = np.empty((across, down, 2, 8), np.int32)
    for xl in range(across):
        for yl in range(down):
            for yh in range(2):
                for xh in range(8):
                    order[xl, yl, yh, xh] = (yh * down + yl) * side + xh * across + xl
    return order.reshape(-1)


def fir_matrix():
    rows = np.arange(IMG // 2)[:, None]
    cols = np.arange(IMG)[None, :]
    offset = cols - 2 * rows + 1
    taps = np.where((offset == 0) | (offset == 3), 1.0, 0.0) + np.where(
        (offset == 1) | (offset == 2), 3.0, 0.0
    )
    both = np.kron(taps / 8.0, taps / 8.0)
    return both[pixel_order(IMG // 2)][:, pixel_order(IMG)].astype(np.float32)


def dot(a, b):
    return lax.dot_general(a, b, (((1,), (0,)), ((), ())), preferred_element_type=F32)


def dot_nt(a, b):
    return lax.dot_general(a, b, (((1,), (1,)), ((), ())), preferred_element_type=F32)


def dot_tn(a, b):
    return lax.dot_general(a, b, (((0,), (0,)), ((), ())), preferred_element_type=F32)


def two(value):
    high = value.astype(BF16)
    return high, (value - high.astype(F32)).astype(BF16)


def sigmoid(value):
    return 1.0 / (1.0 + jnp.exp(-value))


def rowsum(value):
    return jnp.sum(value, axis=0, keepdims=True)


def group_sums(rows, width):
    chans = rows[0].shape[1]
    at = lax.broadcasted_iota(jnp.int32, (16, chans), 0)
    stack = jnp.zeros((16, chans), F32)
    for n, row in enumerate(rows):
        rest = row
        for part in range(3):
            piece = rest.astype(BF16).astype(F32)
            stack = jnp.where(at == 3 * n + part, piece, stack)
            rest = rest - piece
    one = lax.broadcasted_iota(jnp.int32, (chans, chans), 0) // width
    other = lax.broadcasted_iota(jnp.int32, (chans, chans), 1) // width
    same = jnp.where(one == other, 1.0, 0.0).astype(BF16)
    sums = dot(stack.astype(BF16), same)
    return [sums[3 * n : 3 * n + 1] + sums[3 * n + 1 : 3 * n + 2] + sums[3 * n + 2 : 3 * n + 3] for n in range(len(rows))]


def norm_stats(value, width):
    count = float(value.shape[0] * width)
    center = group_sums([rowsum(value)], width)[0] / count
    shifted = value - center
    spread = group_sums([rowsum(shifted * shifted)], width)[0] / count
    return center, lax.rsqrt(spread + 1e-06)


def norm_back(grad, normed, gain, scale, width):
    count = float(grad.shape[0] * width)
    dbias = rowsum(grad)
    dgain = rowsum(grad * normed)
    first, second = group_sums([dbias * gain, dgain * gain], width)
    back = scale * (grad * gain - first / count - normed * (second / count))
    return back, dgain, dbias


def swish_back(pre):
    gate = sigmoid(pre)
    return gate * (1.0 + pre * (1.0 - gate))


def small(ref, label):
    at, length = label
    rows = max(1, length // LANES)
    return jnp.concatenate(
        [ref[(at + i) // 2, (at + i) % 2 : (at + i) % 2 + 1, :] for i in range(rows)], axis=1
    ) if rows > 1 else ref[at // 2, at % 2 : at % 2 + 1, :]


def add_small(ref, label, value):
    at, _ = label
    for i in range(value.shape[1] // LANES):
        j = at + i
        ref[j // 2, j % 2 : j % 2 + 1, :] += value[:, i * LANES : (i + 1) * LANES]


def fill_halo(ref, b, across, down):
    chans = ref.shape[-1]
    zero = jnp.zeros((across, 8, chans), F32)
    last = ref[b, 1 : across + 1, down].astype(F32)
    ref[b, 1 : across + 1, 0] = jnp.concatenate([zero, last[:, 0:8]], axis=1).astype(BF16)
    first = ref[b, 1 : across + 1, 1].astype(F32)
    ref[b, 1 : across + 1, down + 1] = jnp.concatenate([first[:, 8:16], zero], axis=1).astype(BF16)
    tiles = (down + 2) * 2
    at = lax.broadcasted_iota(jnp.int32, (tiles, 8, chans), 1)
    side = ref[b, across].astype(F32).reshape(tiles, 8, chans)
    side = jnp.where(at == 0, 0.0, pltpu.roll(side, 1, axis=1))
    ref[b, 0] = side.reshape(down + 2, 16, chans).astype(BF16)
    side = ref[b, 1].astype(F32).reshape(tiles, 8, chans)
    side = jnp.where(at == 7, 0.0, pltpu.roll(side, 7, axis=1))
    ref[b, across + 1] = side.reshape(down + 2, 16, chans).astype(BF16)


def set_inner(ref, b, across, down, value):
    chans = value.shape[1]
    ref[b, 1 : across + 1, 1 : down + 1] = value.astype(BF16).reshape(across, down, 16, chans)
    fill_halo(ref, b, across, down)


def taps_of(ref, b, xl, count, down, flip):
    chans = ref.shape[-1]
    parts = []
    for dy, dx in TAPS:
        y, x = (2 - dy, 2 - dx) if flip else (dy, dx)
        parts.append(ref[b, xl + x : xl + x + count, y : y + down].reshape(count * down * 16, chans))
    return jnp.concatenate(parts, axis=1)


def tap_columns(ref, chans):
    return jnp.concatenate([ref[t * chans : (t + 1) * chans, :] for t in range(9)], axis=1)


def picks(o):
    row = lax.broadcasted_iota(jnp.int32, (6 * LANES, 2 * NF), 0)
    col = lax.broadcasted_iota(jnp.int32, (6 * LANES, 2 * NF), 1)
    return jnp.where(row == CHAN * col + o, 1.0, 0.0).astype(BF16)


SAVED = dict(
    xin=((PIX, LANES), BF16),
    tiny=((HALF, LANES), BF16),
    h0=((PIX, NF), F32),
    ed1=((4, 10, 16, NF), BF16),
    sk0=((HALF, NF), BF16),
    a1=((HALF, MID), F32),
    ed2=((4, 10, 16, MID), BF16),
    h1=((HALF, MID), F32),
    g=((HALF, MID), BF16),
    qkv=((HALF, 3 * MID), BF16),
    prob=((HALF, HALF), BF16),
    mixed=((HALF, MID), BF16),
    h2=((HALF, MID), F32),
    eu1=((6, 18, 16, MID), BF16),
    sku=((PIX, MID), BF16),
    b1=((PIX, NF), F32),
    eu2=((6, 18, 16, NF), BF16),
    h3=((PIX, NF), F32),
    final=((PIX, 2 * NF), BF16),
    stats=((16, MID), F32),
)
EARLY = list(dict(sm=0, xin=0, tiny=0, h0=0, ed1=0, sk0=0, a1=0, ed2=0, h1=0, g=0, qkv=0, prob=0, mixed=0, h2=0))
TIME_SAVED = dict(
    t1=((8, TEMB), F32),
    s1=((8, TEMB), BF16),
    t2=((8, TEMB), F32),
    tact=((8, TEMB), BF16),
)


def in_step(parts):
    for _ in zip(*parts, strict=True):
        pass


def forward_kernel(piece_marks, slots, names, sent, *refs):
    r_pieces, refs = refs[: len(piece_marks)], refs[len(piece_marks) :]
    r = SimpleNamespace(**dict(zip(names, refs)))
    me = r.me[0]
    copies = []
    early = [name for name in sent if name[:2] == "w_" or name in TIME_SAVED or name in EARLY]

    def send(names):
        for name in names:
            source, target = getattr(r, name), getattr(r, "out_" + name)
            copies.append(pltpu.make_async_copy(source, target, r.sems.at[len(copies)]))
            copies[-1].start()

    stage, sm = r.stage, r.sm
    for n, (marks, first) in enumerate(piece_marks):
        for i, mark in enumerate(marks):
            home = jnp.bitwise_xor(me, mark)
            block = r_pieces[n][i].astype(F32)
            rows = min(block.shape[0], ROWS - first)
            stage[pl.ds(pl.multiple_of(home * ROWS + first, 8), rows), :] = block[:rows]
            if rows < block.shape[0]:
                sm[home] = block[rows:]
    for label in WEIGHTS:
        at, depth, width = getattr(MATS, label)
        out = getattr(r, "w_" + label)
        if width == CHAN:
            flat = jnp.concatenate([stage[pl.ds(at + i, 9, stride=6), :] for i in range(6)], axis=1).astype(BF16)
            out[...] = jnp.zeros(out.shape, BF16)
            pad = jnp.zeros((7, 2 * NF), F32)
            for o in range(CHAN):
                out[16 * o : 16 * o + 16, :] = jnp.concatenate([dot(flat, picks(o)), pad], axis=0).astype(BF16)
            continue
        if depth == 9 * CHAN:
            out[...] = jnp.zeros(out.shape, BF16)
            pad = jnp.zeros((7, NF), F32)
            for c in range(CHAN):
                part = stage[pl.ds(at + c, 9, stride=CHAN), :]
                out[16 * c : 16 * c + 16, :] = jnp.concatenate([part, pad], axis=0).astype(BF16)
            continue
        if depth == CHAN:
            out[...] = jnp.zeros(out.shape, BF16)
            pad = jnp.zeros((15, LANES), F32)
            for j in range(2):
                part = stage[pl.ds(at + j, CHAN, stride=2), :]
                for c in range(CHAN):
                    row = jnp.concatenate([part[c : c + 1], pad], axis=0)
                    out[16 * c : 16 * c + 16, j * LANES : (j + 1) * LANES] = row.astype(BF16)
            continue
        pad = out.shape[0] - depth
        for j in range(width // LANES):
            part = stage[pl.ds(at + j, depth, stride=width // LANES), :] if width > LANES else stage[pl.ds(at, depth), :]
            if pad:
                part = jnp.concatenate([part, jnp.zeros((pad, LANES), F32)], axis=0)
            out[:, j * LANES : (j + 1) * LANES] = part.astype(BF16)

    t1 = dot(r.feats[...], r.w_temb_one[...]) + small(sm, SMALLS.temb_one_b)
    r.t1[...] = t1
    s1 = (t1 * sigmoid(t1)).astype(BF16)
    r.s1[...] = s1
    t2 = dot(s1, r.w_temb_two[...]) + small(sm, SMALLS.temb_two_b)
    r.t2[...] = t2
    tact = (t2 * sigmoid(t2)).astype(BF16)
    r.tact[...] = tact
    r.pd[...] = dot(tact, r.w_down_time[...]) + (small(sm, SMALLS.down_time_b) + small(sm, SMALLS.down_one_b))
    r.pu[...] = dot(tact, r.w_up_time[...]) + (small(sm, SMALLS.up_time_b) + small(sm, SMALLS.up_one_b))

    def image(b):
        stats = r.stats

        def normed(value, width, gain, bias, at):
            center, scale = norm_stats(value, width)
            chans = value.shape[1]
            stats[b, 2 * at : 2 * at + 1, :chans] = center
            stats[b, 2 * at + 1 : 2 * at + 2, :chans] = scale
            return (value - center) * (scale * gain) + bias

        high, rest = (spread(r, part) for part in two(r.images[b] + r.sigma[b] * r.noise[b]))
        r.tiny[b] = (dot(r.shrink[...], high.astype(BF16)) + dot(r.shrink[...], rest.astype(BF16))).astype(BF16)
        field = r.field.at[b]
        set_field(field, high)
        r.xin[b] = tap_lanes(field, False).astype(BF16)
        yield
        h0 = dot(r.xin[b], r.w_conv_in[...]) + small(sm, SMALLS.conv_in_b)
        r.h0[b] = h0
        yield
        y = normed(h0, 4, small(sm, SMALLS.down_gain_a), small(sm, SMALLS.down_bias_a), 0)
        y = y * sigmoid(y)
        yield
        down = dot(r.shrink[...], jnp.concatenate([*two(y), *two(h0)], axis=1))
        set_inner(r.ed1, b, 2, 8, down[:, :NF] + down[:, NF : 2 * NF])
        sk0 = (down[:, 2 * NF : 3 * NF] + down[:, 3 * NF :]).astype(BF16)
        r.sk0[b] = sk0
        yield
        a1 = dot(taps_of(r.ed1, b, 0, 2, 8, False), r.w_down_one[...]) + r.pd[pl.ds(b, 1), :]
        r.a1[b] = a1
        yield
        y = normed(a1, 8, small(sm, SMALLS.down_gain_b), small(sm, SMALLS.down_bias_b), 1)
        set_inner(r.ed2, b, 2, 8, y * sigmoid(y))
        yield
        a2 = dot(taps_of(r.ed2, b, 0, 2, 8, False), r.w_down_two[...]) + dot(sk0, r.w_down_skip[...])
        a2 = (a2 + (small(sm, SMALLS.down_two_b) + small(sm, SMALLS.down_skip_b))) * INV_ROOT
        h1 = (a2 + dot(r.tiny[b], r.w_pyramid[...]) + small(sm, SMALLS.pyramid_b)) * INV_ROOT
        r.h1[b] = h1
        yield
        g = normed(h1, 8, small(sm, SMALLS.attn_gain), small(sm, SMALLS.attn_bias), 2).astype(BF16)
        r.g[b] = g
        yield
        proj = dot(g, r.w_attn_qkv[...])
        q = (proj[:, :MID] + small(sm, SMALLS.query_b)).astype(BF16)
        k = proj[:, MID : 2 * MID].astype(BF16)
        v = (proj[:, 2 * MID :] + small(sm, SMALLS.value_b)).astype(BF16)
        r.qkv[b] = jnp.concatenate([q, k, v], axis=1)
        yield
        scores = dot_nt(q, k) * (MID**-0.5)
        yield
        weight = jnp.exp(scores - jnp.max(scores, axis=1, keepdims=True))
        prob = (weight / jnp.sum(weight, axis=1, keepdims=True)).astype(BF16)
        r.prob[b] = prob
        yield
        mixed = dot(prob, v).astype(BF16)
        r.mixed[b] = mixed
        yield
        h2 = (h1 + dot(mixed, r.w_attn_out[...]) + small(sm, SMALLS.attn_out_b)) * INV_ROOT
        r.h2[b] = h2
        yield
        if b == 0:
            send(early)
        y = normed(h2, 8, small(sm, SMALLS.up_gain_a), small(sm, SMALLS.up_bias_a), 3)
        y = y * sigmoid(y)
        coarse = jnp.concatenate([*two(y), *two(h2)], axis=1)
        yield
        for xl in range(4):
            fine = dot(r.grow[xl * 256 : (xl + 1) * 256, :], coarse)
            part = (fine[:, :MID] + fine[:, MID : 2 * MID]).astype(BF16)
            r.eu1[b, xl + 1, 1:17] = part.reshape(16, 16, MID)
            r.sku[b, xl * 256 : (xl + 1) * 256, :] = (fine[:, 2 * MID : 3 * MID] + fine[:, 3 * MID :]).astype(BF16)
        fill_halo(r.eu1, b, 4, 16)
        yield
        for xl in range(4):
            r.b1[b, xl * 256 : (xl + 1) * 256, :] = (
                dot(taps_of(r.eu1, b, xl, 1, 16, False), r.w_up_one[...]) + r.pu[pl.ds(b, 1), :]
            )
        yield
        y = normed(r.b1[b], 4, small(sm, SMALLS.up_gain_b), small(sm, SMALLS.up_bias_b), 4)
        set_inner(r.eu2, b, 4, 16, y * sigmoid(y))
        yield
        bias = small(sm, SMALLS.up_two_b) + small(sm, SMALLS.up_skip_b)
        for xl in range(4):
            part = slice(xl * 256, (xl + 1) * 256)
            up = dot(taps_of(r.eu2, b, xl, 1, 16, False), r.w_up_two[...])
            r.h3[b, part, :] = (up + dot(r.sku[b, part, :], r.w_up_skip[...]) + bias) * INV_ROOT
        yield
        gain, bias = small(sm, SMALLS.final_gain), small(sm, SMALLS.final_bias)
        y = normed(r.h3[b], 8, gain[:, :NF], bias[:, :NF], 5)
        r.final[b, :, :NF] = (y * sigmoid(y)).astype(BF16)
        yield
        y = normed(r.h0[b], 8, gain[:, NF:], bias[:, NF:], 6)
        r.final[b, :, NF:] = (y * sigmoid(y)).astype(BF16)
        yield
        wide = dot_nt(r.final[b], r.w_conv_out[...])
        field = r.field.at[b]
        set_field(field, wide)
        total = tap_lanes(field, False)
        high, rest = two(total)
        wide = two((dot(high, r.unfan[...]) + dot(rest, r.unfan[...])) * r.own_x[...])
        err = dot(r.y_rows[...], wide[0]) + dot(r.y_rows[...], wide[1]) + r.out_bias[...] + r.noise[b]
        r.err[b] = err
        r.err16[b] = err.astype(BF16)

    prepare_out_bias(r, sm)
    in_step([image(b) for b in range(slots)])
    send(name for name in sent if name not in early)
    for copy in copies:
        copy.wait()


def prepare_out_bias(r, sm):
    bias = small(sm, SMALLS.conv_out_b)
    total = jnp.zeros((1, IMG * CHAN), F32)
    for c in range(CHAN):
        total += bias[:, c : c + 1] * r.colours[c : c + 1, :]
    r.out_bias[...] = jnp.broadcast_to(total, (IMG, IMG * CHAN))


def spread(r, value):
    wide = dot(r.y_of[...], value) * r.own_x[...]
    return dot(wide.astype(BF16), r.fan[...])


def pixel_maps():
    order = pixel_order(IMG)
    column, lane = np.arange(IMG * CHAN), np.arange(LANES)
    y_of = order[:, None] // IMG == np.arange(IMG)
    own_x = order[:, None] % IMG == column // CHAN
    fan = column[:, None] % CHAN == lane // 16
    colours = np.arange(8)[:, None] == column % CHAN
    maps = dict(y_of=y_of, y_rows=y_of.T, fan=fan, unfan=fan.T & (lane % 16 < 9)[:, None])
    maps = {name: value.astype(BF16) for name, value in maps.items()}
    return maps | dict(own_x=own_x.astype(np.float32), colours=colours.astype(np.float32))


def set_field(field, value):
    field[1:5, 1:17] = value.reshape(4, 16, 16, LANES)
    zero = jnp.zeros((4, 8, LANES), F32)
    field[1:5, 0] = jnp.concatenate([zero, field[1:5, 16, 0:8]], axis=1)
    field[1:5, 17] = jnp.concatenate([field[1:5, 1, 8:16], zero], axis=1)
    at = lax.broadcasted_iota(jnp.int32, (36, 8, LANES), 1)
    side = pltpu.roll(field[4].reshape(36, 8, LANES), 1, axis=1)
    field[0] = jnp.where(at == 0, 0.0, side).reshape(18, 16, LANES)
    side = pltpu.roll(field[1].reshape(36, 8, LANES), 7, axis=1)
    field[5] = jnp.where(at == 7, 0.0, side).reshape(18, 16, LANES)


def backward_kernel(slots, names, fetched, *refs):
    r = SimpleNamespace(**dict(zip(names, refs)))
    copies = []
    for n, name in enumerate(fetched):
        copies.append(pltpu.make_async_copy(getattr(r, "in_" + name), getattr(r, name), r.sems.at[n]))
        copies[-1].start()

    def arrive(name):
        while len(copies) > len(fetched) - 1 - fetched.index(name):
            copies.pop(0).wait()

    me = r.me[0]
    sm, stage, gsm = r.sm, r.stage, r.gsm
    stats = r.stats
    total = jnp.sum(sm[...], axis=0)[SMALL_ROWS : SMALL_ROWS + 1, 0:1]
    theirs = sm[jnp.bitwise_xor(me, BLOCKS // 2), SMALL_ROWS : SMALL_ROWS + 1, :]
    gsm[...] = jnp.zeros(gsm.shape, F32)
    r.dpd[...] = jnp.zeros(r.dpd.shape, F32)
    r.dpu[...] = jnp.zeros(r.dpu.shape, F32)
    r.dout_sum[...] = jnp.zeros(r.dout_sum.shape, F32)
    r.loss[...] = jnp.zeros(r.loss.shape, F32)
    counts, pairs = r.ints[0], r.ints
    other_counts = theirs[:, 1:2]

    def put(label, value, first=0):
        at, _, width = label
        step = width // LANES
        for j in range(step):
            part = value[:, j * LANES : (j + 1) * LANES]
            if step == 1:
                stage[pl.ds(at + first, value.shape[0]), :] = part
            else:
                stage[pl.ds(at + first * step + j, value.shape[0], stride=step), :] = part

    def image(b):
        def stat(at, chans):
            return stats[b, 2 * at : 2 * at + 1, :chans], stats[b, 2 * at + 1 : 2 * at + 2, :chans]

        def renorm(value, at, gain, bias):
            center, scale = stat(at, value.shape[1])
            normed = (value - center) * scale
            return normed, normed * gain + bias, scale

        err = r.err[b]
        mine = r.other[pairs[1 + b]].astype(F32)
        gap = err - mine
        live = jnp.where(b < counts, 1.0, 0.0)
        scale = 1.0 / (total * (CHAN * PIX))
        r.loss[...] += (live * scale) * (0.5 * err * err + 0.25 * gap * gap)
        grad = (live * scale) * (err + 0.5 * gap)
        for s in range(slots):
            on = jnp.where((theirs[:, 2 + s : 3 + s] == b) & (s < other_counts), 0.5 * scale, 0.0)
            grad += on * (err - r.other[s].astype(F32))
        yield
        if b == 0:
            arrive(FETCH_ORDER[6])
        r.dout_sum[...] += grad
        field = r.field.at[b]
        set_field(field, spread(r, grad.astype(BF16)))
        cols = tap_lanes(field, True).astype(BF16)
        r.cols[b] = cols
        yield
        gain, bias = small(sm, SMALLS.final_gain), small(sm, SMALLS.final_bias)
        back = dot(cols, r.w_conv_out[...])
        yield
        n3, y3, scale3 = renorm(r.h3[b], 5, gain[:, :NF], bias[:, :NF])
        dh3, dgain, dbias = norm_back(back[:, :NF] * swish_back(y3), n3, gain[:, :NF], scale3, 8)
        n0, y0, scale0 = renorm(r.h0[b], 6, gain[:, NF:], bias[:, NF:])
        dh0, dgain0, dbias0 = norm_back(back[:, NF:] * swish_back(y0), n0, gain[:, NF:], scale0, 8)
        add_small(gsm, SMALLS.final_gain, jnp.concatenate([dgain, dgain0], axis=1))
        add_small(gsm, SMALLS.final_bias, jnp.concatenate([dbias, dbias0], axis=1))
        r.dh0[b] = dh0
        yield
        dh3 = dh3 * INV_ROOT
        add_small(gsm, SMALLS.up_two_b, rowsum(dh3))
        set_inner(r.gu2, b, 4, 16, dh3)
        yield
        turned = tap_columns(r.w_up_two, NF)
        for xl in range(4):
            r.wide[b, xl * 256 : (xl + 1) * 256, :] = dot_nt(taps_of(r.gu2, b, xl, 1, 16, True), turned)
        yield
        gain, bias = small(sm, SMALLS.up_gain_b), small(sm, SMALLS.up_bias_b)
        n, y, scale1 = renorm(r.b1[b], 4, gain, bias)
        db1, dgain, dbias = norm_back(r.wide[b] * swish_back(y), n, gain, scale1, 4)
        add_small(gsm, SMALLS.up_gain_b, dgain)
        add_small(gsm, SMALLS.up_bias_b, dbias)
        r.dpu[pl.ds(b, 1), :] = rowsum(db1)
        set_inner(r.gu1, b, 4, 16, db1)
        yield
        turned = tap_columns(r.w_up_one, MID)
        half = jnp.zeros((HALF, 2 * MID), F32)
        for xl in range(4):
            branch = dot_nt(taps_of(r.gu1, b, xl, 1, 16, True), turned)
            skip = dot_nt(r.gu2[b, xl + 1, 1:17].reshape(256, NF), r.w_up_skip[...])
            both = jnp.concatenate([branch.astype(BF16), skip.astype(BF16)], axis=1)
            half += dot(r.shrink[:, xl * 256 : (xl + 1) * 256], both)
        half = half * 4.0
        yield
        if b == 0:
            arrive(FETCH_ORDER[-1])
            arrive(fetched[-1])
        gain, bias = small(sm, SMALLS.up_gain_a), small(sm, SMALLS.up_bias_a)
        n, y, scale2 = renorm(r.h2[b], 3, gain, bias)
        dh2, dgain, dbias = norm_back(half[:, :MID] * swish_back(y), n, gain, scale2, 8)
        add_small(gsm, SMALLS.up_gain_a, dgain)
        add_small(gsm, SMALLS.up_bias_a, dbias)
        dh2 = (dh2 + half[:, MID:]) * INV_ROOT
        add_small(gsm, SMALLS.attn_out_b, rowsum(dh2))
        datt = dh2.astype(BF16)
        r.datt[b] = datt
        yield
        dmixed = dot_nt(datt, r.w_attn_out[...]).astype(BF16)
        q, k, v = r.qkv[b, :, :MID], r.qkv[b, :, MID : 2 * MID], r.qkv[b, :, 2 * MID :]
        prob = r.prob[b]
        dprob = dot_nt(dmixed, v)
        yield
        dv = dot_tn(prob, dmixed)
        yield
        wide = prob.astype(F32)
        dscore = wide * (dprob - jnp.sum(wide * dprob, axis=1, keepdims=True))
        dscore = (dscore * (MID**-0.5)).astype(BF16)
        yield
        dq = dot(dscore, k)
        dk = dot_tn(dscore, q)
        add_small(gsm, SMALLS.query_b, rowsum(dq))
        add_small(gsm, SMALLS.value_b, rowsum(dv))
        dqkv = jnp.concatenate([dq, dk, dv], axis=1).astype(BF16)
        r.dqkv[b] = dqkv
        yield
        dg = dot_nt(dqkv, r.w_attn_qkv[...])
        yield
        gain, bias = small(sm, SMALLS.attn_gain), small(sm, SMALLS.attn_bias)
        n, _, scale2 = renorm(r.h1[b], 2, gain, bias)
        dh1, dgain, dbias = norm_back(dg, n, gain, scale2, 8)
        add_small(gsm, SMALLS.attn_gain, dgain)
        add_small(gsm, SMALLS.attn_bias, dbias)
        dh1 = (dh1 + dh2) * INV_ROOT
        r.dpyr[b] = dh1.astype(BF16)
        add_small(gsm, SMALLS.pyramid_b, rowsum(dh1))
        da2 = dh1 * INV_ROOT
        add_small(gsm, SMALLS.down_two_b, rowsum(da2))
        set_inner(r.gd2, b, 2, 8, da2)
        yield
        dsk0 = dot_nt(r.gd2[b, 1:3, 1:9].reshape(HALF, MID), r.w_down_skip[...])
        turned = tap_columns(r.w_down_two, MID)
        du = dot_nt(taps_of(r.gd2, b, 0, 2, 8, True), turned)
        yield
        gain, bias = small(sm, SMALLS.down_gain_b), small(sm, SMALLS.down_bias_b)
        n, y, scale2 = renorm(r.a1[b], 1, gain, bias)
        da1, dgain, dbias = norm_back(du * swish_back(y), n, gain, scale2, 8)
        add_small(gsm, SMALLS.down_gain_b, dgain)
        add_small(gsm, SMALLS.down_bias_b, dbias)
        r.dpd[pl.ds(b, 1), :] = rowsum(da1)
        set_inner(r.gd1, b, 2, 8, da1)
        yield
        turned = tap_columns(r.w_down_one, NF)
        dd0 = dot_nt(taps_of(r.gd1, b, 0, 2, 8, True), turned)
        both = jnp.concatenate([dd0, dsk0], axis=1).astype(BF16)
        fine = dot(r.grow[...], both) * 0.25
        yield
        gain, bias = small(sm, SMALLS.down_gain_a), small(sm, SMALLS.down_bias_a)
        n, y, scale1 = renorm(r.h0[b], 0, gain, bias)
        back0, dgain, dbias = norm_back(fine[:, :NF] * swish_back(y), n, gain, scale1, 4)
        add_small(gsm, SMALLS.down_gain_a, dgain)
        add_small(gsm, SMALLS.down_bias_a, dbias)
        dh0 = r.dh0[b] + back0 + fine[:, NF:]
        add_small(gsm, SMALLS.conv_in_b, rowsum(dh0))
        r.din[b] = dh0.astype(BF16)

    in_step([image(b) for b in range(slots)])

    whole = slots * PIX
    fewer = slots * HALF
    def conv_grad(label, acts, grads, across, down):
        chans, rows = acts.shape[-1], slots * across * down * 16
        left = acts[:, 1 : across + 1, 1 : down + 1].reshape(rows, chans)
        for dy in range(3):
            right = jnp.concatenate(
                [
                    grads[:, 2 - dx : 2 - dx + across, 2 - dy : 2 - dy + down].reshape(rows, grads.shape[-1])
                    for dx in range(3)
                ],
                axis=1,
            )
            back = dot_tn(left, right)
            for dx in range(3):
                put(label, back[:, dx * grads.shape[-1] : (dx + 1) * grads.shape[-1]], (3 * dy + dx) * chans)

    dpd, dpu = r.dpd[...], r.dpu[...]
    for label in (SMALLS.down_time_b, SMALLS.down_one_b):
        add_small(gsm, label, rowsum(dpd))
    for label in (SMALLS.up_time_b, SMALLS.up_one_b):
        add_small(gsm, label, rowsum(dpu))
    dpd16, dpu16 = dpd.astype(BF16), dpu.astype(BF16)
    put(MATS.down_time, dot_tn(r.tact[...], dpd16))
    put(MATS.up_time, dot_tn(r.tact[...], dpu16))
    dtact = dot_nt(dpd16, r.w_down_time[...]) + dot_nt(dpu16, r.w_up_time[...])
    dt2 = dtact * swish_back(r.t2[...])
    add_small(gsm, SMALLS.temb_two_b, rowsum(dt2))
    put(MATS.temb_two, dot_tn(r.s1[...], dt2.astype(BF16)))
    dt1 = dot_nt(dt2.astype(BF16), r.w_temb_two[...]) * swish_back(r.t1[...])
    add_small(gsm, SMALLS.temb_one_b, rowsum(dt1))
    put(MATS.temb_one, dot_tn(r.feats[...], dt1.astype(BF16)))
    for label, twin in ((SMALLS.up_skip_b, SMALLS.up_two_b), (SMALLS.down_skip_b, SMALLS.down_two_b)):
        value = small(gsm, twin)
        add_small(gsm, label, value)
    sums = rowsum(r.dout_sum[...])
    lane = lax.broadcasted_iota(jnp.int32, (1, LANES), 1)
    total_bias = jnp.zeros((1, LANES), F32)
    for c in range(CHAN):
        own = jnp.sum(sums * r.colours[c : c + 1, :], axis=1, keepdims=True)
        total_bias += jnp.where(lane == c, own, 0.0)
    add_small(gsm, SMALLS.conv_out_b, total_bias)
    dout = dot_tn(r.cols[...].reshape(whole, LANES), r.final[...].reshape(whole, 2 * NF))
    flat = jnp.zeros((16, 6 * LANES), F32)
    for o in range(CHAN):
        flat += dot_nt(dout[16 * o : 16 * o + 16].astype(BF16), picks(o))
    at = MATS.conv_out[0]
    for i in range(6):
        for t in range(9):
            stage[at + 6 * t + i : at + 6 * t + i + 1, :] = flat[t : t + 1, i * LANES : (i + 1) * LANES]

    last = MATS.conv_out[0] + 54
    stage[last : BLOCKS * ROWS, :] = jnp.zeros((BLOCKS * ROWS - last, LANES), F32)
    put(MATS.up_skip, dot_tn(r.sku[...].reshape(whole, MID), r.gu2[:, 1:5, 1:17].reshape(whole, NF)))
    conv_grad(MATS.up_two, r.eu2, r.gu2, 4, 16)
    conv_grad(MATS.up_one, r.eu1, r.gu1, 4, 16)
    put(MATS.attn_out, dot_tn(r.mixed[...].reshape(fewer, MID), r.datt[...].reshape(fewer, MID)))
    put(MATS.attn_qkv, dot_tn(r.g[...].reshape(fewer, MID), r.dqkv[...].reshape(fewer, 3 * MID)))
    put(MATS.down_skip, dot_tn(r.sk0[...].reshape(fewer, NF), r.gd2[:, 1:3, 1:9].reshape(fewer, MID)))
    conv_grad(MATS.down_two, r.ed2, r.gd2, 2, 8)
    conv_grad(MATS.down_one, r.ed1, r.gd1, 2, 8)
    back = dot_tn(r.tiny[...].reshape(fewer, LANES), r.dpyr[...].reshape(fewer, MID))
    put(MATS.pyramid, jnp.concatenate([back[16 * c : 16 * c + 1] for c in range(CHAN)], axis=0))
    back = dot_tn(r.xin[...].reshape(whole, LANES), r.din[...].reshape(whole, NF))
    for c in range(CHAN):
        stage[pl.ds(MATS.conv_in[0] + c, 9, stride=CHAN), :] = back[16 * c : 16 * c + 9]
    ring, sems = r.ring, r.ring_sems

    class sending:
        def __init__(self, upper, lower, d, slot):
            place = block_place(jnp.bitwise_xor(d, me))
            self.copies = [
                pltpu.make_async_copy(ring.at[slot, :CUT], upper.at[place], sems.at[0, slot]),
                pltpu.make_async_copy(ring.at[slot, CUT:], lower.at[place], sems.at[1, slot]),
            ]

        def start(self):
            for copy in self.copies:
                copy.start()

        def wait(self):
            for copy in self.copies:
                copy.wait()

    def give(d, carry):
        slot = d % RING

        @pl.when(d >= RING)
        def _():
            sending(r.stay, r.stay_low, d, slot).wait()

        block = jnp.concatenate([stage[pl.ds(pl.multiple_of(d * ROWS, 8), ROWS), :], gsm[d]], axis=0)
        ring[slot] = block.astype(BF16)
        goes = jnp.bitwise_xor(d, me) % 2 == 1

        @pl.when(goes)
        def _():
            sending(r.leave, r.leave_low, d, slot).start()

        @pl.when(jnp.logical_not(goes))
        def _():
            sending(r.stay, r.stay_low, d, slot).start()

        return carry

    lax.fori_loop(0, BLOCKS, give, 0)
    for d in range(BLOCKS - RING, BLOCKS):
        sending(r.stay, r.stay_low, d, d % RING).wait()


def tap_lanes(field, flip):
    lane = lax.broadcasted_iota(jnp.int32, (PIX, LANES), 1) % 16
    total = jnp.zeros((PIX, LANES), F32)
    for t, (dy, dx) in enumerate(TAPS):
        y, x = (2 - dy, 2 - dx) if flip else (dy, dx)
        total = jnp.where(lane == t, field[x : x + 4, y : y + 16].reshape(PIX, LANES), total)
    return total


def block_place(mark):
    low, high, x, y = (mark // 2) % 2, (mark // 4) % 2, (mark // 8) % 2, mark // 16
    return high * 8 + (4 * y + 2 * x + high * 2 * (x - y)) + low


def vmem():
    return pl.BlockSpec(memory_space=pltpu.VMEM)


def anywhere():
    return pl.BlockSpec(memory_space=pl.ANY)


def smem():
    return pl.BlockSpec(memory_space=pltpu.SMEM)


LIMIT = 60 * 1024 * 1024


def run_forward(me, sigma, pieces, marks, data):
    slots = data.images.shape[0]
    ins = dict(me=me, sigma=sigma) | vars(data)
    outs = {"w_" + label: (WEIGHT_SHAPES[label], BF16) for label in WEIGHTS}
    outs |= dict(sm=((BLOCKS, 8, LANES), F32)) | TIME_SAVED
    outs |= {label: ((slots,) + shape, dtype) for label, (shape, dtype) in SAVED.items()}
    outs |= dict(err=((slots, IMG, IMG * CHAN), F32), err16=((slots, IMG, IMG * CHAN), BF16))
    scratch = dict(
        stage=((BLOCKS * ROWS, LANES), F32),
        pd=((8, MID), F32),
        pu=((8, NF), F32),
        out_bias=((IMG, IMG * CHAN), F32),
        field=((slots, 6, 18, 16, LANES), F32),
    )
    names = list(ins) + ["out_" + label for label in outs] + list(outs) + list(scratch) + ["sems"]
    results = pl.pallas_call(
        functools.partial(forward_kernel, marks, slots, names, list(outs)),
        out_shape=[jax.ShapeDtypeStruct(*v) for v in outs.values()],
        in_specs=[vmem()] * len(pieces) + [smem()] * 2 + [vmem()] * (len(ins) - 2),
        out_specs=[anywhere()] * len(outs),
        scratch_shapes=[pltpu.VMEM(*v) for v in (outs | scratch).values()] + [pltpu.SemaphoreType.DMA((len(outs),))],
        compiler_params=pltpu.CompilerParams(vmem_limit_bytes=LIMIT),
        name="forward",
    )(*pieces, *ins.values())
    return SimpleNamespace(**dict(zip(outs, results)))


FETCH_ORDER = list(
    dict(
        w_conv_out=0,
        h3=0,
        h0=0,
        w_up_two=0,
        b1=0,
        w_up_skip=0,
        w_up_one=0,
        h2=0,
        w_attn_out=0,
        qkv=0,
        prob=0,
        w_attn_qkv=0,
        h1=0,
        w_down_skip=0,
        w_down_two=0,
        a1=0,
        w_down_one=0,
        w_down_time=0,
        w_up_time=0,
        t2=0,
        s1=0,
        w_temb_two=0,
        t1=0,
        tact=0,
        final=0,
        sku=0,
        eu2=0,
        eu1=0,
        mixed=0,
        g=0,
        sk0=0,
        ed2=0,
        ed1=0,
        xin=0,
        tiny=0,
    )
)


def run_backward(me, ints, other, kept, data):
    slots = other.shape[0]
    ins = dict(me=me, ints=ints)
    scalars = len(ins)
    ins |= dict(other=other, err=kept.err, sm=kept.sm, stats=kept.stats)
    ins |= dict(y_of=data.y_of, own_x=data.own_x, fan=data.fan, colours=data.colours)
    direct = len(ins)
    fetched = dict(shrink=data.shrink)
    fetched |= {name: getattr(kept, name) for name in FETCH_ORDER}
    fetched |= dict(grow=data.grow, feats=data.feats)
    ins |= {"in_" + name: value for name, value in fetched.items()}
    upper = ((BLOCKS // 2, CUT, LANES), BF16)
    lower = ((BLOCKS // 2, BLOCK - CUT, LANES), BF16)
    outs = dict(stay=upper, stay_low=lower, leave=upper, leave_low=lower, loss=((IMG, IMG * CHAN), F32))
    scratch = {name: (value.shape, value.dtype) for name, value in fetched.items()}
    scratch |= dict(
        stage=((BLOCKS * ROWS, LANES), F32),
        gsm=((BLOCKS, 8, LANES), F32),
        ring=((RING, BLOCK, LANES), BF16),
        dpd=((8, MID), F32),
        dpu=((8, NF), F32),
        dout_sum=((IMG, IMG * CHAN), F32),
        field=((slots, 6, 18, 16, LANES), F32),
        cols=((slots, PIX, LANES), BF16),
        gu2=((slots, 6, 18, 16, NF), BF16),
        gu1=((slots, 6, 18, 16, NF), BF16),
        gd2=((slots, 4, 10, 16, MID), BF16),
        gd1=((slots, 4, 10, 16, MID), BF16),
        wide=((slots, PIX, NF), F32),
        dh0=((slots, PIX, NF), F32),
        din=((slots, PIX, NF), BF16),
        datt=((slots, HALF, MID), BF16),
        dqkv=((slots, HALF, 3 * MID), BF16),
        dpyr=((slots, HALF, MID), BF16),
    )
    names = list(ins) + list(outs) + list(scratch) + ["sems", "ring_sems"]
    results = pl.pallas_call(
        functools.partial(backward_kernel, slots, names, list(fetched)),
        out_shape=[jax.ShapeDtypeStruct(*v) for v in outs.values()],
        in_specs=[smem()] * scalars + [vmem()] * (direct - scalars) + [anywhere()] * (len(ins) - direct),
        out_specs=[anywhere()] * 4 + [vmem()],
        scratch_shapes=[pltpu.VMEM(*v) for v in scratch.values()]
        + [pltpu.SemaphoreType.DMA((len(fetched),)), pltpu.SemaphoreType.DMA((2, RING))],
        compiler_params=pltpu.CompilerParams(vmem_limit_bytes=LIMIT),
        name="backward",
    )(*ins.values())
    return SimpleNamespace(**dict(zip(outs, results)))


def swap(value, axis, mask):
    size = lax.axis_size(axis)
    return lax.ppermute(value, axis, [(i, i ^ mask) for i in range(size)])


def sum_everywhere(value):
    for axis in (NARROW, WIDE):
        bit = 1
        while bit < lax.axis_size(axis):
            value = value + swap(value, axis, bit)
            bit *= 2
    return value


def notes(live, ints):
    return jnp.pad(jnp.concatenate([live, ints]).astype(F32), (0, LANES - 1 - ints.shape[0]))[None]


def gather_all(params, smalls, ints, meanwhile):
    if lax.axis_size(WIDE) == 4 and lax.axis_size(NARROW) == 8:
        rows = params.reshape(ROWS, LANES)
        tail = jnp.pad(notes(ints[:1], ints), ((0, BLOCK - ROWS - SMALL_ROWS - 1), (0, 0)))
        tail = jnp.concatenate([rows[CUT:], smalls.reshape(SMALL_ROWS, LANES), tail])
        owns = [rows[:CUT].astype(BF16)[None], tail.astype(BF16)[None]]
        near, side, far = [], [], []
        for own in owns:
            z1, z2, z3 = (swap(own, NARROW, m) for m in (2, 4, 6))
            near.append((jnp.concatenate([own, z1]), jnp.concatenate([z2, z3])))
        near[0], first = lax.optimization_barrier((near[0], meanwhile[:2]))
        for a, b in near:
            side.append((swap(a, WIDE, 1), swap(b, WIDE, 2)))
        side[0], second = lax.optimization_barrier((side[0], meanwhile[2:]))
        for (a, b), (ax, by) in zip(near, side):
            far.append((swap(jnp.concatenate([a, ax]), WIDE, 2), swap(jnp.concatenate([b, by]), WIDE, 1)))
        pieces, marks = [], []
        for part in range(2):
            arrays = [jnp.concatenate(near[part]), jnp.concatenate(side[part]), *far[part]]
            lists = [[0, 2, 4, 6], [8, 10, 20, 22], [16, 18, 24, 26], [12, 14, 28, 30]]
            pieces += arrays + [swap(array, NARROW, 1) for array in arrays]
            marks += [(at, part * CUT) for at in lists] + [([m + 1 for m in at], part * CUT) for at in lists]
        return pieces, marks, True, first + second
    whole = lax.all_gather(params.astype(BF16), AXES, axis=0, tiled=True).reshape(BLOCKS, ROWS, LANES)
    little = lax.all_gather(smalls.astype(BF16), AXES, axis=0, tiled=True).reshape(BLOCKS, SMALL_ROWS, LANES)
    live = lax.all_gather(ints[:1], AXES, axis=0, tiled=True).reshape(BLOCKS, -1).sum(axis=1)
    others = swap(ints, WIDE, lax.axis_size(WIDE) // 2)
    extra = jnp.stack([notes(live[d : d + 1], others) for d in range(BLOCKS)])
    extra = jnp.pad(extra, ((0, 0), (0, BLOCK - ROWS - SMALL_ROWS - 1), (0, 0))).astype(BF16)
    return [jnp.concatenate([whole, little, extra], axis=1)], [(list(range(BLOCKS)), 0)], False, meanwhile


def scatter_sums(stay, leave, relative):
    if relative:

        def join(kept, received):
            return (kept.astype(F32) + received.astype(F32)).astype(BF16)

        parts = [join(a, swap(b, NARROW, 1)) for a, b in zip(stay, leave)]
        parts = [part.reshape((2, 2, BLOCKS // 8) + part.shape[1:]) for part in parts]
        parts = [(join(a[0], swap(a[1], WIDE, 2)), join(b[0], swap(b[1], WIDE, 1))) for a, b in parts]
        parts = [(join(a[:2], swap(a[2:], WIDE, 1)), join(b[:2], swap(b[2:], WIDE, 2))) for a, b in parts]
        done = []
        for a, b in parts:
            own = a[0].astype(F32)
            for value, mask in ((a[1], 2), (b[0], 4), (b[1], 6)):
                own = own + swap(value, NARROW, mask).astype(F32)
            done.append(own)
        own = jnp.concatenate(done)
        return own[:ROWS].reshape(-1), own[ROWS : ROWS + SMALL_ROWS].reshape(-1)
    stay, leave = jnp.concatenate(stay, axis=1), jnp.concatenate(leave, axis=1)
    grads = jnp.stack([(leave if d % 2 else stay)[block_place(d)] for d in range(BLOCKS)])
    large = grads[:, :ROWS].reshape(-1).astype(F32)
    little = grads[:, ROWS : ROWS + SMALL_ROWS].reshape(-1).astype(F32)
    return (
        lax.psum_scatter(large, AXES, scatter_dimension=0, tiled=True),
        lax.psum_scatter(little, AXES, scatter_dimension=0, tiled=True),
    )


def adamw(weight, moment, second, grad, rate):
    moment_new = 0.5 * moment + 0.5 * grad
    second_new = 0.99 * second + 0.01 * grad * grad
    direction = moment_new / (1.0 - 0.5**STEP) / (jnp.sqrt(second_new / (1.0 - 0.99**STEP)) + 1e-08)
    return (weight - rate * (direction + 0.01 * weight), moment_new, second_new)


def body(
    params,
    first_moment,
    second_moment,
    smalls,
    small_first,
    small_second,
    images,
    noise,
    sigma,
    freq,
    counts,
    partner,
):
    slots = images.shape[0]
    ints = jnp.concatenate([counts, partner[0]]).astype(jnp.int32)
    shrink = fir_matrix()
    phase = jnp.log(sigma)[:, None] * freq[None, :] * (2.0 * math.pi)
    feats = jnp.concatenate([jnp.sin(phase), jnp.cos(phase)], axis=-1)
    feats = jnp.pad(feats.astype(BF16), ((0, 8 - slots), (0, 0)))
    own = (feats, images.reshape(slots, IMG, IMG * CHAN), noise.reshape(slots, IMG, IMG * CHAN))
    pieces, marks, relative, own = gather_all(params, smalls, ints, own)
    index = lax.axis_index(WIDE) * lax.axis_size(NARROW) + lax.axis_index(NARROW)
    me = (index if relative else jnp.zeros_like(index)).astype(jnp.int32)[None]
    data = SimpleNamespace(
        feats=own[0],
        images=own[1],
        noise=own[2],
        shrink=jnp.asarray(shrink, BF16),
        grow=jnp.asarray(4.0 * shrink.T, BF16),
        **{name: jnp.asarray(value) for name, value in pixel_maps().items()},
    )
    kept = run_forward(me, sigma, pieces, marks, data)
    other = swap(kept.err16, WIDE, lax.axis_size(WIDE) // 2)
    done = run_backward(me, ints, other, kept, data)
    grad_params, grad_smalls = scatter_sums((done.stay, done.stay_low), (done.leave, done.leave_low), relative)
    squares = jnp.sum(grad_params * grad_params) + jnp.sum(grad_smalls * grad_smalls)
    lane = lax.broadcasted_iota(jnp.int32, (1, LANES), 1)
    both = sum_everywhere(jnp.where(lane == 0, squares, jnp.where(lane == 1, jnp.sum(done.loss), 0.0)))
    loss, grad_norm = both[0, 1], jnp.sqrt(both[0, 0])
    factor = jnp.minimum(1.0, 0.01 / (grad_norm + 1e-06))
    small_grad = factor * grad_smalls
    new_params, new_first, new_second = adamw(
        params, first_moment, second_moment, factor * grad_params, 0.15
    )
    new_smalls, new_small_first, new_small_second = adamw(
        smalls, small_first, small_second, small_grad, 0.2
    )
    return (
        loss,
        grad_norm,
        new_params,
        new_first,
        new_second,
        new_smalls,
        new_small_first,
        new_small_second,
        small_grad,
    )


def solution(mesh):
    flat, rows = P(AXES), P(AXES, None)
    return jax.shard_map(
        body,
        mesh=mesh,
        in_specs=(flat, flat, flat, flat, flat, flat, rows, rows, flat, P(), flat, rows),
        out_specs=(P(), P(), flat, flat, flat, flat, flat, flat, flat),
        check_vma=False,
    )
```

```python
import functools
import math
from types import SimpleNamespace

import jax
import jax.numpy as jnp
import numpy as np
from jax import lax
from jax.experimental import pallas as pl
from jax.experimental.pallas import tpu as pltpu
from jax.sharding import PartitionSpec as P

NF = 128
MID = 256
TEMB = 512
NFOUR = 128
IMG = 32
GROUPS = 32
CHAN = 3
STEP = 7
PIX = IMG * IMG
HALF = PIX // 4
INV_ROOT = 0.7071067811865476
WIDE, NARROW = AXES = ("wide", "narrow")
F32 = jnp.float32
BF16 = jnp.bfloat16

LANES = 128
BLOCKS = 32
ROWS = 552
SMALL_ROWS = 2
BLOCK = 560
CUT = 288


def mat_layout():
    return dict(
        temb_one=(2 * NFOUR, TEMB),
        temb_two=(TEMB, TEMB),
        conv_in=(9 * CHAN, NF),
        pyramid=(CHAN, MID),
        down_one=(9 * NF, MID),
        down_time=(TEMB, MID),
        down_two=(9 * MID, MID),
        down_skip=(NF, MID),
        attn_qkv=(MID, 3 * MID),
        attn_out=(MID, MID),
        up_one=(9 * MID, NF),
        up_time=(TEMB, NF),
        up_two=(9 * NF, NF),
        up_skip=(MID, NF),
        conv_out=(9 * 2 * NF, CHAN),
    )


def small_layout():
    return dict(
        temb_one_b=TEMB,
        temb_two_b=TEMB,
        conv_in_b=NF,
        pyramid_b=MID,
        down_gain_a=NF,
        down_bias_a=NF,
        down_one_b=MID,
        down_time_b=MID,
        down_gain_b=MID,
        down_bias_b=MID,
        down_two_b=MID,
        down_skip_b=MID,
        attn_gain=MID,
        attn_bias=MID,
        query_b=MID,
        value_b=MID,
        attn_out_b=MID,
        up_gain_a=MID,
        up_bias_a=MID,
        up_one_b=NF,
        up_time_b=NF,
        up_gain_b=NF,
        up_bias_b=NF,
        up_two_b=NF,
        up_skip_b=NF,
        final_gain=2 * NF,
        final_bias=2 * NF,
        conv_out_b=CHAN,
    )


def offsets():
    mats, smalls, used = {}, {}, 0
    for label, shape in mat_layout().items():
        mats[label] = (used // LANES,) + shape
        used += math.prod(shape)
    used = 0
    for label, length in small_layout().items():
        smalls[label] = (used // LANES, length)
        used += length
    return SimpleNamespace(**mats), SimpleNamespace(**smalls)


MATS, SMALLS = offsets()
WEIGHTS = list(mat_layout())
WEIGHT_SHAPES = mat_layout() | dict(conv_in=(LANES, NF), pyramid=(LANES, MID), conv_out=(LANES, 2 * NF))
RING = 8
TAPS = [(dy, dx) for dy in range(3) for dx in range(3)]


def pixel_order(side):
    across, down = side // 8, side // 2
    order = np.empty((across, down, 2, 8), np.int32)
    for xl in range(across):
        for yl in range(down):
            for yh in range(2):
                for xh in range(8):
                    order[xl, yl, yh, xh] = (yh * down + yl) * side + xh * across + xl
    return order.reshape(-1)


def fir_matrix():
    rows = np.arange(IMG // 2)[:, None]
    cols = np.arange(IMG)[None, :]
    offset = cols - 2 * rows + 1
    taps = np.where((offset == 0) | (offset == 3), 1.0, 0.0) + np.where(
        (offset == 1) | (offset == 2), 3.0, 0.0
    )
    both = np.kron(taps / 8.0, taps / 8.0)
    return both[pixel_order(IMG // 2)][:, pixel_order(IMG)].astype(np.float32)


def dot(a, b):
    return lax.dot_general(a, b, (((1,), (0,)), ((), ())), preferred_element_type=F32)


def dot_nt(a, b):
    return lax.dot_general(a, b, (((1,), (1,)), ((), ())), preferred_element_type=F32)


def dot_tn(a, b):
    return lax.dot_general(a, b, (((0,), (0,)), ((), ())), preferred_element_type=F32)


def two(value):
    high = value.astype(BF16)
    return high, (value - high.astype(F32)).astype(BF16)


def sigmoid(value):
    return 1.0 / (1.0 + jnp.exp(-value))


def rowsum(value):
    return jnp.sum(value, axis=0, keepdims=True)


def group_sums(rows, width):
    chans = rows[0].shape[1]
    at = lax.broadcasted_iota(jnp.int32, (16, chans), 0)
    stack = jnp.zeros((16, chans), F32)
    for n, row in enumerate(rows):
        rest = row
        for part in range(3):
            piece = rest.astype(BF16).astype(F32)
            stack = jnp.where(at == 3 * n + part, piece, stack)
            rest = rest - piece
    one = lax.broadcasted_iota(jnp.int32, (chans, chans), 0) // width
    other = lax.broadcasted_iota(jnp.int32, (chans, chans), 1) // width
    same = jnp.where(one == other, 1.0, 0.0).astype(BF16)
    sums = dot(stack.astype(BF16), same)
    return [sums[3 * n : 3 * n + 1] + sums[3 * n + 1 : 3 * n + 2] + sums[3 * n + 2 : 3 * n + 3] for n in range(len(rows))]


def norm_stats(value, width):
    count = float(value.shape[0] * width)
    center = group_sums([rowsum(value)], width)[0] / count
    yield
    shifted = value - center
    spread = group_sums([rowsum(shifted * shifted)], width)[0] / count
    yield
    return center, lax.rsqrt(spread + 1e-06)


def norm_back(grad, normed, gain, scale, width):
    count = float(grad.shape[0] * width)
    dbias = rowsum(grad)
    dgain = rowsum(grad * normed)
    first, second = group_sums([dbias * gain, dgain * gain], width)
    yield
    back = scale * (grad * gain - first / count - normed * (second / count))
    return back, dgain, dbias


def swish_back(pre):
    gate = sigmoid(pre)
    return gate * (1.0 + pre * (1.0 - gate))


def small(ref, label):
    at, length = label
    rows = max(1, length // LANES)
    return jnp.concatenate(
        [ref[(at + i) // 2, (at + i) % 2 : (at + i) % 2 + 1, :] for i in range(rows)], axis=1
    ) if rows > 1 else ref[at // 2, at % 2 : at % 2 + 1, :]


def add_small(ref, label, value):
    at, _ = label
    for i in range(value.shape[1] // LANES):
        j = at + i
        ref[j // 2, j % 2 : j % 2 + 1, :] += value[:, i * LANES : (i + 1) * LANES]


def fill_halo(ref, b, across, down):
    chans = ref.shape[-1]
    zero = jnp.zeros((across, 8, chans), F32)
    last = ref[b, 1 : across + 1, down].astype(F32)
    ref[b, 1 : across + 1, 0] = jnp.concatenate([zero, last[:, 0:8]], axis=1).astype(BF16)
    first = ref[b, 1 : across + 1, 1].astype(F32)
    ref[b, 1 : across + 1, down + 1] = jnp.concatenate([first[:, 8:16], zero], axis=1).astype(BF16)
    tiles = (down + 2) * 2
    at = lax.broadcasted_iota(jnp.int32, (tiles, 8, chans), 1)
    side = ref[b, across].astype(F32).reshape(tiles, 8, chans)
    side = jnp.where(at == 0, 0.0, pltpu.roll(side, 1, axis=1))
    ref[b, 0] = side.reshape(down + 2, 16, chans).astype(BF16)
    side = ref[b, 1].astype(F32).reshape(tiles, 8, chans)
    side = jnp.where(at == 7, 0.0, pltpu.roll(side, 7, axis=1))
    ref[b, across + 1] = side.reshape(down + 2, 16, chans).astype(BF16)


def set_inner(ref, b, across, down, value):
    chans = value.shape[1]
    ref[b, 1 : across + 1, 1 : down + 1] = value.astype(BF16).reshape(across, down, 16, chans)
    fill_halo(ref, b, across, down)


def taps_of(ref, b, xl, count, down, flip):
    chans = ref.shape[-1]
    parts = []
    for dy, dx in TAPS:
        y, x = (2 - dy, 2 - dx) if flip else (dy, dx)
        parts.append(ref[b, xl + x : xl + x + count, y : y + down].reshape(count * down * 16, chans))
    return jnp.concatenate(parts, axis=1)


def tap_columns(ref, chans):
    return jnp.concatenate([ref[t * chans : (t + 1) * chans, :] for t in range(9)], axis=1)


def picks(o):
    row = lax.broadcasted_iota(jnp.int32, (6 * LANES, 2 * NF), 0)
    col = lax.broadcasted_iota(jnp.int32, (6 * LANES, 2 * NF), 1)
    return jnp.where(row == CHAN * col + o, 1.0, 0.0).astype(BF16)


SAVED = dict(
    xin=((PIX, LANES), BF16),
    tiny=((HALF, LANES), BF16),
    h0=((PIX, NF), F32),
    ed1=((4, 10, 16, NF), BF16),
    sk0=((HALF, NF), BF16),
    a1=((HALF, MID), F32),
    ed2=((4, 10, 16, MID), BF16),
    h1=((HALF, MID), F32),
    g=((HALF, MID), BF16),
    qkv=((HALF, 3 * MID), BF16),
    prob=((HALF, HALF), BF16),
    mixed=((HALF, MID), BF16),
    h2=((HALF, MID), F32),
    eu1=((6, 18, 16, MID), BF16),
    sku=((PIX, MID), BF16),
    b1=((PIX, NF), F32),
    eu2=((6, 18, 16, NF), BF16),
    h3=((PIX, NF), F32),
    final=((PIX, 2 * NF), BF16),
    stats=((16, MID), F32),
)
EARLY = list(dict(sm=0, xin=0, tiny=0, h0=0, ed1=0, sk0=0, a1=0, ed2=0, h1=0, g=0, qkv=0, prob=0, mixed=0, h2=0))
TIME_SAVED = dict(
    t1=((8, TEMB), F32),
    s1=((8, TEMB), BF16),
    t2=((8, TEMB), F32),
    tact=((8, TEMB), BF16),
)


def in_step(parts):
    for _ in zip(*parts, strict=True):
        pass


def forward_kernel(piece_marks, slots, names, sent, *refs):
    r_pieces, refs = refs[: len(piece_marks)], refs[len(piece_marks) :]
    r = SimpleNamespace(**dict(zip(names, refs)))
    me = r.me[0]
    copies = []
    early = [name for name in sent if name[:2] == "w_" or name in TIME_SAVED or name in EARLY]

    def send(names):
        for name in names:
            source, target = getattr(r, name), getattr(r, "out_" + name)
            copies.append(pltpu.make_async_copy(source, target, r.sems.at[len(copies)]))
            copies[-1].start()

    stage, sm = r.stage, r.sm
    for n, (marks, first) in enumerate(piece_marks):
        for i, mark in enumerate(marks):
            home = jnp.bitwise_xor(me, mark)
            block = r_pieces[n][i].astype(F32)
            rows = min(block.shape[0], ROWS - first)
            stage[pl.ds(pl.multiple_of(home * ROWS + first, 8), rows), :] = block[:rows]
            if rows < block.shape[0]:
                sm[home] = block[rows:]
    for label in WEIGHTS:
        at, depth, width = getattr(MATS, label)
        out = getattr(r, "w_" + label)
        if width == CHAN:
            flat = jnp.concatenate([stage[pl.ds(at + i, 9, stride=6), :] for i in range(6)], axis=1).astype(BF16)
            out[...] = jnp.zeros(out.shape, BF16)
            pad = jnp.zeros((7, 2 * NF), F32)
            for o in range(CHAN):
                out[16 * o : 16 * o + 16, :] = jnp.concatenate([dot(flat, picks(o)), pad], axis=0).astype(BF16)
            continue
        if depth == 9 * CHAN:
            out[...] = jnp.zeros(out.shape, BF16)
            pad = jnp.zeros((7, NF), F32)
            for c in range(CHAN):
                part = stage[pl.ds(at + c, 9, stride=CHAN), :]
                out[16 * c : 16 * c + 16, :] = jnp.concatenate([part, pad], axis=0).astype(BF16)
            continue
        if depth == CHAN:
            out[...] = jnp.zeros(out.shape, BF16)
            pad = jnp.zeros((15, LANES), F32)
            for j in range(2):
                part = stage[pl.ds(at + j, CHAN, stride=2), :]
                for c in range(CHAN):
                    row = jnp.concatenate([part[c : c + 1], pad], axis=0)
                    out[16 * c : 16 * c + 16, j * LANES : (j + 1) * LANES] = row.astype(BF16)
            continue
        pad = out.shape[0] - depth
        for j in range(width // LANES):
            part = stage[pl.ds(at + j, depth, stride=width // LANES), :] if width > LANES else stage[pl.ds(at, depth), :]
            if pad:
                part = jnp.concatenate([part, jnp.zeros((pad, LANES), F32)], axis=0)
            out[:, j * LANES : (j + 1) * LANES] = part.astype(BF16)

    t1 = dot(r.feats[...], r.w_temb_one[...]) + small(sm, SMALLS.temb_one_b)
    r.t1[...] = t1
    s1 = (t1 * sigmoid(t1)).astype(BF16)
    r.s1[...] = s1
    t2 = dot(s1, r.w_temb_two[...]) + small(sm, SMALLS.temb_two_b)
    r.t2[...] = t2
    tact = (t2 * sigmoid(t2)).astype(BF16)
    r.tact[...] = tact
    r.pd[...] = dot(tact, r.w_down_time[...]) + (small(sm, SMALLS.down_time_b) + small(sm, SMALLS.down_one_b))
    r.pu[...] = dot(tact, r.w_up_time[...]) + (small(sm, SMALLS.up_time_b) + small(sm, SMALLS.up_one_b))

    def image(b):
        stats = r.stats

        def normed(value, width, gain, bias, at):
            center, scale = yield from norm_stats(value, width)
            chans = value.shape[1]
            stats[b, 2 * at : 2 * at + 1, :chans] = center
            stats[b, 2 * at + 1 : 2 * at + 2, :chans] = scale
            return (value - center) * (scale * gain) + bias

        high, rest = (spread(r, part) for part in two(r.images[b] + r.sigma[b] * r.noise[b]))
        r.tiny[b] = (dot(r.shrink[...], high.astype(BF16)) + dot(r.shrink[...], rest.astype(BF16))).astype(BF16)
        field = r.field.at[b]
        set_field(field, high)
        r.xin[b] = tap_lanes(field, False).astype(BF16)
        yield
        h0 = dot(r.xin[b], r.w_conv_in[...]) + small(sm, SMALLS.conv_in_b)
        r.h0[b] = h0
        yield
        y = (yield from normed(h0, 4, small(sm, SMALLS.down_gain_a), small(sm, SMALLS.down_bias_a), 0))
        y = y * sigmoid(y)
        yield
        down = dot(r.shrink[...], jnp.concatenate([*two(y), *two(h0)], axis=1))
        set_inner(r.ed1, b, 2, 8, down[:, :NF] + down[:, NF : 2 * NF])
        sk0 = (down[:, 2 * NF : 3 * NF] + down[:, 3 * NF :]).astype(BF16)
        r.sk0[b] = sk0
        yield
        a1 = dot(taps_of(r.ed1, b, 0, 2, 8, False), r.w_down_one[...]) + r.pd[pl.ds(b, 1), :]
        r.a1[b] = a1
        yield
        y = (yield from normed(a1, 8, small(sm, SMALLS.down_gain_b), small(sm, SMALLS.down_bias_b), 1))
        set_inner(r.ed2, b, 2, 8, y * sigmoid(y))
        yield
        a2 = dot(taps_of(r.ed2, b, 0, 2, 8, False), r.w_down_two[...]) + dot(sk0, r.w_down_skip[...])
        a2 = (a2 + (small(sm, SMALLS.down_two_b) + small(sm, SMALLS.down_skip_b))) * INV_ROOT
        h1 = (a2 + dot(r.tiny[b], r.w_pyramid[...]) + small(sm, SMALLS.pyramid_b)) * INV_ROOT
        r.h1[b] = h1
        yield
        g = (yield from normed(h1, 8, small(sm, SMALLS.attn_gain), small(sm, SMALLS.attn_bias), 2)).astype(BF16)
        r.g[b] = g
        yield
        proj = dot(g, r.w_attn_qkv[...])
        q = (proj[:, :MID] + small(sm, SMALLS.query_b)).astype(BF16)
        k = proj[:, MID : 2 * MID].astype(BF16)
        v = (proj[:, 2 * MID :] + small(sm, SMALLS.value_b)).astype(BF16)
        r.qkv[b] = jnp.concatenate([q, k, v], axis=1)
        yield
        scores = dot_nt(q, k) * (MID**-0.5)
        yield
        weight = jnp.exp(scores - jnp.max(scores, axis=1, keepdims=True))
        prob = (weight / jnp.sum(weight, axis=1, keepdims=True)).astype(BF16)
        r.prob[b] = prob
        yield
        mixed = dot(prob, v).astype(BF16)
        r.mixed[b] = mixed
        yield
        h2 = (h1 + dot(mixed, r.w_attn_out[...]) + small(sm, SMALLS.attn_out_b)) * INV_ROOT
        r.h2[b] = h2
        yield
        if b == 0:
            send(early)
        y = (yield from normed(h2, 8, small(sm, SMALLS.up_gain_a), small(sm, SMALLS.up_bias_a), 3))
        y = y * sigmoid(y)
        coarse = jnp.concatenate([*two(y), *two(h2)], axis=1)
        yield
        for xl in range(4):
            fine = dot(r.grow[xl * 256 : (xl + 1) * 256, :], coarse)
            part = (fine[:, :MID] + fine[:, MID : 2 * MID]).astype(BF16)
            r.eu1[b, xl + 1, 1:17] = part.reshape(16, 16, MID)
            r.sku[b, xl * 256 : (xl + 1) * 256, :] = (fine[:, 2 * MID : 3 * MID] + fine[:, 3 * MID :]).astype(BF16)
        fill_halo(r.eu1, b, 4, 16)
        yield
        for xl in range(4):
            r.b1[b, xl * 256 : (xl + 1) * 256, :] = (
                dot(taps_of(r.eu1, b, xl, 1, 16, False), r.w_up_one[...]) + r.pu[pl.ds(b, 1), :]
            )
            yield
        yield
        y = (yield from normed(r.b1[b], 4, small(sm, SMALLS.up_gain_b), small(sm, SMALLS.up_bias_b), 4))
        set_inner(r.eu2, b, 4, 16, y * sigmoid(y))
        yield
        bias = small(sm, SMALLS.up_two_b) + small(sm, SMALLS.up_skip_b)
        for xl in range(4):
            part = slice(xl * 256, (xl + 1) * 256)
            up = dot(taps_of(r.eu2, b, xl, 1, 16, False), r.w_up_two[...])
            r.h3[b, part, :] = (up + dot(r.sku[b, part, :], r.w_up_skip[...]) + bias) * INV_ROOT
            yield
        yield
        gain, bias = small(sm, SMALLS.final_gain), small(sm, SMALLS.final_bias)
        y = (yield from normed(r.h3[b], 8, gain[:, :NF], bias[:, :NF], 5))
        r.final[b, :, :NF] = (y * sigmoid(y)).astype(BF16)
        yield
        y = (yield from normed(r.h0[b], 8, gain[:, NF:], bias[:, NF:], 6))
        r.final[b, :, NF:] = (y * sigmoid(y)).astype(BF16)
        yield
        wide = dot_nt(r.final[b], r.w_conv_out[...])
        field = r.field.at[b]
        set_field(field, wide)
        total = tap_lanes(field, False)
        high, rest = two(total)
        wide = two((dot(high, r.unfan[...]) + dot(rest, r.unfan[...])) * r.own_x[...])
        err = dot(r.y_rows[...], wide[0]) + dot(r.y_rows[...], wide[1]) + r.out_bias[...] + r.noise[b]
        r.err[b] = err
        r.err16[b] = err.astype(BF16)

    prepare_out_bias(r, sm)
    in_step([image(b) for b in range(slots)])
    send(name for name in sent if name not in early)
    for copy in copies:
        copy.wait()


def prepare_out_bias(r, sm):
    bias = small(sm, SMALLS.conv_out_b)
    total = jnp.zeros((1, IMG * CHAN), F32)
    for c in range(CHAN):
        total += bias[:, c : c + 1] * r.colours[c : c + 1, :]
    r.out_bias[...] = jnp.broadcast_to(total, (IMG, IMG * CHAN))


def spread(r, value):
    wide = dot(r.y_of[...], value) * r.own_x[...]
    return dot(wide.astype(BF16), r.fan[...])


def pixel_maps():
    order = pixel_order(IMG)
    column, lane = np.arange(IMG * CHAN), np.arange(LANES)
    y_of = order[:, None] // IMG == np.arange(IMG)
    own_x = order[:, None] % IMG == column // CHAN
    fan = column[:, None] % CHAN == lane // 16
    colours = np.arange(8)[:, None] == column % CHAN
    maps = dict(y_of=y_of, y_rows=y_of.T, fan=fan, unfan=fan.T & (lane % 16 < 9)[:, None])
    maps = {name: value.astype(BF16) for name, value in maps.items()}
    return maps | dict(own_x=own_x.astype(np.float32), colours=colours.astype(np.float32))


def set_field(field, value):
    field[1:5, 1:17] = value.reshape(4, 16, 16, LANES)
    zero = jnp.zeros((4, 8, LANES), F32)
    field[1:5, 0] = jnp.concatenate([zero, field[1:5, 16, 0:8]], axis=1)
    field[1:5, 17] = jnp.concatenate([field[1:5, 1, 8:16], zero], axis=1)
    at = lax.broadcasted_iota(jnp.int32, (36, 8, LANES), 1)
    side = pltpu.roll(field[4].reshape(36, 8, LANES), 1, axis=1)
    field[0] = jnp.where(at == 0, 0.0, side).reshape(18, 16, LANES)
    side = pltpu.roll(field[1].reshape(36, 8, LANES), 7, axis=1)
    field[5] = jnp.where(at == 7, 0.0, side).reshape(18, 16, LANES)


def backward_kernel(slots, names, fetched, *refs):
    r = SimpleNamespace(**dict(zip(names, refs)))
    copies = []
    for n, name in enumerate(fetched):
        copies.append(pltpu.make_async_copy(getattr(r, "in_" + name), getattr(r, name), r.sems.at[n]))
        copies[-1].start()

    def arrive(name):
        while len(copies) > len(fetched) - 1 - fetched.index(name):
            copies.pop(0).wait()

    me = r.me[0]
    sm, stage, gsm = r.sm, r.stage, r.gsm
    stats = r.stats
    total = jnp.sum(sm[...], axis=0)[SMALL_ROWS : SMALL_ROWS + 1, 0:1]
    theirs = sm[jnp.bitwise_xor(me, BLOCKS // 2), SMALL_ROWS : SMALL_ROWS + 1, :]
    gsm[...] = jnp.zeros(gsm.shape, F32)
    r.dpd[...] = jnp.zeros(r.dpd.shape, F32)
    r.dpu[...] = jnp.zeros(r.dpu.shape, F32)
    r.dout_sum[...] = jnp.zeros(r.dout_sum.shape, F32)
    r.loss[...] = jnp.zeros(r.loss.shape, F32)
    counts, pairs = r.ints[0], r.ints
    other_counts = theirs[:, 1:2]

    def put(label, value, first=0):
        at, _, width = label
        step = width // LANES
        for j in range(step):
            part = value[:, j * LANES : (j + 1) * LANES]
            if step == 1:
                stage[pl.ds(at + first, value.shape[0]), :] = part
            else:
                stage[pl.ds(at + first * step + j, value.shape[0], stride=step), :] = part

    def image(b):
        def stat(at, chans):
            return stats[b, 2 * at : 2 * at + 1, :chans], stats[b, 2 * at + 1 : 2 * at + 2, :chans]

        def renorm(value, at, gain, bias):
            center, scale = stat(at, value.shape[1])
            normed = (value - center) * scale
            return normed, normed * gain + bias, scale

        err = r.err[b]
        mine = r.other[pairs[1 + b]].astype(F32)
        gap = err - mine
        live = jnp.where(b < counts, 1.0, 0.0)
        scale = 1.0 / (total * (CHAN * PIX))
        r.loss[...] += (live * scale) * (0.5 * err * err + 0.25 * gap * gap)
        grad = (live * scale) * (err + 0.5 * gap)
        for s in range(slots):
            on = jnp.where((theirs[:, 2 + s : 3 + s] == b) & (s < other_counts), 0.5 * scale, 0.0)
            grad += on * (err - r.other[s].astype(F32))
        yield
        if b == 0:
            arrive(FETCH_ORDER[6])
        r.dout_sum[...] += grad
        field = r.field.at[b]
        set_field(field, spread(r, grad.astype(BF16)))
        cols = tap_lanes(field, True).astype(BF16)
        r.cols[b] = cols
        yield
        gain, bias = small(sm, SMALLS.final_gain), small(sm, SMALLS.final_bias)
        back = dot(cols, r.w_conv_out[...])
        yield
        n3, y3, scale3 = renorm(r.h3[b], 5, gain[:, :NF], bias[:, :NF])
        dh3, dgain, dbias = yield from norm_back(back[:, :NF] * swish_back(y3), n3, gain[:, :NF], scale3, 8)
        n0, y0, scale0 = renorm(r.h0[b], 6, gain[:, NF:], bias[:, NF:])
        dh0, dgain0, dbias0 = yield from norm_back(back[:, NF:] * swish_back(y0), n0, gain[:, NF:], scale0, 8)
        add_small(gsm, SMALLS.final_gain, jnp.concatenate([dgain, dgain0], axis=1))
        add_small(gsm, SMALLS.final_bias, jnp.concatenate([dbias, dbias0], axis=1))
        r.dh0[b] = dh0
        yield
        dh3 = dh3 * INV_ROOT
        add_small(gsm, SMALLS.up_two_b, rowsum(dh3))
        set_inner(r.gu2, b, 4, 16, dh3)
        yield
        turned = tap_columns(r.w_up_two, NF)
        for xl in range(4):
            r.wide[b, xl * 256 : (xl + 1) * 256, :] = dot_nt(taps_of(r.gu2, b, xl, 1, 16, True), turned)
        yield
        gain, bias = small(sm, SMALLS.up_gain_b), small(sm, SMALLS.up_bias_b)
        n, y, scale1 = renorm(r.b1[b], 4, gain, bias)
        db1, dgain, dbias = yield from norm_back(r.wide[b] * swish_back(y), n, gain, scale1, 4)
        add_small(gsm, SMALLS.up_gain_b, dgain)
        add_small(gsm, SMALLS.up_bias_b, dbias)
        r.dpu[pl.ds(b, 1), :] = rowsum(db1)
        set_inner(r.gu1, b, 4, 16, db1)
        yield
        turned = tap_columns(r.w_up_one, MID)
        half = jnp.zeros((HALF, 2 * MID), F32)
        for xl in range(4):
            branch = dot_nt(taps_of(r.gu1, b, xl, 1, 16, True), turned)
            skip = dot_nt(r.gu2[b, xl + 1, 1:17].reshape(256, NF), r.w_up_skip[...])
            both = jnp.concatenate([branch.astype(BF16), skip.astype(BF16)], axis=1)
            half += dot(r.shrink[:, xl * 256 : (xl + 1) * 256], both)
        half = half * 4.0
        yield
        if b == 0:
            arrive(FETCH_ORDER[-1])
            arrive(fetched[-1])
        gain, bias = small(sm, SMALLS.up_gain_a), small(sm, SMALLS.up_bias_a)
        n, y, scale2 = renorm(r.h2[b], 3, gain, bias)
        dh2, dgain, dbias = yield from norm_back(half[:, :MID] * swish_back(y), n, gain, scale2, 8)
        add_small(gsm, SMALLS.up_gain_a, dgain)
        add_small(gsm, SMALLS.up_bias_a, dbias)
        dh2 = (dh2 + half[:, MID:]) * INV_ROOT
        add_small(gsm, SMALLS.attn_out_b, rowsum(dh2))
        datt = dh2.astype(BF16)
        r.datt[b] = datt
        yield
        dmixed = dot_nt(datt, r.w_attn_out[...]).astype(BF16)
        q, k, v = r.qkv[b, :, :MID], r.qkv[b, :, MID : 2 * MID], r.qkv[b, :, 2 * MID :]
        prob = r.prob[b]
        dprob = dot_nt(dmixed, v)
        yield
        dv = dot_tn(prob, dmixed)
        yield
        wide = prob.astype(F32)
        dscore = wide * (dprob - jnp.sum(wide * dprob, axis=1, keepdims=True))
        dscore = (dscore * (MID**-0.5)).astype(BF16)
        yield
        dq = dot(dscore, k)
        dk = dot_tn(dscore, q)
        add_small(gsm, SMALLS.query_b, rowsum(dq))
        add_small(gsm, SMALLS.value_b, rowsum(dv))
        dqkv = jnp.concatenate([dq, dk, dv], axis=1).astype(BF16)
        r.dqkv[b] = dqkv
        yield
        dg = dot_nt(dqkv, r.w_attn_qkv[...])
        yield
        gain, bias = small(sm, SMALLS.attn_gain), small(sm, SMALLS.attn_bias)
        n, _, scale2 = renorm(r.h1[b], 2, gain, bias)
        dh1, dgain, dbias = yield from norm_back(dg, n, gain, scale2, 8)
        add_small(gsm, SMALLS.attn_gain, dgain)
        add_small(gsm, SMALLS.attn_bias, dbias)
        dh1 = (dh1 + dh2) * INV_ROOT
        r.dpyr[b] = dh1.astype(BF16)
        add_small(gsm, SMALLS.pyramid_b, rowsum(dh1))
        da2 = dh1 * INV_ROOT
        add_small(gsm, SMALLS.down_two_b, rowsum(da2))
        set_inner(r.gd2, b, 2, 8, da2)
        yield
        dsk0 = dot_nt(r.gd2[b, 1:3, 1:9].reshape(HALF, MID), r.w_down_skip[...])
        turned = tap_columns(r.w_down_two, MID)
        du = dot_nt(taps_of(r.gd2, b, 0, 2, 8, True), turned)
        yield
        gain, bias = small(sm, SMALLS.down_gain_b), small(sm, SMALLS.down_bias_b)
        n, y, scale2 = renorm(r.a1[b], 1, gain, bias)
        da1, dgain, dbias = yield from norm_back(du * swish_back(y), n, gain, scale2, 8)
        add_small(gsm, SMALLS.down_gain_b, dgain)
        add_small(gsm, SMALLS.down_bias_b, dbias)
        r.dpd[pl.ds(b, 1), :] = rowsum(da1)
        set_inner(r.gd1, b, 2, 8, da1)
        yield
        turned = tap_columns(r.w_down_one, NF)
        dd0 = dot_nt(taps_of(r.gd1, b, 0, 2, 8, True), turned)
        both = jnp.concatenate([dd0, dsk0], axis=1).astype(BF16)
        fine = dot(r.grow[...], both) * 0.25
        yield
        gain, bias = small(sm, SMALLS.down_gain_a), small(sm, SMALLS.down_bias_a)
        n, y, scale1 = renorm(r.h0[b], 0, gain, bias)
        back0, dgain, dbias = yield from norm_back(fine[:, :NF] * swish_back(y), n, gain, scale1, 4)
        add_small(gsm, SMALLS.down_gain_a, dgain)
        add_small(gsm, SMALLS.down_bias_a, dbias)
        dh0 = r.dh0[b] + back0 + fine[:, NF:]
        add_small(gsm, SMALLS.conv_in_b, rowsum(dh0))
        r.din[b] = dh0.astype(BF16)

    in_step([image(b) for b in range(slots)])

    whole = slots * PIX
    fewer = slots * HALF
    def conv_grad(label, acts, grads, across, down):
        chans, rows = acts.shape[-1], slots * across * down * 16
        left = acts[:, 1 : across + 1, 1 : down + 1].reshape(rows, chans)
        out = grads.shape[-1]
        right = jnp.concatenate(
            [grads[:, 2 - dx : 2 - dx + across, 2 - dy : 2 - dy + down].reshape(rows, out) for dy, dx in TAPS], axis=1
        )
        back = dot_tn(left, right)
        for t in range(9):
            put(label, back[:, t * out : (t + 1) * out], t * chans)

    dpd, dpu = r.dpd[...], r.dpu[...]
    for label in (SMALLS.down_time_b, SMALLS.down_one_b):
        add_small(gsm, label, rowsum(dpd))
    for label in (SMALLS.up_time_b, SMALLS.up_one_b):
        add_small(gsm, label, rowsum(dpu))
    dpd16, dpu16 = dpd.astype(BF16), dpu.astype(BF16)
    put(MATS.down_time, dot_tn(r.tact[...], dpd16))
    put(MATS.up_time, dot_tn(r.tact[...], dpu16))
    dtact = dot_nt(dpd16, r.w_down_time[...]) + dot_nt(dpu16, r.w_up_time[...])
    dt2 = dtact * swish_back(r.t2[...])
    add_small(gsm, SMALLS.temb_two_b, rowsum(dt2))
    put(MATS.temb_two, dot_tn(r.s1[...], dt2.astype(BF16)))
    dt1 = dot_nt(dt2.astype(BF16), r.w_temb_two[...]) * swish_back(r.t1[...])
    add_small(gsm, SMALLS.temb_one_b, rowsum(dt1))
    put(MATS.temb_one, dot_tn(r.feats[...], dt1.astype(BF16)))
    for label, twin in ((SMALLS.up_skip_b, SMALLS.up_two_b), (SMALLS.down_skip_b, SMALLS.down_two_b)):
        value = small(gsm, twin)
        add_small(gsm, label, value)
    sums = rowsum(r.dout_sum[...])
    lane = lax.broadcasted_iota(jnp.int32, (1, LANES), 1)
    total_bias = jnp.zeros((1, LANES), F32)
    for c in range(CHAN):
        own = jnp.sum(sums * r.colours[c : c + 1, :], axis=1, keepdims=True)
        total_bias += jnp.where(lane == c, own, 0.0)
    add_small(gsm, SMALLS.conv_out_b, total_bias)
    dout = dot_tn(r.cols[...].reshape(whole, LANES), r.final[...].reshape(whole, 2 * NF))
    flat = jnp.zeros((16, 6 * LANES), F32)
    for o in range(CHAN):
        flat += dot_nt(dout[16 * o : 16 * o + 16].astype(BF16), picks(o))
    at = MATS.conv_out[0]
    for i in range(6):
        for t in range(9):
            stage[at + 6 * t + i : at + 6 * t + i + 1, :] = flat[t : t + 1, i * LANES : (i + 1) * LANES]

    last = MATS.conv_out[0] + 54
    stage[last : BLOCKS * ROWS, :] = jnp.zeros((BLOCKS * ROWS - last, LANES), F32)
    put(MATS.up_skip, dot_tn(r.sku[...].reshape(whole, MID), r.gu2[:, 1:5, 1:17].reshape(whole, NF)))
    conv_grad(MATS.up_two, r.eu2, r.gu2, 4, 16)
    conv_grad(MATS.up_one, r.eu1, r.gu1, 4, 16)
    put(MATS.attn_out, dot_tn(r.mixed[...].reshape(fewer, MID), r.datt[...].reshape(fewer, MID)))
    put(MATS.attn_qkv, dot_tn(r.g[...].reshape(fewer, MID), r.dqkv[...].reshape(fewer, 3 * MID)))
    put(MATS.down_skip, dot_tn(r.sk0[...].reshape(fewer, NF), r.gd2[:, 1:3, 1:9].reshape(fewer, MID)))
    conv_grad(MATS.down_two, r.ed2, r.gd2, 2, 8)
    conv_grad(MATS.down_one, r.ed1, r.gd1, 2, 8)
    back = dot_tn(r.tiny[...].reshape(fewer, LANES), r.dpyr[...].reshape(fewer, MID))
    put(MATS.pyramid, jnp.concatenate([back[16 * c : 16 * c + 1] for c in range(CHAN)], axis=0))
    back = dot_tn(r.xin[...].reshape(whole, LANES), r.din[...].reshape(whole, NF))
    for c in range(CHAN):
        stage[pl.ds(MATS.conv_in[0] + c, 9, stride=CHAN), :] = back[16 * c : 16 * c + 9]
    ring, sems = r.ring, r.ring_sems

    class sending:
        def __init__(self, upper, lower, d, slot):
            place = block_place(jnp.bitwise_xor(d, me))
            self.copies = [
                pltpu.make_async_copy(ring.at[slot, :CUT], upper.at[place], sems.at[0, slot]),
                pltpu.make_async_copy(ring.at[slot, CUT:], lower.at[place], sems.at[1, slot]),
            ]

        def start(self):
            for copy in self.copies:
                copy.start()

        def wait(self):
            for copy in self.copies:
                copy.wait()

    def give(d, carry):
        slot = d % RING

        @pl.when(d >= RING)
        def _():
            sending(r.stay, r.stay_low, d, slot).wait()

        block = jnp.concatenate([stage[pl.ds(pl.multiple_of(d * ROWS, 8), ROWS), :], gsm[d]], axis=0)
        ring[slot] = block.astype(BF16)
        goes = jnp.bitwise_xor(d, me) % 2 == 1

        @pl.when(goes)
        def _():
            sending(r.leave, r.leave_low, d, slot).start()

        @pl.when(jnp.logical_not(goes))
        def _():
            sending(r.stay, r.stay_low, d, slot).start()

        return carry

    lax.fori_loop(0, BLOCKS, give, 0)
    for d in range(BLOCKS - RING, BLOCKS):
        sending(r.stay, r.stay_low, d, d % RING).wait()


def tap_lanes(field, flip):
    lane = lax.broadcasted_iota(jnp.int32, (PIX, LANES), 1) % 16
    total = jnp.zeros((PIX, LANES), F32)
    for t, (dy, dx) in enumerate(TAPS):
        y, x = (2 - dy, 2 - dx) if flip else (dy, dx)
        total = jnp.where(lane == t, field[x : x + 4, y : y + 16].reshape(PIX, LANES), total)
    return total


def block_place(mark):
    low, high, x, y = (mark // 2) % 2, (mark // 4) % 2, (mark // 8) % 2, mark // 16
    return high * 8 + (4 * y + 2 * x + high * 2 * (x - y)) + low


def vmem():
    return pl.BlockSpec(memory_space=pltpu.VMEM)


def anywhere():
    return pl.BlockSpec(memory_space=pl.ANY)


def smem():
    return pl.BlockSpec(memory_space=pltpu.SMEM)


LIMIT = 60 * 1024 * 1024


def run_forward(me, sigma, pieces, marks, data):
    slots = data.images.shape[0]
    ins = dict(me=me, sigma=sigma) | vars(data)
    outs = {"w_" + label: (WEIGHT_SHAPES[label], BF16) for label in WEIGHTS}
    outs |= dict(sm=((BLOCKS, 8, LANES), F32)) | TIME_SAVED
    outs |= {label: ((slots,) + shape, dtype) for label, (shape, dtype) in SAVED.items()}
    outs |= dict(err=((slots, IMG, IMG * CHAN), F32), err16=((slots, IMG, IMG * CHAN), BF16))
    scratch = dict(
        stage=((BLOCKS * ROWS, LANES), F32),
        pd=((8, MID), F32),
        pu=((8, NF), F32),
        out_bias=((IMG, IMG * CHAN), F32),
        field=((slots, 6, 18, 16, LANES), F32),
    )
    names = list(ins) + ["out_" + label for label in outs] + list(outs) + list(scratch) + ["sems"]
    results = pl.pallas_call(
        functools.partial(forward_kernel, marks, slots, names, list(outs)),
        out_shape=[jax.ShapeDtypeStruct(*v) for v in outs.values()],
        in_specs=[vmem()] * len(pieces) + [smem()] * 2 + [vmem()] * (len(ins) - 2),
        out_specs=[anywhere()] * len(outs),
        scratch_shapes=[pltpu.VMEM(*v) for v in (outs | scratch).values()] + [pltpu.SemaphoreType.DMA((len(outs),))],
        compiler_params=pltpu.CompilerParams(vmem_limit_bytes=LIMIT),
        name="forward",
    )(*pieces, *ins.values())
    return SimpleNamespace(**dict(zip(outs, results)))


FETCH_ORDER = list(
    dict(
        w_conv_out=0,
        h3=0,
        h0=0,
        w_up_two=0,
        b1=0,
        w_up_skip=0,
        w_up_one=0,
        h2=0,
        w_attn_out=0,
        qkv=0,
        prob=0,
        w_attn_qkv=0,
        h1=0,
        w_down_skip=0,
        w_down_two=0,
        a1=0,
        w_down_one=0,
        w_down_time=0,
        w_up_time=0,
        t2=0,
        s1=0,
        w_temb_two=0,
        t1=0,
        tact=0,
        final=0,
        sku=0,
        eu2=0,
        eu1=0,
        mixed=0,
        g=0,
        sk0=0,
        ed2=0,
        ed1=0,
        xin=0,
        tiny=0,
    )
)


def run_backward(me, ints, other, kept, data):
    slots = other.shape[0]
    ins = dict(me=me, ints=ints)
    scalars = len(ins)
    ins |= dict(other=other, err=kept.err, sm=kept.sm, stats=kept.stats)
    ins |= dict(y_of=data.y_of, own_x=data.own_x, fan=data.fan, colours=data.colours)
    direct = len(ins)
    fetched = dict(shrink=data.shrink)
    fetched |= {name: getattr(kept, name) for name in FETCH_ORDER}
    fetched |= dict(grow=data.grow, feats=data.feats)
    ins |= {"in_" + name: value for name, value in fetched.items()}
    upper = ((BLOCKS // 2, CUT, LANES), BF16)
    lower = ((BLOCKS // 2, BLOCK - CUT, LANES), BF16)
    outs = dict(stay=upper, stay_low=lower, leave=upper, leave_low=lower, loss=((IMG, IMG * CHAN), F32))
    scratch = {name: (value.shape, value.dtype) for name, value in fetched.items()}
    scratch |= dict(
        stage=((BLOCKS * ROWS, LANES), F32),
        gsm=((BLOCKS, 8, LANES), F32),
        ring=((RING, BLOCK, LANES), BF16),
        dpd=((8, MID), F32),
        dpu=((8, NF), F32),
        dout_sum=((IMG, IMG * CHAN), F32),
        field=((slots, 6, 18, 16, LANES), F32),
        cols=((slots, PIX, LANES), BF16),
        gu2=((slots, 6, 18, 16, NF), BF16),
        gu1=((slots, 6, 18, 16, NF), BF16),
        gd2=((slots, 4, 10, 16, MID), BF16),
        gd1=((slots, 4, 10, 16, MID), BF16),
        wide=((slots, PIX, NF), F32),
        dh0=((slots, PIX, NF), F32),
        din=((slots, PIX, NF), BF16),
        datt=((slots, HALF, MID), BF16),
        dqkv=((slots, HALF, 3 * MID), BF16),
        dpyr=((slots, HALF, MID), BF16),
    )
    names = list(ins) + list(outs) + list(scratch) + ["sems", "ring_sems"]
    results = pl.pallas_call(
        functools.partial(backward_kernel, slots, names, list(fetched)),
        out_shape=[jax.ShapeDtypeStruct(*v) for v in outs.values()],
        in_specs=[smem()] * scalars + [vmem()] * (direct - scalars) + [anywhere()] * (len(ins) - direct),
        out_specs=[anywhere()] * 4 + [vmem()],
        scratch_shapes=[pltpu.VMEM(*v) for v in scratch.values()]
        + [pltpu.SemaphoreType.DMA((len(fetched),)), pltpu.SemaphoreType.DMA((2, RING))],
        compiler_params=pltpu.CompilerParams(vmem_limit_bytes=LIMIT),
        name="backward",
    )(*ins.values())
    return SimpleNamespace(**dict(zip(outs, results)))


def swap(value, axis, mask):
    size = lax.axis_size(axis)
    return lax.ppermute(value, axis, [(i, i ^ mask) for i in range(size)])


def sum_everywhere(value):
    count = lax.axis_size(WIDE) * lax.axis_size(NARROW)
    rows = lax.all_to_all(jnp.broadcast_to(value, (count, LANES)), AXES, 0, 0, tiled=True)
    return jnp.sum(rows, axis=0, keepdims=True)


def notes(live, ints):
    return jnp.pad(jnp.concatenate([live, ints]).astype(F32), (0, LANES - 1 - ints.shape[0]))[None]


def gather_all(params, smalls, ints, meanwhile):
    if lax.axis_size(WIDE) == 4 and lax.axis_size(NARROW) == 8:
        rows = params.reshape(ROWS, LANES)
        tail = jnp.pad(notes(ints[:1], ints), ((0, BLOCK - ROWS - SMALL_ROWS - 1), (0, 0)))
        tail = jnp.concatenate([rows[CUT:], smalls.reshape(SMALL_ROWS, LANES), tail])
        owns = [rows[:CUT].astype(BF16)[None], tail.astype(BF16)[None]]
        near, side, far = [], [], []
        for own in owns:
            z1, z2, z3 = (swap(own, NARROW, m) for m in (2, 4, 6))
            near.append((jnp.concatenate([own, z1]), jnp.concatenate([z2, z3])))
        near[0], first = lax.optimization_barrier((near[0], meanwhile[:2]))
        for a, b in near:
            side.append((swap(a, WIDE, 1), swap(b, WIDE, 2)))
        side[0], second = lax.optimization_barrier((side[0], meanwhile[2:]))
        for (a, b), (ax, by) in zip(near, side):
            far.append((swap(jnp.concatenate([a, ax]), WIDE, 2), swap(jnp.concatenate([b, by]), WIDE, 1)))
        pieces, marks = [], []
        for part in range(2):
            arrays = [jnp.concatenate(near[part]), jnp.concatenate(side[part]), *far[part]]
            lists = [[0, 2, 4, 6], [8, 10, 20, 22], [16, 18, 24, 26], [12, 14, 28, 30]]
            pieces += arrays + [swap(array, NARROW, 1) for array in arrays]
            marks += [(at, part * CUT) for at in lists] + [([m + 1 for m in at], part * CUT) for at in lists]
        return pieces, marks, True, first + second
    whole = lax.all_gather(params.astype(BF16), AXES, axis=0, tiled=True).reshape(BLOCKS, ROWS, LANES)
    little = lax.all_gather(smalls.astype(BF16), AXES, axis=0, tiled=True).reshape(BLOCKS, SMALL_ROWS, LANES)
    live = lax.all_gather(ints[:1], AXES, axis=0, tiled=True).reshape(BLOCKS, -1).sum(axis=1)
    others = swap(ints, WIDE, lax.axis_size(WIDE) // 2)
    extra = jnp.stack([notes(live[d : d + 1], others) for d in range(BLOCKS)])
    extra = jnp.pad(extra, ((0, 0), (0, BLOCK - ROWS - SMALL_ROWS - 1), (0, 0))).astype(BF16)
    return [jnp.concatenate([whole, little, extra], axis=1)], [(list(range(BLOCKS)), 0)], False, meanwhile


def scatter_sums(stay, leave, relative):
    if relative:

        def join(kept, received):
            return (kept.astype(F32) + received.astype(F32)).astype(BF16)

        parts = [join(a, swap(b, NARROW, 1)) for a, b in zip(stay, leave)]
        parts = [part.reshape((2, 2, BLOCKS // 8) + part.shape[1:]) for part in parts]
        parts = [(join(a[0], swap(a[1], WIDE, 2)), join(b[0], swap(b[1], WIDE, 1))) for a, b in parts]
        parts = [(join(a[:2], swap(a[2:], WIDE, 1)), join(b[:2], swap(b[2:], WIDE, 2))) for a, b in parts]
        done = []
        for a, b in parts:
            own = a[0].astype(F32)
            for value, mask in ((a[1], 2), (b[0], 4), (b[1], 6)):
                own = own + swap(value, NARROW, mask).astype(F32)
            done.append(own)
        own = jnp.concatenate(done)
        return own[:ROWS].reshape(-1), own[ROWS : ROWS + SMALL_ROWS].reshape(-1)
    stay, leave = jnp.concatenate(stay, axis=1), jnp.concatenate(leave, axis=1)
    grads = jnp.stack([(leave if d % 2 else stay)[block_place(d)] for d in range(BLOCKS)])
    large = grads[:, :ROWS].reshape(-1).astype(F32)
    little = grads[:, ROWS : ROWS + SMALL_ROWS].reshape(-1).astype(F32)
    return (
        lax.psum_scatter(large, AXES, scatter_dimension=0, tiled=True),
        lax.psum_scatter(little, AXES, scatter_dimension=0, tiled=True),
    )


def adamw(weight, moment, second, grad, rate):
    moment_new = 0.5 * moment + 0.5 * grad
    second_new = 0.99 * second + 0.01 * grad * grad
    direction = moment_new / (1.0 - 0.5**STEP) / (jnp.sqrt(second_new / (1.0 - 0.99**STEP)) + 1e-08)
    return (weight - rate * (direction + 0.01 * weight), moment_new, second_new)


def body(
    params,
    first_moment,
    second_moment,
    smalls,
    small_first,
    small_second,
    images,
    noise,
    sigma,
    freq,
    counts,
    partner,
):
    slots = images.shape[0]
    ints = jnp.concatenate([counts, partner[0]]).astype(jnp.int32)
    shrink = fir_matrix()
    phase = jnp.log(sigma)[:, None] * freq[None, :] * (2.0 * math.pi)
    feats = jnp.concatenate([jnp.sin(phase), jnp.cos(phase)], axis=-1)
    feats = jnp.pad(feats.astype(BF16), ((0, 8 - slots), (0, 0)))
    own = (feats, images.reshape(slots, IMG, IMG * CHAN), noise.reshape(slots, IMG, IMG * CHAN))
    pieces, marks, relative, own = gather_all(params, smalls, ints, own)
    index = lax.axis_index(WIDE) * lax.axis_size(NARROW) + lax.axis_index(NARROW)
    me = (index if relative else jnp.zeros_like(index)).astype(jnp.int32)[None]
    data = SimpleNamespace(
        feats=own[0],
        images=own[1],
        noise=own[2],
        shrink=jnp.asarray(shrink, BF16),
        grow=jnp.asarray(4.0 * shrink.T, BF16),
        **{name: jnp.asarray(value) for name, value in pixel_maps().items()},
    )
    kept = run_forward(me, sigma, pieces, marks, data)
    other = swap(kept.err16, WIDE, lax.axis_size(WIDE) // 2)
    done = run_backward(me, ints, other, kept, data)
    grad_params, grad_smalls = scatter_sums((done.stay, done.stay_low), (done.leave, done.leave_low), relative)
    squares = jnp.sum(grad_params * grad_params) + jnp.sum(grad_smalls * grad_smalls)
    lane = lax.broadcasted_iota(jnp.int32, (1, LANES), 1)
    both = sum_everywhere(jnp.where(lane == 0, squares, jnp.where(lane == 1, jnp.sum(done.loss), 0.0)))
    loss, grad_norm = both[0, 1], jnp.sqrt(both[0, 0])
    factor = jnp.minimum(1.0, 0.01 / (grad_norm + 1e-06))
    small_grad = factor * grad_smalls
    new_params, new_first, new_second = adamw(
        params, first_moment, second_moment, factor * grad_params, 0.15
    )
    new_smalls, new_small_first, new_small_second = adamw(
        smalls, small_first, small_second, small_grad, 0.2
    )
    return (
        loss,
        grad_norm,
        new_params,
        new_first,
        new_second,
        new_smalls,
        new_small_first,
        new_small_second,
        small_grad,
    )


def solution(mesh):
    flat, rows = P(AXES), P(AXES, None)
    return jax.shard_map(
        body,
        mesh=mesh,
        in_specs=(flat, flat, flat, flat, flat, flat, rows, rows, flat, P(), flat, rows),
        out_specs=(P(), P(), flat, flat, flat, flat, flat, flat, flat),
        check_vma=False,
    )
```

```python
import functools
import math
from types import SimpleNamespace

import jax
import jax.numpy as jnp
import numpy as np
from jax import lax
from jax.experimental import pallas as pl
from jax.experimental.pallas import tpu as pltpu
from jax.sharding import PartitionSpec as P

NF = 128
MID = 256
TEMB = 512
NFOUR = 128
IMG = 32
GROUPS = 32
CHAN = 3
STEP = 7
PIX = IMG * IMG
HALF = PIX // 4
INV_ROOT = 0.7071067811865476
WIDE, NARROW = AXES = ("wide", "narrow")
F32 = jnp.float32
BF16 = jnp.bfloat16

LANES = 128
BLOCKS = 32
ROWS = 552
SMALL_ROWS = 2
BLOCK = 560
CUT = 288


def mat_layout():
    return dict(
        temb_one=(2 * NFOUR, TEMB),
        temb_two=(TEMB, TEMB),
        conv_in=(9 * CHAN, NF),
        pyramid=(CHAN, MID),
        down_one=(9 * NF, MID),
        down_time=(TEMB, MID),
        down_two=(9 * MID, MID),
        down_skip=(NF, MID),
        attn_qkv=(MID, 3 * MID),
        attn_out=(MID, MID),
        up_one=(9 * MID, NF),
        up_time=(TEMB, NF),
        up_two=(9 * NF, NF),
        up_skip=(MID, NF),
        conv_out=(9 * 2 * NF, CHAN),
    )


def small_layout():
    return dict(
        temb_one_b=TEMB,
        temb_two_b=TEMB,
        conv_in_b=NF,
        pyramid_b=MID,
        down_gain_a=NF,
        down_bias_a=NF,
        down_one_b=MID,
        down_time_b=MID,
        down_gain_b=MID,
        down_bias_b=MID,
        down_two_b=MID,
        down_skip_b=MID,
        attn_gain=MID,
        attn_bias=MID,
        query_b=MID,
        value_b=MID,
        attn_out_b=MID,
        up_gain_a=MID,
        up_bias_a=MID,
        up_one_b=NF,
        up_time_b=NF,
        up_gain_b=NF,
        up_bias_b=NF,
        up_two_b=NF,
        up_skip_b=NF,
        final_gain=2 * NF,
        final_bias=2 * NF,
        conv_out_b=CHAN,
    )


def offsets():
    mats, smalls, used = {}, {}, 0
    for label, shape in mat_layout().items():
        mats[label] = (used // LANES,) + shape
        used += math.prod(shape)
    used = 0
    for label, length in small_layout().items():
        smalls[label] = (used // LANES, length)
        used += length
    return SimpleNamespace(**mats), SimpleNamespace(**smalls)


MATS, SMALLS = offsets()
WEIGHTS = list(mat_layout())
WEIGHT_SHAPES = mat_layout() | dict(conv_in=(LANES, NF), pyramid=(LANES, MID), conv_out=(LANES, 2 * NF))
RING = 8
TAPS = [(dy, dx) for dy in range(3) for dx in range(3)]


def pixel_order(side):
    across, down = side // 8, side // 2
    order = np.empty((across, down, 2, 8), np.int32)
    for xl in range(across):
        for yl in range(down):
            for yh in range(2):
                for xh in range(8):
                    order[xl, yl, yh, xh] = (yh * down + yl) * side + xh * across + xl
    return order.reshape(-1)


def fir_matrix():
    rows = np.arange(IMG // 2)[:, None]
    cols = np.arange(IMG)[None, :]
    offset = cols - 2 * rows + 1
    taps = np.where((offset == 0) | (offset == 3), 1.0, 0.0) + np.where(
        (offset == 1) | (offset == 2), 3.0, 0.0
    )
    both = np.kron(taps / 8.0, taps / 8.0)
    return both[pixel_order(IMG // 2)][:, pixel_order(IMG)].astype(np.float32)


def dot(a, b):
    return lax.dot_general(a, b, (((1,), (0,)), ((), ())), preferred_element_type=F32)


def dot_nt(a, b):
    return lax.dot_general(a, b, (((1,), (1,)), ((), ())), preferred_element_type=F32)


def dot_tn(a, b):
    return lax.dot_general(a, b, (((0,), (0,)), ((), ())), preferred_element_type=F32)


def two(value):
    high = value.astype(BF16)
    return high, (value - high.astype(F32)).astype(BF16)


def sigmoid(value):
    return 1.0 / (1.0 + jnp.exp(-value))


def rowsum(value):
    return jnp.sum(value, axis=0, keepdims=True)


def group_sums(rows, width):
    chans = rows[0].shape[1]
    at = lax.broadcasted_iota(jnp.int32, (16, chans), 0)
    stack = jnp.zeros((16, chans), F32)
    for n, row in enumerate(rows):
        rest = row
        for part in range(3):
            piece = rest.astype(BF16).astype(F32)
            stack = jnp.where(at == 3 * n + part, piece, stack)
            rest = rest - piece
    one = lax.broadcasted_iota(jnp.int32, (chans, chans), 0) // width
    other = lax.broadcasted_iota(jnp.int32, (chans, chans), 1) // width
    same = jnp.where(one == other, 1.0, 0.0).astype(BF16)
    sums = dot(stack.astype(BF16), same)
    return [sums[3 * n : 3 * n + 1] + sums[3 * n + 1 : 3 * n + 2] + sums[3 * n + 2 : 3 * n + 3] for n in range(len(rows))]


def norm_stats(value, width):
    count = float(value.shape[0] * width)
    center = group_sums([rowsum(value)], width)[0] / count
    yield
    shifted = value - center
    spread = group_sums([rowsum(shifted * shifted)], width)[0] / count
    yield
    return center, lax.rsqrt(spread + 1e-06)


def norm_back(grad, normed, gain, scale, width):
    count = float(grad.shape[0] * width)
    dbias = rowsum(grad)
    dgain = rowsum(grad * normed)
    first, second = group_sums([dbias * gain, dgain * gain], width)
    yield
    back = scale * (grad * gain - first / count - normed * (second / count))
    return back, dgain, dbias


def swish_back(pre):
    gate = sigmoid(pre)
    return gate * (1.0 + pre * (1.0 - gate))


def small(ref, label):
    at, length = label
    rows = max(1, length // LANES)
    return jnp.concatenate(
        [ref[(at + i) // 2, (at + i) % 2 : (at + i) % 2 + 1, :] for i in range(rows)], axis=1
    ) if rows > 1 else ref[at // 2, at % 2 : at % 2 + 1, :]


def add_small(ref, label, value):
    at, _ = label
    for i in range(value.shape[1] // LANES):
        j = at + i
        ref[j // 2, j % 2 : j % 2 + 1, :] += value[:, i * LANES : (i + 1) * LANES]


def fill_halo(ref, b, across, down):
    chans = ref.shape[-1]
    zero = jnp.zeros((across, 8, chans), F32)
    last = ref[b, 1 : across + 1, down].astype(F32)
    ref[b, 1 : across + 1, 0] = jnp.concatenate([zero, last[:, 0:8]], axis=1).astype(BF16)
    first = ref[b, 1 : across + 1, 1].astype(F32)
    ref[b, 1 : across + 1, down + 1] = jnp.concatenate([first[:, 8:16], zero], axis=1).astype(BF16)
    tiles = (down + 2) * 2
    at = lax.broadcasted_iota(jnp.int32, (tiles, 8, chans), 1)
    side = ref[b, across].astype(F32).reshape(tiles, 8, chans)
    side = jnp.where(at == 0, 0.0, pltpu.roll(side, 1, axis=1))
    ref[b, 0] = side.reshape(down + 2, 16, chans).astype(BF16)
    side = ref[b, 1].astype(F32).reshape(tiles, 8, chans)
    side = jnp.where(at == 7, 0.0, pltpu.roll(side, 7, axis=1))
    ref[b, across + 1] = side.reshape(down + 2, 16, chans).astype(BF16)


def set_inner(ref, b, across, down, value):
    chans = value.shape[1]
    ref[b, 1 : across + 1, 1 : down + 1] = value.astype(BF16).reshape(across, down, 16, chans)
    fill_halo(ref, b, across, down)


def taps_of(ref, b, xl, count, down, flip):
    chans = ref.shape[-1]
    parts = []
    for dy, dx in TAPS:
        y, x = (2 - dy, 2 - dx) if flip else (dy, dx)
        parts.append(ref[b, xl + x : xl + x + count, y : y + down].reshape(count * down * 16, chans))
    return jnp.concatenate(parts, axis=1)


def tap_columns(ref, chans):
    return jnp.concatenate([ref[t * chans : (t + 1) * chans, :] for t in range(9)], axis=1)


def picks(o):
    row = lax.broadcasted_iota(jnp.int32, (6 * LANES, 2 * NF), 0)
    col = lax.broadcasted_iota(jnp.int32, (6 * LANES, 2 * NF), 1)
    return jnp.where(row == CHAN * col + o, 1.0, 0.0).astype(BF16)


SAVED = dict(
    xin=((PIX, LANES), BF16),
    tiny=((HALF, LANES), BF16),
    h0=((PIX, NF), F32),
    ed1=((4, 10, 16, NF), BF16),
    sk0=((HALF, NF), BF16),
    a1=((HALF, MID), F32),
    ed2=((4, 10, 16, MID), BF16),
    h1=((HALF, MID), F32),
    g=((HALF, MID), BF16),
    qkv=((HALF, 3 * MID), BF16),
    prob=((HALF, HALF), BF16),
    mixed=((HALF, MID), BF16),
    h2=((HALF, MID), F32),
    eu1=((6, 18, 16, MID), BF16),
    sku=((PIX, MID), BF16),
    b1=((PIX, NF), F32),
    eu2=((6, 18, 16, NF), BF16),
    h3=((PIX, NF), F32),
    final=((PIX, 2 * NF), BF16),
    stats=((16, MID), F32),
)
EARLY = list(dict(sm=0, xin=0, tiny=0, h0=0, ed1=0, sk0=0, a1=0, ed2=0, h1=0, g=0, qkv=0, prob=0, mixed=0, h2=0))
TIME_SAVED = dict(
    t1=((8, TEMB), F32),
    s1=((8, TEMB), BF16),
    t2=((8, TEMB), F32),
    tact=((8, TEMB), BF16),
)


def in_step(parts):
    for _ in zip(*parts, strict=True):
        pass


def forward_kernel(piece_marks, slots, names, sent, *refs):
    r_pieces, refs = refs[: len(piece_marks)], refs[len(piece_marks) :]
    r = SimpleNamespace(**dict(zip(names, refs)))
    me = r.me[0]
    copies = []
    early = [name for name in sent if name[:2] == "w_" or name in TIME_SAVED or name in EARLY]

    def send(names):
        for name in names:
            source, target = getattr(r, name), getattr(r, "out_" + name)
            copies.append(pltpu.make_async_copy(source, target, r.sems.at[len(copies)]))
            copies[-1].start()

    stage, sm = r.stage, r.sm
    for n, (marks, first) in enumerate(piece_marks):
        for i, mark in enumerate(marks):
            home = jnp.bitwise_xor(me, mark)
            block = r_pieces[n][i].astype(F32)
            rows = min(block.shape[0], ROWS - first)
            stage[pl.ds(pl.multiple_of(home * ROWS + first, 8), rows), :] = block[:rows]
            if rows < block.shape[0]:
                sm[home] = block[rows:]
    for label in WEIGHTS:
        at, depth, width = getattr(MATS, label)
        out = getattr(r, "w_" + label)
        if width == CHAN:
            flat = jnp.concatenate([stage[pl.ds(at + i, 9, stride=6), :] for i in range(6)], axis=1).astype(BF16)
            out[...] = jnp.zeros(out.shape, BF16)
            pad = jnp.zeros((7, 2 * NF), F32)
            for o in range(CHAN):
                out[16 * o : 16 * o + 16, :] = jnp.concatenate([dot(flat, picks(o)), pad], axis=0).astype(BF16)
            continue
        if depth == 9 * CHAN:
            out[...] = jnp.zeros(out.shape, BF16)
            pad = jnp.zeros((7, NF), F32)
            for c in range(CHAN):
                part = stage[pl.ds(at + c, 9, stride=CHAN), :]
                out[16 * c : 16 * c + 16, :] = jnp.concatenate([part, pad], axis=0).astype(BF16)
            continue
        if depth == CHAN:
            out[...] = jnp.zeros(out.shape, BF16)
            pad = jnp.zeros((15, LANES), F32)
            for j in range(2):
                part = stage[pl.ds(at + j, CHAN, stride=2), :]
                for c in range(CHAN):
                    row = jnp.concatenate([part[c : c + 1], pad], axis=0)
                    out[16 * c : 16 * c + 16, j * LANES : (j + 1) * LANES] = row.astype(BF16)
            continue
        pad = out.shape[0] - depth
        for j in range(width // LANES):
            part = stage[pl.ds(at + j, depth, stride=width // LANES), :] if width > LANES else stage[pl.ds(at, depth), :]
            if pad:
                part = jnp.concatenate([part, jnp.zeros((pad, LANES), F32)], axis=0)
            out[:, j * LANES : (j + 1) * LANES] = part.astype(BF16)

    t1 = dot(r.feats[...], r.w_temb_one[...]) + small(sm, SMALLS.temb_one_b)
    r.t1[...] = t1
    s1 = (t1 * sigmoid(t1)).astype(BF16)
    r.s1[...] = s1
    t2 = dot(s1, r.w_temb_two[...]) + small(sm, SMALLS.temb_two_b)
    r.t2[...] = t2
    tact = (t2 * sigmoid(t2)).astype(BF16)
    r.tact[...] = tact
    r.pd[...] = dot(tact, r.w_down_time[...]) + (small(sm, SMALLS.down_time_b) + small(sm, SMALLS.down_one_b))
    r.pu[...] = dot(tact, r.w_up_time[...]) + (small(sm, SMALLS.up_time_b) + small(sm, SMALLS.up_one_b))

    def image(b):
        stats = r.stats

        def normed(value, width, gain, bias, at):
            center, scale = yield from norm_stats(value, width)
            chans = value.shape[1]
            stats[b, 2 * at : 2 * at + 1, :chans] = center
            stats[b, 2 * at + 1 : 2 * at + 2, :chans] = scale
            return (value - center) * (scale * gain) + bias

        high, rest = (spread(r, part) for part in two(r.images[b] + r.sigma[b] * r.noise[b]))
        r.tiny[b] = (dot(r.shrink[...], high.astype(BF16)) + dot(r.shrink[...], rest.astype(BF16))).astype(BF16)
        field = r.field.at[b]
        set_field(field, high)
        r.xin[b] = tap_lanes(field, False).astype(BF16)
        yield
        h0 = dot(r.xin[b], r.w_conv_in[...]) + small(sm, SMALLS.conv_in_b)
        r.h0[b] = h0
        yield
        y = (yield from normed(h0, 4, small(sm, SMALLS.down_gain_a), small(sm, SMALLS.down_bias_a), 0))
        y = y * sigmoid(y)
        yield
        down = dot(r.shrink[...], jnp.concatenate([*two(y), *two(h0)], axis=1))
        set_inner(r.ed1, b, 2, 8, down[:, :NF] + down[:, NF : 2 * NF])
        sk0 = (down[:, 2 * NF : 3 * NF] + down[:, 3 * NF :]).astype(BF16)
        r.sk0[b] = sk0
        yield
        a1 = dot(taps_of(r.ed1, b, 0, 2, 8, False), r.w_down_one[...]) + r.pd[pl.ds(b, 1), :]
        r.a1[b] = a1
        yield
        y = (yield from normed(a1, 8, small(sm, SMALLS.down_gain_b), small(sm, SMALLS.down_bias_b), 1))
        set_inner(r.ed2, b, 2, 8, y * sigmoid(y))
        yield
        a2 = dot(taps_of(r.ed2, b, 0, 2, 8, False), r.w_down_two[...]) + dot(sk0, r.w_down_skip[...])
        a2 = (a2 + (small(sm, SMALLS.down_two_b) + small(sm, SMALLS.down_skip_b))) * INV_ROOT
        h1 = (a2 + dot(r.tiny[b], r.w_pyramid[...]) + small(sm, SMALLS.pyramid_b)) * INV_ROOT
        r.h1[b] = h1
        yield
        g = (yield from normed(h1, 8, small(sm, SMALLS.attn_gain), small(sm, SMALLS.attn_bias), 2)).astype(BF16)
        r.g[b] = g
        yield
        proj = dot(g, r.w_attn_qkv[...])
        q = (proj[:, :MID] + small(sm, SMALLS.query_b)).astype(BF16)
        k = proj[:, MID : 2 * MID].astype(BF16)
        v = (proj[:, 2 * MID :] + small(sm, SMALLS.value_b)).astype(BF16)
        r.qkv[b] = jnp.concatenate([q, k, v], axis=1)
        yield
        scores = dot_nt(q, k) * (MID**-0.5)
        yield
        weight = jnp.exp(scores - jnp.max(scores, axis=1, keepdims=True))
        prob = (weight / jnp.sum(weight, axis=1, keepdims=True)).astype(BF16)
        r.prob[b] = prob
        yield
        mixed = dot(prob, v).astype(BF16)
        r.mixed[b] = mixed
        yield
        h2 = (h1 + dot(mixed, r.w_attn_out[...]) + small(sm, SMALLS.attn_out_b)) * INV_ROOT
        r.h2[b] = h2
        yield
        if b == 0:
            send(early)
        y = (yield from normed(h2, 8, small(sm, SMALLS.up_gain_a), small(sm, SMALLS.up_bias_a), 3))
        y = y * sigmoid(y)
        coarse = jnp.concatenate([*two(y), *two(h2)], axis=1)
        yield
        for xl in range(4):
            fine = dot(r.grow[xl * 256 : (xl + 1) * 256, :], coarse)
            part = (fine[:, :MID] + fine[:, MID : 2 * MID]).astype(BF16)
            r.eu1[b, xl + 1, 1:17] = part.reshape(16, 16, MID)
            r.sku[b, xl * 256 : (xl + 1) * 256, :] = (fine[:, 2 * MID : 3 * MID] + fine[:, 3 * MID :]).astype(BF16)
        fill_halo(r.eu1, b, 4, 16)
        yield
        for xl in range(4):
            r.b1[b, xl * 256 : (xl + 1) * 256, :] = (
                dot(taps_of(r.eu1, b, xl, 1, 16, False), r.w_up_one[...]) + r.pu[pl.ds(b, 1), :]
            )
            yield
        yield
        y = (yield from normed(r.b1[b], 4, small(sm, SMALLS.up_gain_b), small(sm, SMALLS.up_bias_b), 4))
        set_inner(r.eu2, b, 4, 16, y * sigmoid(y))
        yield
        bias = small(sm, SMALLS.up_two_b) + small(sm, SMALLS.up_skip_b)
        for xl in range(4):
            part = slice(xl * 256, (xl + 1) * 256)
            up = dot(taps_of(r.eu2, b, xl, 1, 16, False), r.w_up_two[...])
            r.h3[b, part, :] = (up + dot(r.sku[b, part, :], r.w_up_skip[...]) + bias) * INV_ROOT
            yield
        yield
        gain, bias = small(sm, SMALLS.final_gain), small(sm, SMALLS.final_bias)
        y = (yield from normed(r.h3[b], 8, gain[:, :NF], bias[:, :NF], 5))
        r.final[b, :, :NF] = (y * sigmoid(y)).astype(BF16)
        yield
        y = (yield from normed(r.h0[b], 8, gain[:, NF:], bias[:, NF:], 6))
        r.final[b, :, NF:] = (y * sigmoid(y)).astype(BF16)
        yield
        wide = dot_nt(r.final[b], r.w_conv_out[...])
        field = r.field.at[b]
        set_field(field, wide)
        total = tap_lanes(field, False)
        high, rest = two(total)
        wide = two((dot(high, r.unfan[...]) + dot(rest, r.unfan[...])) * r.own_x[...])
        err = dot(r.y_rows[...], wide[0]) + dot(r.y_rows[...], wide[1]) + r.out_bias[...] + r.noise[b]
        r.err[b] = err
        r.err16[b] = err.astype(BF16)

    prepare_out_bias(r, sm)
    in_step([image(b) for b in range(slots)])
    send(name for name in sent if name not in early)
    for copy in copies:
        copy.wait()


def prepare_out_bias(r, sm):
    bias = small(sm, SMALLS.conv_out_b)
    total = jnp.zeros((1, IMG * CHAN), F32)
    for c in range(CHAN):
        total += bias[:, c : c + 1] * r.colours[c : c + 1, :]
    r.out_bias[...] = jnp.broadcast_to(total, (IMG, IMG * CHAN))


def spread(r, value):
    wide = dot(r.y_of[...], value) * r.own_x[...]
    return dot(wide.astype(BF16), r.fan[...])


def pixel_maps():
    order = pixel_order(IMG)
    column, lane = np.arange(IMG * CHAN), np.arange(LANES)
    y_of = order[:, None] // IMG == np.arange(IMG)
    own_x = order[:, None] % IMG == column // CHAN
    fan = column[:, None] % CHAN == lane // 16
    colours = np.arange(8)[:, None] == column % CHAN
    maps = dict(y_of=y_of, y_rows=y_of.T, fan=fan, unfan=fan.T & (lane % 16 < 9)[:, None])
    maps = {name: value.astype(BF16) for name, value in maps.items()}
    return maps | dict(own_x=own_x.astype(np.float32), colours=colours.astype(np.float32))


def set_field(field, value):
    field[1:5, 1:17] = value.reshape(4, 16, 16, LANES)
    zero = jnp.zeros((4, 8, LANES), F32)
    field[1:5, 0] = jnp.concatenate([zero, field[1:5, 16, 0:8]], axis=1)
    field[1:5, 17] = jnp.concatenate([field[1:5, 1, 8:16], zero], axis=1)
    at = lax.broadcasted_iota(jnp.int32, (36, 8, LANES), 1)
    side = pltpu.roll(field[4].reshape(36, 8, LANES), 1, axis=1)
    field[0] = jnp.where(at == 0, 0.0, side).reshape(18, 16, LANES)
    side = pltpu.roll(field[1].reshape(36, 8, LANES), 7, axis=1)
    field[5] = jnp.where(at == 7, 0.0, side).reshape(18, 16, LANES)


def backward_kernel(slots, names, fetched, *refs):
    r = SimpleNamespace(**dict(zip(names, refs)))
    copies = []
    for n, name in enumerate(fetched):
        copies.append(pltpu.make_async_copy(getattr(r, "in_" + name), getattr(r, name), r.sems.at[n]))
        copies[-1].start()

    def arrive(name):
        while len(copies) > len(fetched) - 1 - fetched.index(name):
            copies.pop(0).wait()

    me = r.me[0]
    sm, stage, gsm = r.sm, r.stage, r.gsm
    stats = r.stats
    total = jnp.sum(sm[...], axis=0)[SMALL_ROWS : SMALL_ROWS + 1, 0:1]
    theirs = sm[jnp.bitwise_xor(me, BLOCKS // 2), SMALL_ROWS : SMALL_ROWS + 1, :]
    gsm[...] = jnp.zeros(gsm.shape, F32)
    r.dpd[...] = jnp.zeros(r.dpd.shape, F32)
    r.dpu[...] = jnp.zeros(r.dpu.shape, F32)
    r.dout_sum[...] = jnp.zeros(r.dout_sum.shape, F32)
    r.loss[...] = jnp.zeros(r.loss.shape, F32)
    counts, pairs = r.ints[0], r.ints
    other_counts = theirs[:, 1:2]

    def put(label, value, first=0):
        at, _, width = label
        step = width // LANES
        for j in range(step):
            part = value[:, j * LANES : (j + 1) * LANES]
            if step == 1:
                stage[pl.ds(at + first, value.shape[0]), :] = part
            else:
                stage[pl.ds(at + first * step + j, value.shape[0], stride=step), :] = part

    def image(b):
        def stat(at, chans):
            return stats[b, 2 * at : 2 * at + 1, :chans], stats[b, 2 * at + 1 : 2 * at + 2, :chans]

        def renorm(value, at, gain, bias):
            center, scale = stat(at, value.shape[1])
            normed = (value - center) * scale
            return normed, normed * gain + bias, scale

        err = r.err[b]
        mine = r.other[pairs[1 + b]].astype(F32)
        gap = err - mine
        live = jnp.where(b < counts, 1.0, 0.0)
        scale = 1.0 / (total * (CHAN * PIX))
        r.loss[...] += (live * scale) * (0.5 * err * err + 0.25 * gap * gap)
        grad = (live * scale) * (err + 0.5 * gap)
        for s in range(slots):
            on = jnp.where((theirs[:, 2 + s : 3 + s] == b) & (s < other_counts), 0.5 * scale, 0.0)
            grad += on * (err - r.other[s].astype(F32))
        yield
        if b == 0:
            arrive(FETCH_ORDER[6])
        r.dout_sum[...] += grad
        field = r.field.at[b]
        set_field(field, spread(r, grad.astype(BF16)))
        cols = tap_lanes(field, True).astype(BF16)
        r.cols[b] = cols
        yield
        gain, bias = small(sm, SMALLS.final_gain), small(sm, SMALLS.final_bias)
        back = dot(cols, r.w_conv_out[...])
        yield
        n3, y3, scale3 = renorm(r.h3[b], 5, gain[:, :NF], bias[:, :NF])
        dh3, dgain, dbias = yield from norm_back(back[:, :NF] * swish_back(y3), n3, gain[:, :NF], scale3, 8)
        n0, y0, scale0 = renorm(r.h0[b], 6, gain[:, NF:], bias[:, NF:])
        dh0, dgain0, dbias0 = yield from norm_back(back[:, NF:] * swish_back(y0), n0, gain[:, NF:], scale0, 8)
        add_small(gsm, SMALLS.final_gain, jnp.concatenate([dgain, dgain0], axis=1))
        add_small(gsm, SMALLS.final_bias, jnp.concatenate([dbias, dbias0], axis=1))
        r.dh0[b] = dh0
        yield
        dh3 = dh3 * INV_ROOT
        add_small(gsm, SMALLS.up_two_b, rowsum(dh3))
        set_inner(r.gu2, b, 4, 16, dh3)
        yield
        turned = tap_columns(r.w_up_two, NF)
        for xl in range(4):
            r.wide[b, xl * 256 : (xl + 1) * 256, :] = dot_nt(taps_of(r.gu2, b, xl, 1, 16, True), turned)
        yield
        gain, bias = small(sm, SMALLS.up_gain_b), small(sm, SMALLS.up_bias_b)
        n, y, scale1 = renorm(r.b1[b], 4, gain, bias)
        db1, dgain, dbias = yield from norm_back(r.wide[b] * swish_back(y), n, gain, scale1, 4)
        add_small(gsm, SMALLS.up_gain_b, dgain)
        add_small(gsm, SMALLS.up_bias_b, dbias)
        r.dpu[pl.ds(b, 1), :] = rowsum(db1)
        set_inner(r.gu1, b, 4, 16, db1)
        yield
        turned = tap_columns(r.w_up_one, MID)
        half = jnp.zeros((HALF, 2 * MID), F32)
        for xl in range(4):
            branch = dot_nt(taps_of(r.gu1, b, xl, 1, 16, True), turned)
            skip = dot_nt(r.gu2[b, xl + 1, 1:17].reshape(256, NF), r.w_up_skip[...])
            both = jnp.concatenate([branch.astype(BF16), skip.astype(BF16)], axis=1)
            half += dot(r.shrink[:, xl * 256 : (xl + 1) * 256], both)
        half = half * 4.0
        yield
        if b == 0:
            arrive(FETCH_ORDER[-1])
            arrive(fetched[-1])
        gain, bias = small(sm, SMALLS.up_gain_a), small(sm, SMALLS.up_bias_a)
        n, y, scale2 = renorm(r.h2[b], 3, gain, bias)
        dh2, dgain, dbias = yield from norm_back(half[:, :MID] * swish_back(y), n, gain, scale2, 8)
        add_small(gsm, SMALLS.up_gain_a, dgain)
        add_small(gsm, SMALLS.up_bias_a, dbias)
        dh2 = (dh2 + half[:, MID:]) * INV_ROOT
        add_small(gsm, SMALLS.attn_out_b, rowsum(dh2))
        datt = dh2.astype(BF16)
        r.datt[b] = datt
        yield
        dmixed = dot_nt(datt, r.w_attn_out[...]).astype(BF16)
        q, k, v = r.qkv[b, :, :MID], r.qkv[b, :, MID : 2 * MID], r.qkv[b, :, 2 * MID :]
        prob = r.prob[b]
        dprob = dot_nt(dmixed, v)
        yield
        dv = dot_tn(prob, dmixed)
        yield
        wide = prob.astype(F32)
        dscore = wide * (dprob - jnp.sum(wide * dprob, axis=1, keepdims=True))
        dscore = (dscore * (MID**-0.5)).astype(BF16)
        yield
        dq = dot(dscore, k)
        dk = dot_tn(dscore, q)
        add_small(gsm, SMALLS.query_b, rowsum(dq))
        add_small(gsm, SMALLS.value_b, rowsum(dv))
        dqkv = jnp.concatenate([dq, dk, dv], axis=1).astype(BF16)
        r.dqkv[b] = dqkv
        yield
        dg = dot_nt(dqkv, r.w_attn_qkv[...])
        yield
        gain, bias = small(sm, SMALLS.attn_gain), small(sm, SMALLS.attn_bias)
        n, _, scale2 = renorm(r.h1[b], 2, gain, bias)
        dh1, dgain, dbias = yield from norm_back(dg, n, gain, scale2, 8)
        add_small(gsm, SMALLS.attn_gain, dgain)
        add_small(gsm, SMALLS.attn_bias, dbias)
        dh1 = (dh1 + dh2) * INV_ROOT
        r.dpyr[b] = dh1.astype(BF16)
        add_small(gsm, SMALLS.pyramid_b, rowsum(dh1))
        da2 = dh1 * INV_ROOT
        add_small(gsm, SMALLS.down_two_b, rowsum(da2))
        set_inner(r.gd2, b, 2, 8, da2)
        yield
        dsk0 = dot_nt(r.gd2[b, 1:3, 1:9].reshape(HALF, MID), r.w_down_skip[...])
        turned = tap_columns(r.w_down_two, MID)
        du = dot_nt(taps_of(r.gd2, b, 0, 2, 8, True), turned)
        yield
        gain, bias = small(sm, SMALLS.down_gain_b), small(sm, SMALLS.down_bias_b)
        n, y, scale2 = renorm(r.a1[b], 1, gain, bias)
        da1, dgain, dbias = yield from norm_back(du * swish_back(y), n, gain, scale2, 8)
        add_small(gsm, SMALLS.down_gain_b, dgain)
        add_small(gsm, SMALLS.down_bias_b, dbias)
        r.dpd[pl.ds(b, 1), :] = rowsum(da1)
        set_inner(r.gd1, b, 2, 8, da1)
        yield
        turned = tap_columns(r.w_down_one, NF)
        dd0 = dot_nt(taps_of(r.gd1, b, 0, 2, 8, True), turned)
        both = jnp.concatenate([dd0, dsk0], axis=1).astype(BF16)
        fine = dot(r.grow[...], both) * 0.25
        yield
        gain, bias = small(sm, SMALLS.down_gain_a), small(sm, SMALLS.down_bias_a)
        n, y, scale1 = renorm(r.h0[b], 0, gain, bias)
        back0, dgain, dbias = yield from norm_back(fine[:, :NF] * swish_back(y), n, gain, scale1, 4)
        add_small(gsm, SMALLS.down_gain_a, dgain)
        add_small(gsm, SMALLS.down_bias_a, dbias)
        dh0 = r.dh0[b] + back0 + fine[:, NF:]
        add_small(gsm, SMALLS.conv_in_b, rowsum(dh0))
        r.din[b] = dh0.astype(BF16)

    in_step([image(b) for b in range(slots)])

    whole = slots * PIX
    fewer = slots * HALF
    def conv_grad(label, acts, grads, across, down):
        chans, rows = acts.shape[-1], slots * across * down * 16
        left = acts[:, 1 : across + 1, 1 : down + 1].reshape(rows, chans)
        out = grads.shape[-1]
        right = jnp.concatenate(
            [grads[:, 2 - dx : 2 - dx + across, 2 - dy : 2 - dy + down].reshape(rows, out) for dy, dx in TAPS], axis=1
        )
        back = dot_tn(left, right)
        for t in range(9):
            put(label, back[:, t * out : (t + 1) * out], t * chans)

    dpd, dpu = r.dpd[...], r.dpu[...]
    for label in (SMALLS.down_time_b, SMALLS.down_one_b):
        add_small(gsm, label, rowsum(dpd))
    for label in (SMALLS.up_time_b, SMALLS.up_one_b):
        add_small(gsm, label, rowsum(dpu))
    dpd16, dpu16 = dpd.astype(BF16), dpu.astype(BF16)
    put(MATS.down_time, dot_tn(r.tact[...], dpd16))
    put(MATS.up_time, dot_tn(r.tact[...], dpu16))
    dtact = dot_nt(dpd16, r.w_down_time[...]) + dot_nt(dpu16, r.w_up_time[...])
    dt2 = dtact * swish_back(r.t2[...])
    add_small(gsm, SMALLS.temb_two_b, rowsum(dt2))
    put(MATS.temb_two, dot_tn(r.s1[...], dt2.astype(BF16)))
    dt1 = dot_nt(dt2.astype(BF16), r.w_temb_two[...]) * swish_back(r.t1[...])
    add_small(gsm, SMALLS.temb_one_b, rowsum(dt1))
    put(MATS.temb_one, dot_tn(r.feats[...], dt1.astype(BF16)))
    for label, twin in ((SMALLS.up_skip_b, SMALLS.up_two_b), (SMALLS.down_skip_b, SMALLS.down_two_b)):
        value = small(gsm, twin)
        add_small(gsm, label, value)
    sums = rowsum(r.dout_sum[...])
    lane = lax.broadcasted_iota(jnp.int32, (1, LANES), 1)
    total_bias = jnp.zeros((1, LANES), F32)
    for c in range(CHAN):
        own = jnp.sum(sums * r.colours[c : c + 1, :], axis=1, keepdims=True)
        total_bias += jnp.where(lane == c, own, 0.0)
    add_small(gsm, SMALLS.conv_out_b, total_bias)
    dout = dot_tn(r.cols[...].reshape(whole, LANES), r.final[...].reshape(whole, 2 * NF))
    flat = jnp.zeros((16, 6 * LANES), F32)
    for o in range(CHAN):
        flat += dot_nt(dout[16 * o : 16 * o + 16].astype(BF16), picks(o))
    at = MATS.conv_out[0]
    for i in range(6):
        for t in range(9):
            stage[at + 6 * t + i : at + 6 * t + i + 1, :] = flat[t : t + 1, i * LANES : (i + 1) * LANES]

    last = MATS.conv_out[0] + 54
    stage[last : BLOCKS * ROWS, :] = jnp.zeros((BLOCKS * ROWS - last, LANES), F32)
    put(MATS.up_skip, dot_tn(r.sku[...].reshape(whole, MID), r.gu2[:, 1:5, 1:17].reshape(whole, NF)))
    conv_grad(MATS.up_two, r.eu2, r.gu2, 4, 16)
    conv_grad(MATS.up_one, r.eu1, r.gu1, 4, 16)
    put(MATS.attn_out, dot_tn(r.mixed[...].reshape(fewer, MID), r.datt[...].reshape(fewer, MID)))
    put(MATS.attn_qkv, dot_tn(r.g[...].reshape(fewer, MID), r.dqkv[...].reshape(fewer, 3 * MID)))
    put(MATS.down_skip, dot_tn(r.sk0[...].reshape(fewer, NF), r.gd2[:, 1:3, 1:9].reshape(fewer, MID)))
    conv_grad(MATS.down_two, r.ed2, r.gd2, 2, 8)
    conv_grad(MATS.down_one, r.ed1, r.gd1, 2, 8)
    back = dot_tn(r.tiny[...].reshape(fewer, LANES), r.dpyr[...].reshape(fewer, MID))
    put(MATS.pyramid, jnp.concatenate([back[16 * c : 16 * c + 1] for c in range(CHAN)], axis=0))
    back = dot_tn(r.xin[...].reshape(whole, LANES), r.din[...].reshape(whole, NF))
    for c in range(CHAN):
        stage[pl.ds(MATS.conv_in[0] + c, 9, stride=CHAN), :] = back[16 * c : 16 * c + 9]
    ring, sems = r.ring, r.ring_sems

    class sending:
        def __init__(self, upper, lower, d, slot):
            place = block_place(jnp.bitwise_xor(d, me))
            self.copies = [
                pltpu.make_async_copy(ring.at[slot, :CUT], upper.at[place], sems.at[0, slot]),
                pltpu.make_async_copy(ring.at[slot, CUT:], lower.at[place], sems.at[1, slot]),
            ]

        def start(self):
            for copy in self.copies:
                copy.start()

        def wait(self):
            for copy in self.copies:
                copy.wait()

    def give(d, carry):
        slot = d % RING

        @pl.when(d >= RING)
        def _():
            sending(r.stay, r.stay_low, d, slot).wait()

        block = jnp.concatenate([stage[pl.ds(pl.multiple_of(d * ROWS, 8), ROWS), :], gsm[d]], axis=0)
        ring[slot] = block.astype(BF16)
        goes = jnp.bitwise_xor(d, me) % 2 == 1

        @pl.when(goes)
        def _():
            sending(r.leave, r.leave_low, d, slot).start()

        @pl.when(jnp.logical_not(goes))
        def _():
            sending(r.stay, r.stay_low, d, slot).start()

        return carry

    lax.fori_loop(0, BLOCKS, give, 0)
    for d in range(BLOCKS - RING, BLOCKS):
        sending(r.stay, r.stay_low, d, d % RING).wait()


def tap_lanes(field, flip):
    lane = lax.broadcasted_iota(jnp.int32, (PIX, LANES), 1) % 16
    total = jnp.zeros((PIX, LANES), F32)
    for t, (dy, dx) in enumerate(TAPS):
        y, x = (2 - dy, 2 - dx) if flip else (dy, dx)
        total = jnp.where(lane == t, field[x : x + 4, y : y + 16].reshape(PIX, LANES), total)
    return total


def block_place(mark):
    low, high, x, y = (mark // 2) % 2, (mark // 4) % 2, (mark // 8) % 2, mark // 16
    return high * 8 + (4 * y + 2 * x + high * 2 * (x - y)) + low


def vmem():
    return pl.BlockSpec(memory_space=pltpu.VMEM)


def anywhere():
    return pl.BlockSpec(memory_space=pl.ANY)


def smem():
    return pl.BlockSpec(memory_space=pltpu.SMEM)


LIMIT = 60 * 1024 * 1024


def run_forward(me, sigma, pieces, marks, data):
    slots = data.images.shape[0]
    ins = dict(me=me, sigma=sigma) | vars(data)
    outs = {"w_" + label: (WEIGHT_SHAPES[label], BF16) for label in WEIGHTS}
    outs |= dict(sm=((BLOCKS, 8, LANES), F32)) | TIME_SAVED
    outs |= {label: ((slots,) + shape, dtype) for label, (shape, dtype) in SAVED.items()}
    outs |= dict(err=((slots, IMG, IMG * CHAN), F32), err16=((slots, IMG, IMG * CHAN), BF16))
    scratch = dict(
        stage=((BLOCKS * ROWS, LANES), F32),
        pd=((8, MID), F32),
        pu=((8, NF), F32),
        out_bias=((IMG, IMG * CHAN), F32),
        field=((slots, 6, 18, 16, LANES), F32),
    )
    names = list(ins) + ["out_" + label for label in outs] + list(outs) + list(scratch) + ["sems"]
    results = pl.pallas_call(
        functools.partial(forward_kernel, marks, slots, names, list(outs)),
        out_shape=[jax.ShapeDtypeStruct(*v) for v in outs.values()],
        in_specs=[vmem()] * len(pieces) + [smem()] * 2 + [vmem()] * (len(ins) - 2),
        out_specs=[anywhere()] * len(outs),
        scratch_shapes=[pltpu.VMEM(*v) for v in (outs | scratch).values()] + [pltpu.SemaphoreType.DMA((len(outs),))],
        compiler_params=pltpu.CompilerParams(vmem_limit_bytes=LIMIT),
        name="forward",
    )(*pieces, *ins.values())
    return SimpleNamespace(**dict(zip(outs, results)))


FETCH_ORDER = list(
    dict(
        w_conv_out=0,
        h3=0,
        h0=0,
        w_up_two=0,
        b1=0,
        w_up_skip=0,
        w_up_one=0,
        h2=0,
        w_attn_out=0,
        qkv=0,
        prob=0,
        w_attn_qkv=0,
        h1=0,
        w_down_skip=0,
        w_down_two=0,
        a1=0,
        w_down_one=0,
        w_down_time=0,
        w_up_time=0,
        t2=0,
        s1=0,
        w_temb_two=0,
        t1=0,
        tact=0,
        final=0,
        sku=0,
        eu2=0,
        eu1=0,
        mixed=0,
        g=0,
        sk0=0,
        ed2=0,
        ed1=0,
        xin=0,
        tiny=0,
    )
)


def run_backward(me, ints, other, kept, data):
    slots = other.shape[0]
    ins = dict(me=me, ints=ints)
    scalars = len(ins)
    ins |= dict(other=other, err=kept.err, sm=kept.sm, stats=kept.stats)
    ins |= dict(y_of=data.y_of, own_x=data.own_x, fan=data.fan, colours=data.colours)
    direct = len(ins)
    fetched = dict(shrink=data.shrink)
    fetched |= {name: getattr(kept, name) for name in FETCH_ORDER}
    fetched |= dict(grow=data.grow, feats=data.feats)
    ins |= {"in_" + name: value for name, value in fetched.items()}
    upper = ((BLOCKS // 2, CUT, LANES), BF16)
    lower = ((BLOCKS // 2, BLOCK - CUT, LANES), BF16)
    outs = dict(stay=upper, stay_low=lower, leave=upper, leave_low=lower, loss=((IMG, IMG * CHAN), F32))
    scratch = {name: (value.shape, value.dtype) for name, value in fetched.items()}
    scratch |= dict(
        stage=((BLOCKS * ROWS, LANES), F32),
        gsm=((BLOCKS, 8, LANES), F32),
        ring=((RING, BLOCK, LANES), BF16),
        dpd=((8, MID), F32),
        dpu=((8, NF), F32),
        dout_sum=((IMG, IMG * CHAN), F32),
        field=((slots, 6, 18, 16, LANES), F32),
        cols=((slots, PIX, LANES), BF16),
        gu2=((slots, 6, 18, 16, NF), BF16),
        gu1=((slots, 6, 18, 16, NF), BF16),
        gd2=((slots, 4, 10, 16, MID), BF16),
        gd1=((slots, 4, 10, 16, MID), BF16),
        wide=((slots, PIX, NF), F32),
        dh0=((slots, PIX, NF), F32),
        din=((slots, PIX, NF), BF16),
        datt=((slots, HALF, MID), BF16),
        dqkv=((slots, HALF, 3 * MID), BF16),
        dpyr=((slots, HALF, MID), BF16),
    )
    names = list(ins) + list(outs) + list(scratch) + ["sems", "ring_sems"]
    results = pl.pallas_call(
        functools.partial(backward_kernel, slots, names, list(fetched)),
        out_shape=[jax.ShapeDtypeStruct(*v) for v in outs.values()],
        in_specs=[smem()] * scalars + [vmem()] * (direct - scalars) + [anywhere()] * (len(ins) - direct),
        out_specs=[anywhere()] * 4 + [vmem()],
        scratch_shapes=[pltpu.VMEM(*v) for v in scratch.values()]
        + [pltpu.SemaphoreType.DMA((len(fetched),)), pltpu.SemaphoreType.DMA((2, RING))],
        compiler_params=pltpu.CompilerParams(vmem_limit_bytes=LIMIT),
        name="backward",
    )(*ins.values())
    return SimpleNamespace(**dict(zip(outs, results)))


def swap(value, axis, mask):
    size = lax.axis_size(axis)
    return lax.ppermute(value, axis, [(i, i ^ mask) for i in range(size)])


def sum_everywhere(value):
    count = lax.axis_size(WIDE) * lax.axis_size(NARROW)
    rows = lax.all_to_all(jnp.broadcast_to(value, (count, LANES)), AXES, 0, 0, tiled=True)
    return jnp.sum(rows, axis=0, keepdims=True)


def notes(live, ints):
    return jnp.pad(jnp.concatenate([live, ints]).astype(F32), (0, LANES - 1 - ints.shape[0]))[None]


def gather_all(params, smalls, ints, meanwhile):
    if lax.axis_size(WIDE) == 4 and lax.axis_size(NARROW) == 8:
        rows = params.reshape(ROWS, LANES)
        tail = jnp.pad(notes(ints[:1], ints), ((0, BLOCK - ROWS - SMALL_ROWS - 1), (0, 0)))
        tail = jnp.concatenate([rows, smalls.reshape(SMALL_ROWS, LANES), tail])
        owns = [tail.astype(BF16)[None]]
        near, side, far = [], [], []
        for own in owns:
            z1, z2, z3 = (swap(own, NARROW, m) for m in (2, 4, 6))
            near.append((jnp.concatenate([own, z1]), jnp.concatenate([z2, z3])))
        near[0], first = lax.optimization_barrier((near[0], meanwhile[:2]))
        for a, b in near:
            side.append((swap(a, WIDE, 1), swap(b, WIDE, 2)))
        side[0], second = lax.optimization_barrier((side[0], meanwhile[2:]))
        for (a, b), (ax, by) in zip(near, side):
            far.append((swap(jnp.concatenate([a, ax]), WIDE, 2), swap(jnp.concatenate([b, by]), WIDE, 1)))
        pieces, marks = [], []
        for part in range(len(owns)):
            arrays = [jnp.concatenate(near[part]), jnp.concatenate(side[part]), *far[part]]
            lists = [[0, 2, 4, 6], [8, 10, 20, 22], [16, 18, 24, 26], [12, 14, 28, 30]]
            pieces += arrays + [swap(array, NARROW, 1) for array in arrays]
            marks += [(at, part * CUT) for at in lists] + [([m + 1 for m in at], part * CUT) for at in lists]
        return pieces, marks, True, first + second
    whole = lax.all_gather(params.astype(BF16), AXES, axis=0, tiled=True).reshape(BLOCKS, ROWS, LANES)
    little = lax.all_gather(smalls.astype(BF16), AXES, axis=0, tiled=True).reshape(BLOCKS, SMALL_ROWS, LANES)
    live = lax.all_gather(ints[:1], AXES, axis=0, tiled=True).reshape(BLOCKS, -1).sum(axis=1)
    others = swap(ints, WIDE, lax.axis_size(WIDE) // 2)
    extra = jnp.stack([notes(live[d : d + 1], others) for d in range(BLOCKS)])
    extra = jnp.pad(extra, ((0, 0), (0, BLOCK - ROWS - SMALL_ROWS - 1), (0, 0))).astype(BF16)
    return [jnp.concatenate([whole, little, extra], axis=1)], [(list(range(BLOCKS)), 0)], False, meanwhile


def collect_kernel(count, *refs):
    pieces, loss, own, rows = refs[:count], refs[count], refs[count + 1], refs[count + 2]
    first, squares = 0, jnp.zeros((1, LANES), F32)
    for n in range(0, count, 4):
        total = sum(piece[...].astype(F32) for piece in pieces[n : n + 4])
        own[first : first + total.shape[0], :] = total
        first += total.shape[0]
        squares += rowsum(total * total)
    squares = jnp.sum(squares, axis=1, keepdims=True)
    part = jnp.sum(rowsum(loss[...]), axis=1, keepdims=True)
    lane = lax.broadcasted_iota(jnp.int32, rows.shape, 1)
    rows[...] = jnp.where(lane == 0, squares, jnp.where(lane == 1, part, 0.0))


def collect(pieces, loss):
    count = lax.axis_size(WIDE) * lax.axis_size(NARROW)
    return pl.pallas_call(
        functools.partial(collect_kernel, len(pieces)),
        out_shape=[jax.ShapeDtypeStruct((BLOCK, LANES), F32), jax.ShapeDtypeStruct((count, LANES), F32)],
        in_specs=[vmem()] * (len(pieces) + 1),
        out_specs=[vmem()] * 2,
        name="collect",
    )(*pieces, loss)


def update_kernel(rows, own, *refs):
    ins, (loss, norm, *outs) = refs[:6], refs[6:]
    both = rowsum(rows[...])
    grad_norm = jnp.sqrt(both[:, 0:1])
    loss[...] = both[:, 1:2]
    norm[...] = grad_norm
    factor = jnp.minimum(1.0, 0.01 / (grad_norm + 1e-06))
    grad = factor * own[:ROWS, :]
    for ref, value in zip(outs, adamw(*(ref[...] for ref in ins[:3]), grad, 0.15)):
        ref[...] = value
    grad = factor * own[ROWS : ROWS + SMALL_ROWS, :]
    outs[6][...] = grad
    for ref, value in zip(outs[3:6], adamw(*(ref[...] for ref in ins[3:]), grad, 0.2)):
        ref[...] = value


def update(rows, own, vectors):
    vectors = [vector.reshape(-1, LANES) for vector in vectors]
    one = jax.ShapeDtypeStruct((1, 1), F32)
    like = [jax.ShapeDtypeStruct(vector.shape, F32) for vector in vectors]
    outs = pl.pallas_call(
        update_kernel,
        out_shape=[one, one] + like + like[3:4],
        in_specs=[vmem()] * 8,
        out_specs=[vmem()] * 9,
        name="update",
    )(rows, own, *vectors)
    return [value.reshape(()) for value in outs[:2]] + [value.reshape(-1) for value in outs[2:]]


def scatter_sums(stay, leave, loss, relative):
    if relative:

        def join(kept, received):
            return (kept.astype(F32) + received.astype(F32)).astype(BF16)

        parts = [join(a, swap(b, NARROW, 1)) for a, b in zip(stay, leave)]
        parts = [part.reshape((2, 2, BLOCKS // 8) + part.shape[1:]) for part in parts]
        pairs = []
        for a, b in parts:
            if pairs:
                pairs[0], (a, b) = lax.optimization_barrier((pairs[0], (a, b)))
            pairs.append((join(a[0], swap(a[1], WIDE, 2)), join(b[0], swap(b[1], WIDE, 1))))
        parts = [(join(a[:2], swap(a[2:], WIDE, 1)), join(b[:2], swap(b[2:], WIDE, 2))) for a, b in pairs]
        pieces = []
        for a, b in parts:
            pieces.append(a[0])
            pieces += [swap(value, NARROW, mask) for value, mask in ((a[1], 2), (b[0], 4), (b[1], 6))]
        return collect(pieces, loss)
    stay, leave = jnp.concatenate(stay, axis=1), jnp.concatenate(leave, axis=1)
    grads = jnp.stack([(leave if d % 2 else stay)[block_place(d)] for d in range(BLOCKS)])
    large = grads[:, :ROWS].reshape(-1).astype(F32)
    little = grads[:, ROWS : ROWS + SMALL_ROWS].reshape(-1).astype(F32)
    return (
        lax.psum_scatter(large, AXES, scatter_dimension=0, tiled=True),
        lax.psum_scatter(little, AXES, scatter_dimension=0, tiled=True),
    )


def adamw(weight, moment, second, grad, rate):
    moment_new = 0.5 * moment + 0.5 * grad
    second_new = 0.99 * second + 0.01 * grad * grad
    direction = moment_new / (1.0 - 0.5**STEP) / (jnp.sqrt(second_new / (1.0 - 0.99**STEP)) + 1e-08)
    return (weight - rate * (direction + 0.01 * weight), moment_new, second_new)


def body(
    params,
    first_moment,
    second_moment,
    smalls,
    small_first,
    small_second,
    images,
    noise,
    sigma,
    freq,
    counts,
    partner,
):
    slots = images.shape[0]
    ints = jnp.concatenate([counts, partner[0]]).astype(jnp.int32)
    shrink = fir_matrix()
    phase = jnp.log(sigma)[:, None] * freq[None, :] * (2.0 * math.pi)
    feats = jnp.concatenate([jnp.sin(phase), jnp.cos(phase)], axis=-1)
    feats = jnp.pad(feats.astype(BF16), ((0, 8 - slots), (0, 0)))
    own = (feats, images.reshape(slots, IMG, IMG * CHAN), noise.reshape(slots, IMG, IMG * CHAN))
    pieces, marks, relative, own = gather_all(params, smalls, ints, own)
    index = lax.axis_index(WIDE) * lax.axis_size(NARROW) + lax.axis_index(NARROW)
    me = (index if relative else jnp.zeros_like(index)).astype(jnp.int32)[None]
    data = SimpleNamespace(
        feats=own[0],
        images=own[1],
        noise=own[2],
        shrink=jnp.asarray(shrink, BF16),
        grow=jnp.asarray(4.0 * shrink.T, BF16),
        **{name: jnp.asarray(value) for name, value in pixel_maps().items()},
    )
    kept = run_forward(me, sigma, pieces, marks, data)
    other = swap(kept.err16, WIDE, lax.axis_size(WIDE) // 2)
    done = run_backward(me, ints, other, kept, data)
    vectors = [params, first_moment, second_moment, smalls, small_first, small_second]
    sums = scatter_sums((done.stay, done.stay_low), (done.leave, done.leave_low), done.loss, relative)
    if relative:
        own, rows = sums
        return tuple(update(lax.all_to_all(rows, AXES, 0, 0, tiled=True), own, vectors))
    grad_params, grad_smalls = sums
    squares = jnp.sum(grad_params * grad_params) + jnp.sum(grad_smalls * grad_smalls)
    lane = lax.broadcasted_iota(jnp.int32, (1, LANES), 1)
    both = sum_everywhere(jnp.where(lane == 0, squares, jnp.where(lane == 1, jnp.sum(done.loss), 0.0)))
    loss, grad_norm = both[0, 1], jnp.sqrt(both[0, 0])
    factor = jnp.minimum(1.0, 0.01 / (grad_norm + 1e-06))
    small_grad = factor * grad_smalls
    new_params, new_first, new_second = adamw(
        params, first_moment, second_moment, factor * grad_params, 0.15
    )
    new_smalls, new_small_first, new_small_second = adamw(
        smalls, small_first, small_second, small_grad, 0.2
    )
    return (
        loss,
        grad_norm,
        new_params,
        new_first,
        new_second,
        new_smalls,
        new_small_first,
        new_small_second,
        small_grad,
    )


def solution(mesh):
    flat, rows = P(AXES), P(AXES, None)
    return jax.shard_map(
        body,
        mesh=mesh,
        in_specs=(flat, flat, flat, flat, flat, flat, rows, rows, flat, P(), flat, rows),
        out_specs=(P(), P(), flat, flat, flat, flat, flat, flat, flat),
        check_vma=False,
    )
```

```python
import functools
import math
from types import SimpleNamespace

import jax
import jax.numpy as jnp
import numpy as np
from jax import lax
from jax.experimental import pallas as pl
from jax.experimental.pallas import tpu as pltpu
from jax.sharding import PartitionSpec as P

NF = 128
MID = 256
TEMB = 512
NFOUR = 128
IMG = 32
GROUPS = 32
CHAN = 3
STEP = 7
PIX = IMG * IMG
HALF = PIX // 4
INV_ROOT = 0.7071067811865476
WIDE, NARROW = AXES = ("wide", "narrow")
F32 = jnp.float32
BF16 = jnp.bfloat16

LANES = 128
BLOCKS = 32
ROWS = 552
SMALL_ROWS = 2
BLOCK = 560
CUT = 288


def mat_layout():
    return dict(
        temb_one=(2 * NFOUR, TEMB),
        temb_two=(TEMB, TEMB),
        conv_in=(9 * CHAN, NF),
        pyramid=(CHAN, MID),
        down_one=(9 * NF, MID),
        down_time=(TEMB, MID),
        down_two=(9 * MID, MID),
        down_skip=(NF, MID),
        attn_qkv=(MID, 3 * MID),
        attn_out=(MID, MID),
        up_one=(9 * MID, NF),
        up_time=(TEMB, NF),
        up_two=(9 * NF, NF),
        up_skip=(MID, NF),
        conv_out=(9 * 2 * NF, CHAN),
    )


def small_layout():
    return dict(
        temb_one_b=TEMB,
        temb_two_b=TEMB,
        conv_in_b=NF,
        pyramid_b=MID,
        down_gain_a=NF,
        down_bias_a=NF,
        down_one_b=MID,
        down_time_b=MID,
        down_gain_b=MID,
        down_bias_b=MID,
        down_two_b=MID,
        down_skip_b=MID,
        attn_gain=MID,
        attn_bias=MID,
        query_b=MID,
        value_b=MID,
        attn_out_b=MID,
        up_gain_a=MID,
        up_bias_a=MID,
        up_one_b=NF,
        up_time_b=NF,
        up_gain_b=NF,
        up_bias_b=NF,
        up_two_b=NF,
        up_skip_b=NF,
        final_gain=2 * NF,
        final_bias=2 * NF,
        conv_out_b=CHAN,
    )


def offsets():
    mats, smalls, used = {}, {}, 0
    for label, shape in mat_layout().items():
        mats[label] = (used // LANES,) + shape
        used += math.prod(shape)
    used = 0
    for label, length in small_layout().items():
        smalls[label] = (used // LANES, length)
        used += length
    return SimpleNamespace(**mats), SimpleNamespace(**smalls)


MATS, SMALLS = offsets()
WEIGHTS = list(mat_layout())
WEIGHT_SHAPES = mat_layout() | dict(conv_in=(LANES, NF), pyramid=(LANES, MID), conv_out=(LANES, 2 * NF))
RING = 8
TAPS = [(dy, dx) for dy in range(3) for dx in range(3)]


def pixel_order(side):
    across, down = side // 8, side // 2
    order = np.empty((across, down, 2, 8), np.int32)
    for xl in range(across):
        for yl in range(down):
            for yh in range(2):
                for xh in range(8):
                    order[xl, yl, yh, xh] = (yh * down + yl) * side + xh * across + xl
    return order.reshape(-1)


def fir_matrix():
    rows = np.arange(IMG // 2)[:, None]
    cols = np.arange(IMG)[None, :]
    offset = cols - 2 * rows + 1
    taps = np.where((offset == 0) | (offset == 3), 1.0, 0.0) + np.where(
        (offset == 1) | (offset == 2), 3.0, 0.0
    )
    both = np.kron(taps / 8.0, taps / 8.0)
    return both[pixel_order(IMG // 2)][:, pixel_order(IMG)].astype(np.float32)


def dot(a, b):
    return lax.dot_general(a, b, (((1,), (0,)), ((), ())), preferred_element_type=F32)


def dot_nt(a, b):
    return lax.dot_general(a, b, (((1,), (1,)), ((), ())), preferred_element_type=F32)


def dot_tn(a, b):
    return lax.dot_general(a, b, (((0,), (0,)), ((), ())), preferred_element_type=F32)


def two(value):
    high = value.astype(BF16)
    return high, (value - high.astype(F32)).astype(BF16)


def sigmoid(value):
    return 0.5 * jnp.tanh(0.5 * value) + 0.5


def rowsum(value):
    return jnp.sum(value, axis=0, keepdims=True)


def group_sums(rows, width):
    chans = rows[0].shape[1]
    at = lax.broadcasted_iota(jnp.int32, (16, chans), 0)
    stack = jnp.zeros((16, chans), F32)
    for n, row in enumerate(rows):
        rest = row
        for part in range(3):
            piece = rest.astype(BF16).astype(F32)
            stack = jnp.where(at == 3 * n + part, piece, stack)
            rest = rest - piece
    one = lax.broadcasted_iota(jnp.int32, (chans, chans), 0) // width
    other = lax.broadcasted_iota(jnp.int32, (chans, chans), 1) // width
    same = jnp.where(one == other, 1.0, 0.0).astype(BF16)
    sums = dot(stack.astype(BF16), same)
    return [sums[3 * n : 3 * n + 1] + sums[3 * n + 1 : 3 * n + 2] + sums[3 * n + 2 : 3 * n + 3] for n in range(len(rows))]


def norm_stats(value, width):
    count = float(value.shape[0] * width)
    center = group_sums([rowsum(value)], width)[0] / count
    yield
    shifted = value - center
    spread = group_sums([rowsum(shifted * shifted)], width)[0] / count
    yield
    return center, lax.rsqrt(spread + 1e-06)


def norm_back(grad, normed, gain, scale, width):
    count = float(grad.shape[0] * width)
    dbias = rowsum(grad)
    dgain = rowsum(grad * normed)
    first, second = group_sums([dbias * gain, dgain * gain], width)
    yield
    back = scale * (grad * gain - first / count - normed * (second / count))
    return back, dgain, dbias


def swish_back(pre):
    gate = sigmoid(pre)
    return gate * (1.0 + pre * (1.0 - gate))


def small(ref, label):
    at, length = label
    rows = max(1, length // LANES)
    return jnp.concatenate(
        [ref[(at + i) // 2, (at + i) % 2 : (at + i) % 2 + 1, :] for i in range(rows)], axis=1
    ) if rows > 1 else ref[at // 2, at % 2 : at % 2 + 1, :]


def add_small(ref, label, value):
    at, _ = label
    for i in range(value.shape[1] // LANES):
        j = at + i
        ref[j // 2, j % 2 : j % 2 + 1, :] += value[:, i * LANES : (i + 1) * LANES]


def fill_halo(ref, b, across, down):
    chans = ref.shape[-1]
    zero = jnp.zeros((across, 8, chans), F32)
    last = ref[b, 1 : across + 1, down].astype(F32)
    ref[b, 1 : across + 1, 0] = jnp.concatenate([zero, last[:, 0:8]], axis=1).astype(BF16)
    first = ref[b, 1 : across + 1, 1].astype(F32)
    ref[b, 1 : across + 1, down + 1] = jnp.concatenate([first[:, 8:16], zero], axis=1).astype(BF16)
    tiles = (down + 2) * 2
    at = lax.broadcasted_iota(jnp.int32, (tiles, 8, chans), 1)
    side = ref[b, across].astype(F32).reshape(tiles, 8, chans)
    side = jnp.where(at == 0, 0.0, pltpu.roll(side, 1, axis=1))
    ref[b, 0] = side.reshape(down + 2, 16, chans).astype(BF16)
    side = ref[b, 1].astype(F32).reshape(tiles, 8, chans)
    side = jnp.where(at == 7, 0.0, pltpu.roll(side, 7, axis=1))
    ref[b, across + 1] = side.reshape(down + 2, 16, chans).astype(BF16)


def set_inner(ref, b, across, down, value):
    chans = value.shape[1]
    ref[b, 1 : across + 1, 1 : down + 1] = value.astype(BF16).reshape(across, down, 16, chans)
    fill_halo(ref, b, across, down)


def taps_of(ref, b, xl, count, down, flip):
    chans = ref.shape[-1]
    parts = []
    for dy, dx in TAPS:
        y, x = (2 - dy, 2 - dx) if flip else (dy, dx)
        parts.append(ref[b, xl + x : xl + x + count, y : y + down].reshape(count * down * 16, chans))
    return jnp.concatenate(parts, axis=1)


def tap_columns(ref, chans):
    return jnp.concatenate([ref[t * chans : (t + 1) * chans, :] for t in range(9)], axis=1)


def picks(o):
    row = lax.broadcasted_iota(jnp.int32, (6 * LANES, 2 * NF), 0)
    col = lax.broadcasted_iota(jnp.int32, (6 * LANES, 2 * NF), 1)
    return jnp.where(row == CHAN * col + o, 1.0, 0.0).astype(BF16)


SAVED = dict(
    xin=((PIX, LANES), BF16),
    tiny=((HALF, LANES), BF16),
    h0=((PIX, NF), F32),
    ed1=((4, 10, 16, NF), BF16),
    sk0=((HALF, NF), BF16),
    a1=((HALF, MID), F32),
    ed2=((4, 10, 16, MID), BF16),
    h1=((HALF, MID), F32),
    g=((HALF, MID), BF16),
    qkv=((HALF, 3 * MID), BF16),
    prob=((HALF, HALF), BF16),
    mixed=((HALF, MID), BF16),
    h2=((HALF, MID), F32),
    eu1=((6, 18, 16, MID), BF16),
    sku=((PIX, MID), BF16),
    b1=((PIX, NF), F32),
    eu2=((6, 18, 16, NF), BF16),
    h3=((PIX, NF), F32),
    final=((PIX, 2 * NF), BF16),
    stats=((16, MID), F32),
)
EARLY = list(dict(sm=0, xin=0, tiny=0, h0=0, ed1=0, sk0=0, a1=0, ed2=0, h1=0, g=0, qkv=0, prob=0, mixed=0, h2=0))
TIME_SAVED = dict(
    t1=((8, TEMB), F32),
    s1=((8, TEMB), BF16),
    t2=((8, TEMB), F32),
    tact=((8, TEMB), BF16),
)


def in_step(parts):
    for _ in zip(*parts, strict=True):
        pass


def forward_kernel(piece_marks, slots, names, sent, *refs):
    r_pieces, refs = refs[: len(piece_marks)], refs[len(piece_marks) :]
    r = SimpleNamespace(**dict(zip(names, refs)))
    me = r.me[0]
    copies = []
    early = [name for name in sent if name[:2] == "w_" or name in TIME_SAVED or name in EARLY]

    def send(names):
        for name in names:
            source, target = getattr(r, name), getattr(r, "out_" + name)
            copies.append(pltpu.make_async_copy(source, target, r.sems.at[len(copies)]))
            copies[-1].start()

    stage, sm = r.stage, r.sm
    for n, (marks, first) in enumerate(piece_marks):
        for i, mark in enumerate(marks):
            home = jnp.bitwise_xor(me, mark)
            block = r_pieces[n][i].astype(F32)
            rows = min(block.shape[0], ROWS - first)
            stage[pl.ds(pl.multiple_of(home * ROWS + first, 8), rows), :] = block[:rows]
            if rows < block.shape[0]:
                sm[home] = block[rows:]
    for label in WEIGHTS:
        at, depth, width = getattr(MATS, label)
        out = getattr(r, "w_" + label)
        if width == CHAN:
            flat = jnp.concatenate([stage[pl.ds(at + i, 9, stride=6), :] for i in range(6)], axis=1).astype(BF16)
            out[...] = jnp.zeros(out.shape, BF16)
            pad = jnp.zeros((7, 2 * NF), F32)
            for o in range(CHAN):
                out[16 * o : 16 * o + 16, :] = jnp.concatenate([dot(flat, picks(o)), pad], axis=0).astype(BF16)
            continue
        if depth == 9 * CHAN:
            out[...] = jnp.zeros(out.shape, BF16)
            pad = jnp.zeros((7, NF), F32)
            for c in range(CHAN):
                part = stage[pl.ds(at + c, 9, stride=CHAN), :]
                out[16 * c : 16 * c + 16, :] = jnp.concatenate([part, pad], axis=0).astype(BF16)
            continue
        if depth == CHAN:
            out[...] = jnp.zeros(out.shape, BF16)
            pad = jnp.zeros((15, LANES), F32)
            for j in range(2):
                part = stage[pl.ds(at + j, CHAN, stride=2), :]
                for c in range(CHAN):
                    row = jnp.concatenate([part[c : c + 1], pad], axis=0)
                    out[16 * c : 16 * c + 16, j * LANES : (j + 1) * LANES] = row.astype(BF16)
            continue
        pad = out.shape[0] - depth
        for j in range(width // LANES):
            part = stage[pl.ds(at + j, depth, stride=width // LANES), :] if width > LANES else stage[pl.ds(at, depth), :]
            if pad:
                part = jnp.concatenate([part, jnp.zeros((pad, LANES), F32)], axis=0)
            out[:, j * LANES : (j + 1) * LANES] = part.astype(BF16)

    t1 = dot(r.feats[...], r.w_temb_one[...]) + small(sm, SMALLS.temb_one_b)
    r.t1[...] = t1
    s1 = (t1 * sigmoid(t1)).astype(BF16)
    r.s1[...] = s1
    t2 = dot(s1, r.w_temb_two[...]) + small(sm, SMALLS.temb_two_b)
    r.t2[...] = t2
    tact = (t2 * sigmoid(t2)).astype(BF16)
    r.tact[...] = tact
    r.pd[...] = dot(tact, r.w_down_time[...]) + (small(sm, SMALLS.down_time_b) + small(sm, SMALLS.down_one_b))
    r.pu[...] = dot(tact, r.w_up_time[...]) + (small(sm, SMALLS.up_time_b) + small(sm, SMALLS.up_one_b))

    def image(b):
        stats = r.stats

        def normed(value, width, gain, bias, at):
            center, scale = yield from norm_stats(value, width)
            chans = value.shape[1]
            stats[b, 2 * at : 2 * at + 1, :chans] = center
            stats[b, 2 * at + 1 : 2 * at + 2, :chans] = scale
            return (value - center) * (scale * gain) + bias

        high, rest = (spread(r, part) for part in two(r.images[b] + r.sigma[b] * r.noise[b]))
        r.tiny[b] = (dot(r.shrink[...], high.astype(BF16)) + dot(r.shrink[...], rest.astype(BF16))).astype(BF16)
        field = r.field.at[b]
        set_field(field, high)
        r.xin[b] = tap_lanes(field, False).astype(BF16)
        yield
        h0 = dot(r.xin[b], r.w_conv_in[...]) + small(sm, SMALLS.conv_in_b)
        r.h0[b] = h0
        yield
        y = (yield from normed(h0, 4, small(sm, SMALLS.down_gain_a), small(sm, SMALLS.down_bias_a), 0))
        y = y * sigmoid(y)
        yield
        down = dot(r.shrink[...], jnp.concatenate([*two(y), *two(h0)], axis=1))
        set_inner(r.ed1, b, 2, 8, down[:, :NF] + down[:, NF : 2 * NF])
        sk0 = (down[:, 2 * NF : 3 * NF] + down[:, 3 * NF :]).astype(BF16)
        r.sk0[b] = sk0
        yield
        a1 = dot(taps_of(r.ed1, b, 0, 2, 8, False), r.w_down_one[...]) + r.pd[pl.ds(b, 1), :]
        r.a1[b] = a1
        yield
        y = (yield from normed(a1, 8, small(sm, SMALLS.down_gain_b), small(sm, SMALLS.down_bias_b), 1))
        set_inner(r.ed2, b, 2, 8, y * sigmoid(y))
        yield
        a2 = dot(taps_of(r.ed2, b, 0, 2, 8, False), r.w_down_two[...]) + dot(sk0, r.w_down_skip[...])
        a2 = (a2 + (small(sm, SMALLS.down_two_b) + small(sm, SMALLS.down_skip_b))) * INV_ROOT
        h1 = (a2 + dot(r.tiny[b], r.w_pyramid[...]) + small(sm, SMALLS.pyramid_b)) * INV_ROOT
        r.h1[b] = h1
        yield
        g = (yield from normed(h1, 8, small(sm, SMALLS.attn_gain), small(sm, SMALLS.attn_bias), 2)).astype(BF16)
        r.g[b] = g
        yield
        proj = dot(g, r.w_attn_qkv[...])
        q = (proj[:, :MID] + small(sm, SMALLS.query_b)).astype(BF16)
        k = proj[:, MID : 2 * MID].astype(BF16)
        v = (proj[:, 2 * MID :] + small(sm, SMALLS.value_b)).astype(BF16)
        r.qkv[b] = jnp.concatenate([q, k, v], axis=1)
        yield
        scores = dot_nt(q, k) * (MID**-0.5)
        yield
        weight = jnp.exp(scores - jnp.max(scores, axis=1, keepdims=True))
        prob = (weight * (1.0 / jnp.sum(weight, axis=1, keepdims=True))).astype(BF16)
        r.prob[b] = prob
        yield
        mixed = dot(prob, v).astype(BF16)
        r.mixed[b] = mixed
        yield
        h2 = (h1 + dot(mixed, r.w_attn_out[...]) + small(sm, SMALLS.attn_out_b)) * INV_ROOT
        r.h2[b] = h2
        yield
        if b == 0:
            send(early)
        y = (yield from normed(h2, 8, small(sm, SMALLS.up_gain_a), small(sm, SMALLS.up_bias_a), 3))
        y = y * sigmoid(y)
        coarse = jnp.concatenate([*two(y), *two(h2)], axis=1)
        yield
        for xl in range(4):
            fine = dot(r.grow[xl * 256 : (xl + 1) * 256, :], coarse)
            part = (fine[:, :MID] + fine[:, MID : 2 * MID]).astype(BF16)
            r.eu1[b, xl + 1, 1:17] = part.reshape(16, 16, MID)
            r.sku[b, xl * 256 : (xl + 1) * 256, :] = (fine[:, 2 * MID : 3 * MID] + fine[:, 3 * MID :]).astype(BF16)
        fill_halo(r.eu1, b, 4, 16)
        yield
        for xl in range(4):
            r.b1[b, xl * 256 : (xl + 1) * 256, :] = (
                dot(taps_of(r.eu1, b, xl, 1, 16, False), r.w_up_one[...]) + r.pu[pl.ds(b, 1), :]
            )
            yield
        yield
        y = (yield from normed(r.b1[b], 4, small(sm, SMALLS.up_gain_b), small(sm, SMALLS.up_bias_b), 4))
        set_inner(r.eu2, b, 4, 16, y * sigmoid(y))
        yield
        bias = small(sm, SMALLS.up_two_b) + small(sm, SMALLS.up_skip_b)
        for xl in range(4):
            part = slice(xl * 256, (xl + 1) * 256)
            up = dot(taps_of(r.eu2, b, xl, 1, 16, False), r.w_up_two[...])
            r.h3[b, part, :] = (up + dot(r.sku[b, part, :], r.w_up_skip[...]) + bias) * INV_ROOT
            yield
        yield
        gain, bias = small(sm, SMALLS.final_gain), small(sm, SMALLS.final_bias)
        y = (yield from normed(r.h3[b], 8, gain[:, :NF], bias[:, :NF], 5))
        r.final[b, :, :NF] = (y * sigmoid(y)).astype(BF16)
        yield
        y = (yield from normed(r.h0[b], 8, gain[:, NF:], bias[:, NF:], 6))
        r.final[b, :, NF:] = (y * sigmoid(y)).astype(BF16)
        yield
        wide = dot_nt(r.final[b], r.w_conv_out[...])
        field = r.field.at[b]
        set_field(field, wide)
        total = tap_lanes(field, False)
        high, rest = two(total)
        wide = two((dot(high, r.unfan[...]) + dot(rest, r.unfan[...])) * r.own_x[...])
        err = dot(r.y_rows[...], wide[0]) + dot(r.y_rows[...], wide[1]) + r.out_bias[...] + r.noise[b]
        r.err[b] = err
        r.err16[b] = err.astype(BF16)

    prepare_out_bias(r, sm)
    in_step([image(b) for b in range(slots)])
    send(name for name in sent if name not in early)
    for copy in copies:
        copy.wait()


def prepare_out_bias(r, sm):
    bias = small(sm, SMALLS.conv_out_b)
    total = jnp.zeros((1, IMG * CHAN), F32)
    for c in range(CHAN):
        total += bias[:, c : c + 1] * r.colours[c : c + 1, :]
    r.out_bias[...] = jnp.broadcast_to(total, (IMG, IMG * CHAN))


def spread(r, value):
    wide = dot(r.y_of[...], value) * r.own_x[...]
    return dot(wide.astype(BF16), r.fan[...])


def pixel_maps():
    order = pixel_order(IMG)
    column, lane = np.arange(IMG * CHAN), np.arange(LANES)
    y_of = order[:, None] // IMG == np.arange(IMG)
    own_x = order[:, None] % IMG == column // CHAN
    fan = column[:, None] % CHAN == lane // 16
    colours = np.arange(8)[:, None] == column % CHAN
    maps = dict(y_of=y_of, y_rows=y_of.T, fan=fan, unfan=fan.T & (lane % 16 < 9)[:, None])
    maps = {name: value.astype(BF16) for name, value in maps.items()}
    return maps | dict(own_x=own_x.astype(np.float32), colours=colours.astype(np.float32))


def set_field(field, value):
    field[1:5, 1:17] = value.reshape(4, 16, 16, LANES)
    zero = jnp.zeros((4, 8, LANES), F32)
    field[1:5, 0] = jnp.concatenate([zero, field[1:5, 16, 0:8]], axis=1)
    field[1:5, 17] = jnp.concatenate([field[1:5, 1, 8:16], zero], axis=1)
    at = lax.broadcasted_iota(jnp.int32, (36, 8, LANES), 1)
    side = pltpu.roll(field[4].reshape(36, 8, LANES), 1, axis=1)
    field[0] = jnp.where(at == 0, 0.0, side).reshape(18, 16, LANES)
    side = pltpu.roll(field[1].reshape(36, 8, LANES), 7, axis=1)
    field[5] = jnp.where(at == 7, 0.0, side).reshape(18, 16, LANES)


def backward_kernel(slots, names, fetched, *refs):
    r = SimpleNamespace(**dict(zip(names, refs)))
    copies = []
    for n, name in enumerate(fetched):
        copies.append(pltpu.make_async_copy(getattr(r, "in_" + name), getattr(r, name), r.sems.at[n]))
        copies[-1].start()

    def arrive(name):
        while len(copies) > len(fetched) - 1 - fetched.index(name):
            copies.pop(0).wait()

    me = r.me[0]
    sm, stage, gsm = r.sm, r.stage, r.gsm
    stats = r.stats
    total = jnp.sum(sm[...], axis=0)[SMALL_ROWS : SMALL_ROWS + 1, 0:1]
    theirs = sm[jnp.bitwise_xor(me, BLOCKS // 2), SMALL_ROWS : SMALL_ROWS + 1, :]
    gsm[...] = jnp.zeros(gsm.shape, F32)
    r.dpd[...] = jnp.zeros(r.dpd.shape, F32)
    r.dpu[...] = jnp.zeros(r.dpu.shape, F32)
    r.dout_sum[...] = jnp.zeros(r.dout_sum.shape, F32)
    r.loss[...] = jnp.zeros(r.loss.shape, F32)
    counts, pairs = r.ints[0], r.ints
    other_counts = theirs[:, 1:2]

    def put(label, value, first=0):
        at, _, width = label
        step = width // LANES
        for j in range(step):
            part = value[:, j * LANES : (j + 1) * LANES]
            if step == 1:
                stage[pl.ds(at + first, value.shape[0]), :] = part
            else:
                stage[pl.ds(at + first * step + j, value.shape[0], stride=step), :] = part

    def image(b):
        def stat(at, chans):
            return stats[b, 2 * at : 2 * at + 1, :chans], stats[b, 2 * at + 1 : 2 * at + 2, :chans]

        def renorm(value, at, gain, bias):
            center, scale = stat(at, value.shape[1])
            normed = (value - center) * scale
            return normed, normed * gain + bias, scale

        err = r.err[b]
        mine = r.other[pairs[1 + b]].astype(F32)
        gap = err - mine
        live = jnp.where(b < counts, 1.0, 0.0)
        scale = 1.0 / (total * (CHAN * PIX))
        r.loss[...] += (live * scale) * (0.5 * err * err + 0.25 * gap * gap)
        grad = (live * scale) * (err + 0.5 * gap)
        for s in range(slots):
            on = jnp.where((theirs[:, 2 + s : 3 + s] == b) & (s < other_counts), 0.5 * scale, 0.0)
            grad += on * (err - r.other[s].astype(F32))
        yield
        if b == 0:
            arrive(FETCH_ORDER[6])
        r.dout_sum[...] += grad
        field = r.field.at[b]
        set_field(field, spread(r, grad.astype(BF16)))
        cols = tap_lanes(field, True).astype(BF16)
        r.cols[b] = cols
        yield
        gain, bias = small(sm, SMALLS.final_gain), small(sm, SMALLS.final_bias)
        back = dot(cols, r.w_conv_out[...])
        yield
        n3, y3, scale3 = renorm(r.h3[b], 5, gain[:, :NF], bias[:, :NF])
        dh3, dgain, dbias = yield from norm_back(back[:, :NF] * swish_back(y3), n3, gain[:, :NF], scale3, 8)
        n0, y0, scale0 = renorm(r.h0[b], 6, gain[:, NF:], bias[:, NF:])
        dh0, dgain0, dbias0 = yield from norm_back(back[:, NF:] * swish_back(y0), n0, gain[:, NF:], scale0, 8)
        add_small(gsm, SMALLS.final_gain, jnp.concatenate([dgain, dgain0], axis=1))
        add_small(gsm, SMALLS.final_bias, jnp.concatenate([dbias, dbias0], axis=1))
        r.dh0[b] = dh0
        yield
        dh3 = dh3 * INV_ROOT
        add_small(gsm, SMALLS.up_two_b, rowsum(dh3))
        set_inner(r.gu2, b, 4, 16, dh3)
        yield
        turned = tap_columns(r.w_up_two, NF)
        for xl in range(4):
            r.wide[b, xl * 256 : (xl + 1) * 256, :] = dot_nt(taps_of(r.gu2, b, xl, 1, 16, True), turned)
        yield
        gain, bias = small(sm, SMALLS.up_gain_b), small(sm, SMALLS.up_bias_b)
        n, y, scale1 = renorm(r.b1[b], 4, gain, bias)
        db1, dgain, dbias = yield from norm_back(r.wide[b] * swish_back(y), n, gain, scale1, 4)
        add_small(gsm, SMALLS.up_gain_b, dgain)
        add_small(gsm, SMALLS.up_bias_b, dbias)
        r.dpu[pl.ds(b, 1), :] = rowsum(db1)
        set_inner(r.gu1, b, 4, 16, db1)
        yield
        turned = tap_columns(r.w_up_one, MID)
        half = jnp.zeros((HALF, 2 * MID), F32)
        for xl in range(4):
            branch = dot_nt(taps_of(r.gu1, b, xl, 1, 16, True), turned)
            skip = dot_nt(r.gu2[b, xl + 1, 1:17].reshape(256, NF), r.w_up_skip[...])
            both = jnp.concatenate([branch.astype(BF16), skip.astype(BF16)], axis=1)
            half += dot(r.shrink[:, xl * 256 : (xl + 1) * 256], both)
        half = half * 4.0
        yield
        if b == 0:
            arrive(FETCH_ORDER[-1])
            arrive(fetched[-1])
        gain, bias = small(sm, SMALLS.up_gain_a), small(sm, SMALLS.up_bias_a)
        n, y, scale2 = renorm(r.h2[b], 3, gain, bias)
        dh2, dgain, dbias = yield from norm_back(half[:, :MID] * swish_back(y), n, gain, scale2, 8)
        add_small(gsm, SMALLS.up_gain_a, dgain)
        add_small(gsm, SMALLS.up_bias_a, dbias)
        dh2 = (dh2 + half[:, MID:]) * INV_ROOT
        add_small(gsm, SMALLS.attn_out_b, rowsum(dh2))
        datt = dh2.astype(BF16)
        r.datt[b] = datt
        yield
        dmixed = dot_nt(datt, r.w_attn_out[...]).astype(BF16)
        q, k, v = r.qkv[b, :, :MID], r.qkv[b, :, MID : 2 * MID], r.qkv[b, :, 2 * MID :]
        prob = r.prob[b]
        dprob = dot_nt(dmixed, v)
        yield
        dv = dot_tn(prob, dmixed)
        yield
        wide = prob.astype(F32)
        dscore = wide * (dprob - jnp.sum(wide * dprob, axis=1, keepdims=True))
        dscore = (dscore * (MID**-0.5)).astype(BF16)
        yield
        dq = dot(dscore, k)
        dk = dot_tn(dscore, q)
        add_small(gsm, SMALLS.query_b, rowsum(dq))
        add_small(gsm, SMALLS.value_b, rowsum(dv))
        dqkv = jnp.concatenate([dq, dk, dv], axis=1).astype(BF16)
        r.dqkv[b] = dqkv
        yield
        dg = dot_nt(dqkv, r.w_attn_qkv[...])
        yield
        gain, bias = small(sm, SMALLS.attn_gain), small(sm, SMALLS.attn_bias)
        n, _, scale2 = renorm(r.h1[b], 2, gain, bias)
        dh1, dgain, dbias = yield from norm_back(dg, n, gain, scale2, 8)
        add_small(gsm, SMALLS.attn_gain, dgain)
        add_small(gsm, SMALLS.attn_bias, dbias)
        dh1 = (dh1 + dh2) * INV_ROOT
        r.dpyr[b] = dh1.astype(BF16)
        add_small(gsm, SMALLS.pyramid_b, rowsum(dh1))
        da2 = dh1 * INV_ROOT
        add_small(gsm, SMALLS.down_two_b, rowsum(da2))
        set_inner(r.gd2, b, 2, 8, da2)
        yield
        dsk0 = dot_nt(r.gd2[b, 1:3, 1:9].reshape(HALF, MID), r.w_down_skip[...])
        turned = tap_columns(r.w_down_two, MID)
        du = dot_nt(taps_of(r.gd2, b, 0, 2, 8, True), turned)
        yield
        gain, bias = small(sm, SMALLS.down_gain_b), small(sm, SMALLS.down_bias_b)
        n, y, scale2 = renorm(r.a1[b], 1, gain, bias)
        da1, dgain, dbias = yield from norm_back(du * swish_back(y), n, gain, scale2, 8)
        add_small(gsm, SMALLS.down_gain_b, dgain)
        add_small(gsm, SMALLS.down_bias_b, dbias)
        r.dpd[pl.ds(b, 1), :] = rowsum(da1)
        set_inner(r.gd1, b, 2, 8, da1)
        yield
        turned = tap_columns(r.w_down_one, NF)
        dd0 = dot_nt(taps_of(r.gd1, b, 0, 2, 8, True), turned)
        both = jnp.concatenate([dd0, dsk0], axis=1).astype(BF16)
        fine = dot(r.grow[...], both) * 0.25
        yield
        gain, bias = small(sm, SMALLS.down_gain_a), small(sm, SMALLS.down_bias_a)
        n, y, scale1 = renorm(r.h0[b], 0, gain, bias)
        back0, dgain, dbias = yield from norm_back(fine[:, :NF] * swish_back(y), n, gain, scale1, 4)
        add_small(gsm, SMALLS.down_gain_a, dgain)
        add_small(gsm, SMALLS.down_bias_a, dbias)
        dh0 = r.dh0[b] + back0 + fine[:, NF:]
        add_small(gsm, SMALLS.conv_in_b, rowsum(dh0))
        r.din[b] = dh0.astype(BF16)

    in_step([image(b) for b in range(slots)])

    whole = slots * PIX
    fewer = slots * HALF
    def conv_grad(label, acts, grads, across, down):
        chans, rows = acts.shape[-1], slots * across * down * 16
        left = acts[:, 1 : across + 1, 1 : down + 1].reshape(rows, chans)
        out = grads.shape[-1]
        right = jnp.concatenate(
            [grads[:, 2 - dx : 2 - dx + across, 2 - dy : 2 - dy + down].reshape(rows, out) for dy, dx in TAPS], axis=1
        )
        back = dot_tn(left, right)
        for t in range(9):
            put(label, back[:, t * out : (t + 1) * out], t * chans)

    dpd, dpu = r.dpd[...], r.dpu[...]
    for label in (SMALLS.down_time_b, SMALLS.down_one_b):
        add_small(gsm, label, rowsum(dpd))
    for label in (SMALLS.up_time_b, SMALLS.up_one_b):
        add_small(gsm, label, rowsum(dpu))
    dpd16, dpu16 = dpd.astype(BF16), dpu.astype(BF16)
    put(MATS.down_time, dot_tn(r.tact[...], dpd16))
    put(MATS.up_time, dot_tn(r.tact[...], dpu16))
    dtact = dot_nt(dpd16, r.w_down_time[...]) + dot_nt(dpu16, r.w_up_time[...])
    dt2 = dtact * swish_back(r.t2[...])
    add_small(gsm, SMALLS.temb_two_b, rowsum(dt2))
    put(MATS.temb_two, dot_tn(r.s1[...], dt2.astype(BF16)))
    dt1 = dot_nt(dt2.astype(BF16), r.w_temb_two[...]) * swish_back(r.t1[...])
    add_small(gsm, SMALLS.temb_one_b, rowsum(dt1))
    put(MATS.temb_one, dot_tn(r.feats[...], dt1.astype(BF16)))
    for label, twin in ((SMALLS.up_skip_b, SMALLS.up_two_b), (SMALLS.down_skip_b, SMALLS.down_two_b)):
        value = small(gsm, twin)
        add_small(gsm, label, value)
    sums = rowsum(r.dout_sum[...])
    lane = lax.broadcasted_iota(jnp.int32, (1, LANES), 1)
    total_bias = jnp.zeros((1, LANES), F32)
    for c in range(CHAN):
        own = jnp.sum(sums * r.colours[c : c + 1, :], axis=1, keepdims=True)
        total_bias += jnp.where(lane == c, own, 0.0)
    add_small(gsm, SMALLS.conv_out_b, total_bias)
    dout = dot_tn(r.cols[...].reshape(whole, LANES), r.final[...].reshape(whole, 2 * NF))
    flat = jnp.zeros((16, 6 * LANES), F32)
    for o in range(CHAN):
        flat += dot_nt(dout[16 * o : 16 * o + 16].astype(BF16), picks(o))
    at = MATS.conv_out[0]
    for i in range(6):
        for t in range(9):
            stage[at + 6 * t + i : at + 6 * t + i + 1, :] = flat[t : t + 1, i * LANES : (i + 1) * LANES]

    last = MATS.conv_out[0] + 54
    stage[last : BLOCKS * ROWS, :] = jnp.zeros((BLOCKS * ROWS - last, LANES), F32)
    put(MATS.up_skip, dot_tn(r.sku[...].reshape(whole, MID), r.gu2[:, 1:5, 1:17].reshape(whole, NF)))
    conv_grad(MATS.up_two, r.eu2, r.gu2, 4, 16)
    conv_grad(MATS.up_one, r.eu1, r.gu1, 4, 16)
    put(MATS.attn_out, dot_tn(r.mixed[...].reshape(fewer, MID), r.datt[...].reshape(fewer, MID)))
    put(MATS.attn_qkv, dot_tn(r.g[...].reshape(fewer, MID), r.dqkv[...].reshape(fewer, 3 * MID)))
    put(MATS.down_skip, dot_tn(r.sk0[...].reshape(fewer, NF), r.gd2[:, 1:3, 1:9].reshape(fewer, MID)))
    conv_grad(MATS.down_two, r.ed2, r.gd2, 2, 8)
    conv_grad(MATS.down_one, r.ed1, r.gd1, 2, 8)
    back = dot_tn(r.tiny[...].reshape(fewer, LANES), r.dpyr[...].reshape(fewer, MID))
    put(MATS.pyramid, jnp.concatenate([back[16 * c : 16 * c + 1] for c in range(CHAN)], axis=0))
    back = dot_tn(r.xin[...].reshape(whole, LANES), r.din[...].reshape(whole, NF))
    for c in range(CHAN):
        stage[pl.ds(MATS.conv_in[0] + c, 9, stride=CHAN), :] = back[16 * c : 16 * c + 9]
    ring, sems = r.ring, r.ring_sems

    class sending:
        def __init__(self, upper, lower, d, slot):
            place = block_place(jnp.bitwise_xor(d, me))
            self.copies = [
                pltpu.make_async_copy(ring.at[slot, :CUT], upper.at[place], sems.at[0, slot]),
                pltpu.make_async_copy(ring.at[slot, CUT:], lower.at[place], sems.at[1, slot]),
            ]

        def start(self):
            for copy in self.copies:
                copy.start()

        def wait(self):
            for copy in self.copies:
                copy.wait()

    def give(d, carry):
        slot = d % RING

        @pl.when(d >= RING)
        def _():
            sending(r.stay, r.stay_low, d, slot).wait()

        block = jnp.concatenate([stage[pl.ds(pl.multiple_of(d * ROWS, 8), ROWS), :], gsm[d]], axis=0)
        ring[slot] = block.astype(BF16)
        goes = jnp.bitwise_xor(d, me) % 2 == 1

        @pl.when(goes)
        def _():
            sending(r.leave, r.leave_low, d, slot).start()

        @pl.when(jnp.logical_not(goes))
        def _():
            sending(r.stay, r.stay_low, d, slot).start()

        return carry

    lax.fori_loop(0, BLOCKS, give, 0)
    for d in range(BLOCKS - RING, BLOCKS):
        sending(r.stay, r.stay_low, d, d % RING).wait()


def tap_lanes(field, flip):
    lane = lax.broadcasted_iota(jnp.int32, (PIX, LANES), 1) % 16
    total = jnp.zeros((PIX, LANES), F32)
    for t, (dy, dx) in enumerate(TAPS):
        y, x = (2 - dy, 2 - dx) if flip else (dy, dx)
        total = jnp.where(lane == t, field[x : x + 4, y : y + 16].reshape(PIX, LANES), total)
    return total


def block_place(mark):
    low, high, x, y = (mark // 2) % 2, (mark // 4) % 2, (mark // 8) % 2, mark // 16
    return high * 8 + (4 * y + 2 * x + high * 2 * (x - y)) + low


def vmem():
    return pl.BlockSpec(memory_space=pltpu.VMEM)


def anywhere():
    return pl.BlockSpec(memory_space=pl.ANY)


def smem():
    return pl.BlockSpec(memory_space=pltpu.SMEM)


LIMIT = 60 * 1024 * 1024


def run_forward(me, sigma, pieces, marks, data):
    slots = data.images.shape[0]
    ins = dict(me=me, sigma=sigma) | vars(data)
    outs = {"w_" + label: (WEIGHT_SHAPES[label], BF16) for label in WEIGHTS}
    outs |= dict(sm=((BLOCKS, 8, LANES), F32)) | TIME_SAVED
    outs |= {label: ((slots,) + shape, dtype) for label, (shape, dtype) in SAVED.items()}
    outs |= dict(err=((slots, IMG, IMG * CHAN), F32), err16=((slots, IMG, IMG * CHAN), BF16))
    scratch = dict(
        stage=((BLOCKS * ROWS, LANES), F32),
        pd=((8, MID), F32),
        pu=((8, NF), F32),
        out_bias=((IMG, IMG * CHAN), F32),
        field=((slots, 6, 18, 16, LANES), F32),
    )
    names = list(ins) + ["out_" + label for label in outs] + list(outs) + list(scratch) + ["sems"]
    results = pl.pallas_call(
        functools.partial(forward_kernel, marks, slots, names, list(outs)),
        out_shape=[jax.ShapeDtypeStruct(*v) for v in outs.values()],
        in_specs=[vmem()] * len(pieces) + [smem()] * 2 + [vmem()] * (len(ins) - 2),
        out_specs=[anywhere()] * len(outs),
        scratch_shapes=[pltpu.VMEM(*v) for v in (outs | scratch).values()] + [pltpu.SemaphoreType.DMA((len(outs),))],
        compiler_params=pltpu.CompilerParams(vmem_limit_bytes=LIMIT),
        name="forward",
    )(*pieces, *ins.values())
    return SimpleNamespace(**dict(zip(outs, results)))


FETCH_ORDER = list(
    dict(
        w_conv_out=0,
        h3=0,
        h0=0,
        w_up_two=0,
        b1=0,
        w_up_skip=0,
        w_up_one=0,
        h2=0,
        w_attn_out=0,
        qkv=0,
        prob=0,
        w_attn_qkv=0,
        h1=0,
        w_down_skip=0,
        w_down_two=0,
        a1=0,
        w_down_one=0,
        w_down_time=0,
        w_up_time=0,
        t2=0,
        s1=0,
        w_temb_two=0,
        t1=0,
        tact=0,
        final=0,
        sku=0,
        eu2=0,
        eu1=0,
        mixed=0,
        g=0,
        sk0=0,
        ed2=0,
        ed1=0,
        xin=0,
        tiny=0,
    )
)


def run_backward(me, ints, other, kept, data):
    slots = other.shape[0]
    ins = dict(me=me, ints=ints)
    scalars = len(ins)
    ins |= dict(other=other, err=kept.err, sm=kept.sm, stats=kept.stats)
    ins |= dict(y_of=data.y_of, own_x=data.own_x, fan=data.fan, colours=data.colours)
    direct = len(ins)
    fetched = dict(shrink=data.shrink)
    fetched |= {name: getattr(kept, name) for name in FETCH_ORDER}
    fetched |= dict(grow=data.grow, feats=data.feats)
    ins |= {"in_" + name: value for name, value in fetched.items()}
    upper = ((BLOCKS // 2, CUT, LANES), BF16)
    lower = ((BLOCKS // 2, BLOCK - CUT, LANES), BF16)
    outs = dict(stay=upper, stay_low=lower, leave=upper, leave_low=lower, loss=((IMG, IMG * CHAN), F32))
    scratch = {name: (value.shape, value.dtype) for name, value in fetched.items()}
    scratch |= dict(
        stage=((BLOCKS * ROWS, LANES), F32),
        gsm=((BLOCKS, 8, LANES), F32),
        ring=((RING, BLOCK, LANES), BF16),
        dpd=((8, MID), F32),
        dpu=((8, NF), F32),
        dout_sum=((IMG, IMG * CHAN), F32),
        field=((slots, 6, 18, 16, LANES), F32),
        cols=((slots, PIX, LANES), BF16),
        gu2=((slots, 6, 18, 16, NF), BF16),
        gu1=((slots, 6, 18, 16, NF), BF16),
        gd2=((slots, 4, 10, 16, MID), BF16),
        gd1=((slots, 4, 10, 16, MID), BF16),
        wide=((slots, PIX, NF), F32),
        dh0=((slots, PIX, NF), F32),
        din=((slots, PIX, NF), BF16),
        datt=((slots, HALF, MID), BF16),
        dqkv=((slots, HALF, 3 * MID), BF16),
        dpyr=((slots, HALF, MID), BF16),
    )
    names = list(ins) + list(outs) + list(scratch) + ["sems", "ring_sems"]
    results = pl.pallas_call(
        functools.partial(backward_kernel, slots, names, list(fetched)),
        out_shape=[jax.ShapeDtypeStruct(*v) for v in outs.values()],
        in_specs=[smem()] * scalars + [vmem()] * (direct - scalars) + [anywhere()] * (len(ins) - direct),
        out_specs=[anywhere()] * 4 + [vmem()],
        scratch_shapes=[pltpu.VMEM(*v) for v in scratch.values()]
        + [pltpu.SemaphoreType.DMA((len(fetched),)), pltpu.SemaphoreType.DMA((2, RING))],
        compiler_params=pltpu.CompilerParams(vmem_limit_bytes=LIMIT),
        name="backward",
    )(*ins.values())
    return SimpleNamespace(**dict(zip(outs, results)))


def swap(value, axis, mask):
    size = lax.axis_size(axis)
    return lax.ppermute(value, axis, [(i, i ^ mask) for i in range(size)])


def sum_everywhere(value):
    count = lax.axis_size(WIDE) * lax.axis_size(NARROW)
    rows = lax.all_to_all(jnp.broadcast_to(value, (count, LANES)), AXES, 0, 0, tiled=True)
    return jnp.sum(rows, axis=0, keepdims=True)


def notes(live, ints):
    return jnp.pad(jnp.concatenate([live, ints]).astype(F32), (0, LANES - 1 - ints.shape[0]))[None]


def gather_all(params, smalls, ints, meanwhile):
    if lax.axis_size(WIDE) == 4 and lax.axis_size(NARROW) == 8:
        rows = params.reshape(ROWS, LANES)
        tail = jnp.pad(notes(ints[:1], ints), ((0, BLOCK - ROWS - SMALL_ROWS - 1), (0, 0)))
        tail = jnp.concatenate([rows, smalls.reshape(SMALL_ROWS, LANES), tail])
        owns = [tail.astype(BF16)[None]]
        near, side, far = [], [], []
        for own in owns:
            z1, z2, z3 = (swap(own, NARROW, m) for m in (2, 4, 6))
            near.append((jnp.concatenate([own, z1]), jnp.concatenate([z2, z3])))
        near[0], first = lax.optimization_barrier((near[0], meanwhile[:2]))
        for a, b in near:
            side.append((swap(a, WIDE, 1), swap(b, WIDE, 2)))
        side[0], second = lax.optimization_barrier((side[0], meanwhile[2:]))
        for (a, b), (ax, by) in zip(near, side):
            far.append((swap(jnp.concatenate([a, ax]), WIDE, 2), swap(jnp.concatenate([b, by]), WIDE, 1)))
        pieces, marks = [], []
        for part in range(len(owns)):
            arrays = [jnp.concatenate(near[part]), jnp.concatenate(side[part]), *far[part]]
            lists = [[0, 2, 4, 6], [8, 10, 20, 22], [16, 18, 24, 26], [12, 14, 28, 30]]
            pieces += arrays + [swap(array, NARROW, 1) for array in arrays]
            marks += [(at, part * CUT) for at in lists] + [([m + 1 for m in at], part * CUT) for at in lists]
        return pieces, marks, True, first + second
    whole = lax.all_gather(params.astype(BF16), AXES, axis=0, tiled=True).reshape(BLOCKS, ROWS, LANES)
    little = lax.all_gather(smalls.astype(BF16), AXES, axis=0, tiled=True).reshape(BLOCKS, SMALL_ROWS, LANES)
    live = lax.all_gather(ints[:1], AXES, axis=0, tiled=True).reshape(BLOCKS, -1).sum(axis=1)
    others = swap(ints, WIDE, lax.axis_size(WIDE) // 2)
    extra = jnp.stack([notes(live[d : d + 1], others) for d in range(BLOCKS)])
    extra = jnp.pad(extra, ((0, 0), (0, BLOCK - ROWS - SMALL_ROWS - 1), (0, 0))).astype(BF16)
    return [jnp.concatenate([whole, little, extra], axis=1)], [(list(range(BLOCKS)), 0)], False, meanwhile


def collect_kernel(count, *refs):
    pieces, loss, own, rows = refs[:count], refs[count], refs[count + 1], refs[count + 2]
    first, squares = 0, jnp.zeros((1, LANES), F32)
    for n in range(0, count, 4):
        total = sum(piece[...].astype(F32) for piece in pieces[n : n + 4])
        own[first : first + total.shape[0], :] = total
        first += total.shape[0]
        squares += rowsum(total * total)
    squares = jnp.sum(squares, axis=1, keepdims=True)
    part = jnp.sum(rowsum(loss[...]), axis=1, keepdims=True)
    lane = lax.broadcasted_iota(jnp.int32, rows.shape, 1)
    rows[...] = jnp.where(lane == 0, squares, jnp.where(lane == 1, part, 0.0))


def collect(pieces, loss):
    count = lax.axis_size(WIDE) * lax.axis_size(NARROW)
    return pl.pallas_call(
        functools.partial(collect_kernel, len(pieces)),
        out_shape=[jax.ShapeDtypeStruct((BLOCK, LANES), F32), jax.ShapeDtypeStruct((count, LANES), F32)],
        in_specs=[vmem()] * (len(pieces) + 1),
        out_specs=[vmem()] * 2,
        name="collect",
    )(*pieces, loss)


def update_kernel(rows, own, *refs):
    ins, (loss, norm, *outs) = refs[:6], refs[6:]
    both = rowsum(rows[...])
    grad_norm = jnp.sqrt(both[:, 0:1])
    loss[...] = both[:, 1:2]
    norm[...] = grad_norm
    factor = jnp.minimum(1.0, 0.01 / (grad_norm + 1e-06))
    grad = factor * own[:ROWS, :]
    for ref, value in zip(outs, adamw(*(ref[...] for ref in ins[:3]), grad, 0.15)):
        ref[...] = value
    grad = factor * own[ROWS : ROWS + SMALL_ROWS, :]
    outs[6][...] = grad
    for ref, value in zip(outs[3:6], adamw(*(ref[...] for ref in ins[3:]), grad, 0.2)):
        ref[...] = value


def update(rows, own, vectors):
    vectors = [vector.reshape(-1, LANES) for vector in vectors]
    one = jax.ShapeDtypeStruct((1, 1), F32)
    like = [jax.ShapeDtypeStruct(vector.shape, F32) for vector in vectors]
    outs = pl.pallas_call(
        update_kernel,
        out_shape=[one, one] + like + like[3:4],
        in_specs=[vmem()] * 8,
        out_specs=[vmem()] * 9,
        name="update",
    )(rows, own, *vectors)
    return [value.reshape(()) for value in outs[:2]] + [value.reshape(-1) for value in outs[2:]]


def scatter_sums(stay, leave, loss, relative):
    if relative:

        def join(kept, received):
            return (kept.astype(F32) + received.astype(F32)).astype(BF16)

        parts = [join(a, swap(b, NARROW, 1)) for a, b in zip(stay, leave)]
        parts = [part.reshape((2, 2, BLOCKS // 8) + part.shape[1:]) for part in parts]
        pairs = []
        for a, b in parts:
            if pairs:
                pairs[0], (a, b) = lax.optimization_barrier((pairs[0], (a, b)))
            pairs.append((join(a[0], swap(a[1], WIDE, 2)), join(b[0], swap(b[1], WIDE, 1))))
        parts = [(join(a[:2], swap(a[2:], WIDE, 1)), join(b[:2], swap(b[2:], WIDE, 2))) for a, b in pairs]
        pieces = []
        for a, b in parts:
            pieces.append(a[0])
            pieces += [swap(value, NARROW, mask) for value, mask in ((a[1], 2), (b[0], 4), (b[1], 6))]
        return collect(pieces, loss)
    stay, leave = jnp.concatenate(stay, axis=1), jnp.concatenate(leave, axis=1)
    grads = jnp.stack([(leave if d % 2 else stay)[block_place(d)] for d in range(BLOCKS)])
    large = grads[:, :ROWS].reshape(-1).astype(F32)
    little = grads[:, ROWS : ROWS + SMALL_ROWS].reshape(-1).astype(F32)
    return (
        lax.psum_scatter(large, AXES, scatter_dimension=0, tiled=True),
        lax.psum_scatter(little, AXES, scatter_dimension=0, tiled=True),
    )


def adamw(weight, moment, second, grad, rate):
    moment_new = 0.5 * moment + 0.5 * grad
    second_new = 0.99 * second + 0.01 * grad * grad
    direction = moment_new / (1.0 - 0.5**STEP) / (jnp.sqrt(second_new / (1.0 - 0.99**STEP)) + 1e-08)
    return (weight - rate * (direction + 0.01 * weight), moment_new, second_new)


def body(
    params,
    first_moment,
    second_moment,
    smalls,
    small_first,
    small_second,
    images,
    noise,
    sigma,
    freq,
    counts,
    partner,
):
    slots = images.shape[0]
    ints = jnp.concatenate([counts, partner[0]]).astype(jnp.int32)
    shrink = fir_matrix()
    phase = jnp.log(sigma)[:, None] * freq[None, :] * (2.0 * math.pi)
    feats = jnp.concatenate([jnp.sin(phase), jnp.cos(phase)], axis=-1)
    feats = jnp.pad(feats.astype(BF16), ((0, 8 - slots), (0, 0)))
    own = (feats, images.reshape(slots, IMG, IMG * CHAN), noise.reshape(slots, IMG, IMG * CHAN))
    pieces, marks, relative, own = gather_all(params, smalls, ints, own)
    index = lax.axis_index(WIDE) * lax.axis_size(NARROW) + lax.axis_index(NARROW)
    me = (index if relative else jnp.zeros_like(index)).astype(jnp.int32)[None]
    data = SimpleNamespace(
        feats=own[0],
        images=own[1],
        noise=own[2],
        shrink=jnp.asarray(shrink, BF16),
        grow=jnp.asarray(4.0 * shrink.T, BF16),
        **{name: jnp.asarray(value) for name, value in pixel_maps().items()},
    )
    kept = run_forward(me, sigma, pieces, marks, data)
    other = swap(kept.err16, WIDE, lax.axis_size(WIDE) // 2)
    done = run_backward(me, ints, other, kept, data)
    vectors = [params, first_moment, second_moment, smalls, small_first, small_second]
    sums = scatter_sums((done.stay, done.stay_low), (done.leave, done.leave_low), done.loss, relative)
    if relative:
        own, rows = sums
        return tuple(update(lax.all_to_all(rows, AXES, 0, 0, tiled=True), own, vectors))
    grad_params, grad_smalls = sums
    squares = jnp.sum(grad_params * grad_params) + jnp.sum(grad_smalls * grad_smalls)
    lane = lax.broadcasted_iota(jnp.int32, (1, LANES), 1)
    both = sum_everywhere(jnp.where(lane == 0, squares, jnp.where(lane == 1, jnp.sum(done.loss), 0.0)))
    loss, grad_norm = both[0, 1], jnp.sqrt(both[0, 0])
    factor = jnp.minimum(1.0, 0.01 / (grad_norm + 1e-06))
    small_grad = factor * grad_smalls
    new_params, new_first, new_second = adamw(
        params, first_moment, second_moment, factor * grad_params, 0.15
    )
    new_smalls, new_small_first, new_small_second = adamw(
        smalls, small_first, small_second, small_grad, 0.2
    )
    return (
        loss,
        grad_norm,
        new_params,
        new_first,
        new_second,
        new_smalls,
        new_small_first,
        new_small_second,
        small_grad,
    )


def solution(mesh):
    flat, rows = P(AXES), P(AXES, None)
    return jax.shard_map(
        body,
        mesh=mesh,
        in_specs=(flat, flat, flat, flat, flat, flat, rows, rows, flat, P(), flat, rows),
        out_specs=(P(), P(), flat, flat, flat, flat, flat, flat, flat),
        check_vma=False,
    )
```
